32 devices in a mesh: exp: 8 (over z, x), sky: 4 (over y, core).
Axes of the slice: x: 2, y: 2, z: 4, core: 2. Of those that a mesh axis runs over, the one named last changes fastest.
Arguments:
- image: float32 [8, 2048, 4096], P('exp', 'sky'), may hold values from -21 to 21
- variance: float32 [8, 2048, 4096], P('exp', 'sky'), may hold values from 0.25 to 4
- mask: int32 [8, 128, 256], P('exp', 'sky'), may hold values 0 or 1
- foot_start: int32 [8], replicated, may hold values from 0 to 64
- pair_owner: int32 [8, 8], replicated, may hold values from 0 to 1, as said below
Outputs:
- coadd: float32 [2048, 4096], P('sky', 'exp')
- offsets: float32 [8, 9], replicated
The draws below stay inside these ranges and needn't reach their ends.
Inputs may be any that keep to these rules, and one draw needn't show every extreme that they name: pair_owner is 0 or 1, zero on the diagonal, pair_owner[i, j] and pair_owner[j, i] are never both 1, and every exposure has at least one pair.
All inputs are finite; a program needn't handle non-finite values. No bound on the sum of `mask` on one device may be relied on, other than what follows from the above.
Results may differ from the reference program's by a relative error of at most 0.0003.
Values sent between devices are 32-bit elements; how exact they have to be, the bound alone decides.
No kernel may reach another device: no remote copies, remote signals or barrier semaphores. Data moves between devices by JAX's collectives and lax.ppermute only.
A program may use at most 256 MiB of HBM per device.

```python
import math
import jax
import jax.numpy as jnp
from jax import lax

COLS = 4096
BIN = 16
RADIUS = 10
FOOT = 3072
NEXP = 8
ROWS = 2048


def draw_image(key, part):
    scales = jnp.array([[1.0, 0.6, 0.4], [0.6, 0.4, 0.3], [0.4, 0.3, 0.2]], jnp.float32)
    coef = jax.random.truncated_normal(jax.random.fold_in(key, 11), -3.0, 3.0, (NEXP, 3, 3), jnp.float32) * scales
    noise = jax.random.truncated_normal(jax.random.fold_in(key, 13), -4.0, 4.0, (NEXP, ROWS, COLS), jnp.float32)
    ycoord = (2.0 * jnp.arange(ROWS).astype(jnp.float32) + 1.0) / ROWS - 1.0
    xcoord = (2.0 * jnp.arange(COLS).astype(jnp.float32) + 1.0) / COLS - 1.0
    ty = [jnp.ones_like(ycoord), ycoord, 2.0 * ycoord * ycoord - 1.0]
    tx = [jnp.ones_like(xcoord), xcoord, 2.0 * xcoord * xcoord - 1.0]
    back = jnp.zeros((NEXP, ROWS, COLS), jnp.float32)
    for upper in range(3):
        for lower in range(3):
            back = back + coef[:, upper, lower][:, None, None] * ty[upper][None, :, None] * tx[lower][None, None, :]
    return back + noise


def draw_pair_owner(key, part):
    rank = jax.random.permutation(jax.random.fold_in(key, 21), NEXP)
    keep = jax.random.randint(jax.random.fold_in(key, 22), (NEXP, NEXP), 0, 4)
    keep = jnp.minimum(keep, keep.T)
    rank_i = rank[:, None]
    rank_j = rank[None, :]
    nearby = jnp.abs(rank_i - rank_j) == 1
    exists = (keep != 0) | nearby
    return jnp.where(exists & (rank_i > rank_j), 1, 0).astype(jnp.int32)


def with_ends(drawn, key, least, high):
    index_at = [jax.random.randint(jax.random.fold_in(key, axis), (), 0, length) for axis, length in enumerate(drawn.shape)]
    longest = drawn.shape.index(max(drawn.shape))
    beside = index_at[:longest] + [(index_at[longest] + 1) % drawn.shape[longest]] + index_at[longest + 1:]
    return drawn.at[tuple(index_at)].set(least).at[tuple(beside)].set(high)


def block_scale(rng, extent, cuts, least, high):
    def one(position, parts):
        heights = jax.random.uniform(jax.random.fold_in(jax.random.fold_in(rng, 6), position), (parts,), jnp.float32, least / len(cuts), high / len(cuts))
        return jnp.repeat(jnp.exp(heights), extent[position] // parts).reshape((-1,) + (1,) * (len(extent) - position - 1))

    gain = one(*cuts[0])
    for cut in cuts[1:]:
        gain = gain * one(*cut)
    return gain


def setup_inputs(seed: int = 0) -> dict:
    keys = jax.random.split(jax.random.key(seed), 6)
    image = draw_image(jax.random.fold_in(keys[5], 71), 0)
    variance = jnp.clip(jnp.exp(math.log(4.0) - 2.7725887 * jax.random.uniform(keys[1], (NEXP, ROWS, COLS), jnp.float32) ** block_scale(keys[1], (NEXP, ROWS, COLS), ((0, 8), (1, 4)), -0.2, 0.2)), 0.25, 4.0)
    mask = with_ends((jax.random.randint(keys[2], (NEXP, ROWS // BIN, COLS // BIN), 0, 8) < 7).astype(jnp.int32), jax.random.fold_in(keys[2], 1), 0, 1)
    foot_start = with_ends(jax.random.randint(keys[3], (NEXP,), 0, COLS // (4 * BIN) + 1), jax.random.fold_in(keys[3], 1), 0, (COLS // (4 * BIN) + 1) - 1).astype(jnp.int32)
    pair_owner = draw_pair_owner(jax.random.fold_in(keys[5], 71), 0)
    return dict(image=image, variance=variance, mask=mask, foot_start=foot_start, pair_owner=pair_owner)


HIGH = lax.Precision.HIGHEST
LAMBDA_REG = 0.25
PRIOR = 1.0

def chebyshev(coord):
    return jnp.stack([jnp.ones_like(coord), coord, 2.0 * coord * coord - 1.0])

def centers(count, start, total):
    return (2.0 * (jnp.arange(count) + start).astype(jnp.float32) + 1.0) / total - 1.0

def footprint(count, start, width):
    cells = jnp.arange(count)
    return ((cells >= start) & (cells < start + width)).astype(jnp.float32)

def bin_basis(rows, row_first, total_rows, cols):
    by = chebyshev(centers(rows, row_first, total_rows))
    bx = chebyshev(centers(cols, 0, cols))
    return (by[:, None, :, None] * bx[None, :, None, :]).reshape(9, rows, cols)

def pair_normals(own_image, own_weight, other_image, other_weight, basis):
    weight = own_weight * other_weight / (own_weight + other_weight + 1.0)
    diff = own_image - other_image
    weighted = weight[:, None] * basis[None]
    gram = jnp.einsum('nkpq,lpq->nkl', weighted, basis, precision=HIGH)
    rhs = jnp.einsum('nkpq,npq->nk', weighted, diff, precision=HIGH)
    return (gram, rhs)

def solve_pairs(gram, rhs, owner):
    eye = jnp.eye(9, dtype=jnp.float32)
    safe = jnp.where(owner[..., None, None] > 0, gram, eye)
    factor = jnp.linalg.cholesky(safe)
    half = jax.scipy.linalg.solve_triangular(factor, rhs[..., None], lower=True)
    fit = jax.scipy.linalg.solve_triangular(factor, half, lower=True, trans=1)[..., 0]
    return fit * owner[..., None]

def global_offsets(fits, owner):
    degree = jnp.sum(owner, 1) + jnp.sum(owner, 0) + LAMBDA_REG
    system = jnp.diag(degree) - owner - owner.T
    right = jnp.sum(fits, 1) - jnp.sum(fits, 0)
    factor = jnp.linalg.cholesky(system)
    half = jax.scipy.linalg.solve_triangular(factor, right, lower=True)
    return jax.scipy.linalg.solve_triangular(factor, half, lower=True, trans=1)

def gauss_taps():
    offs = jnp.arange(-RADIUS, RADIUS + 1).astype(jnp.float32)
    taps = jnp.exp(-offs * offs / 50.0)
    return taps / jnp.sum(taps)

def smooth_rows(padded, taps, rows):
    total = taps[0] * padded[0:rows]
    for shift in range(1, 2 * RADIUS + 1):
        total = total + taps[shift] * padded[shift:shift + rows]
    return total

def smooth_cols(field, taps):
    cols = field.shape[1]
    padded = jnp.pad(field, ((0, 0), (RADIUS, RADIUS)))
    total = taps[0] * padded[:, 0:cols]
    for shift in range(1, 2 * RADIUS + 1):
        total = total + taps[shift] * padded[:, shift:shift + cols]
    return total

def expand_blocks(blocks):
    rows_b, cols_b = blocks.shape
    return jnp.broadcast_to(blocks[:, None, :, None], (rows_b, BIN, cols_b, BIN)).reshape(rows_b * BIN, cols_b * BIN)

def reference(image, variance, mask, foot_start, pair_owner):
    bins_row = ROWS // BIN
    bins_col = COLS // BIN
    owner = pair_owner.astype(jnp.float32)

    def binned(items):
        frame, spread, blocks, start = items
        bin_image = frame.reshape(bins_row, BIN, bins_col, BIN).mean(axis=(1, 3))
        inside = footprint(bins_col, start, FOOT // BIN)
        inverse = (1.0 / spread).reshape(bins_row, BIN, bins_col, BIN).sum(axis=(1, 3))
        return (bin_image, inverse * blocks.astype(jnp.float32) * inside[None, :])
    bin_images, bin_weights = lax.map(binned, (image, variance, mask, foot_start))
    basis = bin_basis(bins_row, 0, bins_row, bins_col)

    def owner_normals(items):
        own_image, own_weight = items
        return pair_normals(own_image[None], own_weight[None], bin_images, bin_weights, basis)
    gram, rhs = lax.map(owner_normals, (bin_images, bin_weights))
    fits = solve_pairs(gram, rhs, owner)
    offsets = global_offsets(fits, owner)
    ty = chebyshev(centers(ROWS, 0, ROWS))
    tx = chebyshev(centers(COLS, 0, COLS))
    taps = gauss_taps()

    def accumulate(carry, items):
        numer, denom = carry
        frame, spread, blocks, start, coeffs = items
        background = jnp.dot(jnp.dot(ty.T, coeffs.reshape(3, 3), precision=HIGH), tx, precision=HIGH)
        inside = footprint(COLS, start * BIN, FOOT)
        corrected = (frame - background) * inside[None, :]
        padded = jnp.pad(corrected, ((RADIUS, RADIUS), (0, 0)))
        smoothed = smooth_cols(smooth_rows(padded, taps, ROWS), taps)
        weight = expand_blocks(blocks.astype(jnp.float32)) * inside[None, :] / spread
        return ((numer + weight * smoothed, denom + weight), None)
    zeros = jnp.zeros((ROWS, COLS), jnp.float32)
    (numer, denom), unused = lax.scan(accumulate, (zeros, zeros), (image, variance, mask, foot_start, offsets))
    coadd = numer / (PRIOR + denom)
    return (coadd, offsets)
```

```python
import functools

import jax
import jax.numpy as jnp
import ml_dtypes
import numpy as np
from jax import lax
from jax.experimental import pallas as pl
from jax.experimental.pallas import tpu as pltpu
from jax.sharding import PartitionSpec as P

BIN = 16
RADIUS = 10
HALO = 16
SIDE = 128
TILE = 256

HIGH = lax.Precision.HIGHEST
LAMBDA_REG = 0.25
PRIOR = 1.0
VMEM = 56 * 1024 * 1024
BF16 = jnp.bfloat16
F32 = jnp.float32


def tap_values():
    offs = np.arange(-RADIUS, RADIUS + 1).astype(np.float64)
    taps = np.exp(-offs * offs / 50.0)
    return taps / taps.sum()


def band(out, width, lead):
    taps = tap_values()
    full = np.zeros((out, width), np.float64)
    for shift in range(-RADIUS, RADIUS + 1):
        rows = np.arange(out)
        full[rows, rows + lead + shift] = taps[shift + RADIUS]
    return full


def two_parts(full):
    high = full.astype(np.float32).astype(ml_dtypes.bfloat16)
    low = (full - high.astype(np.float64)).astype(np.float32).astype(ml_dtypes.bfloat16)
    return high, low


def chebyshev(coord, count=3):
    terms = [jnp.ones_like(coord), coord]
    while len(terms) < count:
        terms.append(2.0 * coord * terms[-1] - terms[-2])
    return jnp.stack(terms)


def centers(index, total):
    return (2.0 * index.astype(F32) + 1.0) / total - 1.0


def split_high_low(value):
    high = value.astype(BF16)
    return high, (value - high.astype(F32)).astype(BF16)


def mm(left, right):
    return jnp.dot(left, right, preferred_element_type=F32)


def weights_kernel(plan, width, blocks_ref, start_ref, frame_ref, spread_ref, mask_ref, *outs):
    step = pl.program_id(0)
    bins_ref, weights = outs[0], outs[1:]
    block = blocks_ref[step]
    rows, share = frame_ref.shape
    bins_row, bins_col = mask_ref.shape
    inverse = 1.0 / spread_ref[...]
    cell = (lax.broadcasted_iota(jnp.int32, (bins_col, share), 1) + block * share) // BIN
    spread_out = (lax.broadcasted_iota(jnp.int32, (bins_col, share), 0) == cell).astype(BF16)
    kept = mm(mask_ref[...].astype(F32).astype(BF16), spread_out)
    first = start_ref[0] * BIN
    col = lax.broadcasted_iota(jnp.int32, (1, share), 1) + block * share
    kept = jnp.where((col >= first) & (col < first + width), kept, 0.0)
    kept = jnp.broadcast_to(kept[:, None, :], (bins_row, BIN, share)).reshape(rows, share)
    weight = inverse * kept
    for at, (out, fresh) in enumerate(plan):
        @pl.when(step == at)
        def _(out=out, fresh=fresh):
            weights[out][...] = weight if fresh else weights[out][...] + weight

    sums = jnp.concatenate(
        [
            frame_ref[...].reshape(bins_row, BIN, share).sum(axis=1),
            inverse.reshape(bins_row, BIN, share).sum(axis=1),
        ],
        axis=0,
    )
    cell_t = (lax.broadcasted_iota(jnp.int32, (share, bins_col), 0) + block * share) // BIN
    gather = (lax.broadcasted_iota(jnp.int32, (share, bins_col), 1) == cell_t).astype(BF16)
    top, rest = split_high_low(sums)
    middle = (sums - top.astype(F32)) - rest.astype(F32)
    part = mm(top, gather) + (mm(rest, gather) + mm(middle.astype(BF16), gather))

    @pl.when(step == 0)
    def _():
        bins_ref[...] = part

    @pl.when(step > 0)
    def _():
        bins_ref[...] = bins_ref[...] + part


def pixel_weights(plan, outputs, blocks, start, frame, spread, mask, share, width):
    rows = frame.shape[0]
    bins_row, bins_col = mask.shape
    column = pl.BlockSpec((rows, share), lambda i, blocks, start: (0, blocks[i]))
    whole = lambda shape: pl.BlockSpec(shape, lambda i, blocks, start: (0, 0))
    return pl.pallas_call(
        functools.partial(weights_kernel, plan, width),
        grid_spec=pltpu.PrefetchScalarGridSpec(
            num_scalar_prefetch=2,
            grid=(len(plan),),
            in_specs=[column, column, whole((bins_row, bins_col))],
            out_specs=[whole((2 * bins_row, bins_col))] + [whole((rows, share))] * outputs,
        ),
        out_shape=[jax.ShapeDtypeStruct((2 * bins_row, bins_col), F32)]
        + [jax.ShapeDtypeStruct((rows, share), F32)] * outputs,
        compiler_params=pltpu.CompilerParams(vmem_limit_bytes=VMEM),
        cost_estimate=pl.CostEstimate(
            flops=rows * share * len(plan) * 60, bytes_accessed=rows * share * len(plan) * 12, transcendentals=0
        ),
        name="pixel_weights",
    )(blocks, start, frame, spread, mask)


def smooth_kernel(plan, width, count, blocks_ref, start_ref, *refs):
    step = pl.program_id(0)
    images, (row_hi, row_lo, col_hi, col_lo) = refs[:9], refs[9:13]
    weights, outs = refs[13 : 13 + count], refs[13 + count :]
    block = blocks_ref[step]
    rows, share = images[4].shape
    window = share + 2 * SIDE
    field = jnp.concatenate(
        [jnp.concatenate([images[3 * i + j][...] for j in range(3)], axis=1) for i in range(3)], axis=0
    )
    first = start_ref[0] * BIN
    col = lax.broadcasted_iota(jnp.int32, (1, window), 1) + (block * share - SIDE)
    field = jnp.where((col >= first) & (col < first + width), field, 0.0)
    high, low = split_high_low(field)
    band_hi = row_hi[...]
    along = mm(band_hi, high) + (mm(row_lo[...], high) + mm(band_hi, low))
    high, low = split_high_low(along)
    band_hi = col_hi[...]
    tiles = []
    for tile in range(share // TILE):
        lanes = slice(tile * TILE, (tile + 1) * TILE + 2 * SIDE)
        tiles.append(mm(high[:, lanes], band_hi) + (mm(high[:, lanes], col_lo[...]) + mm(low[:, lanes], band_hi)))
    smoothed = tiles[0] if len(tiles) == 1 else jnp.concatenate(tiles, axis=1)
    col = lax.broadcasted_iota(jnp.int32, (1, share), 1) + block * share
    smoothed = jnp.where((col >= first) & (col < first + width), smoothed, 0.0)
    for at, (out, fresh) in enumerate(plan):
        @pl.when(step == at)
        def _(out=out, fresh=fresh):
            term = weights[out][...] * smoothed
            outs[out][...] = term if fresh else outs[out][...] + term


def smoothed_terms(plan, weights, blocks, start, frame, above, below, share, width):
    rows, cols = frame.shape
    count = len(weights)
    per = share // SIDE
    last = cols // SIDE - 1
    specs = []
    for height in (HALO, rows, HALO):
        specs += [
            pl.BlockSpec((height, SIDE), lambda i, blocks, start: (0, jnp.maximum(blocks[i] * per - 1, 0))),
            pl.BlockSpec((height, share), lambda i, blocks, start: (0, blocks[i])),
            pl.BlockSpec((height, SIDE), lambda i, blocks, start: (0, jnp.minimum(blocks[i] * per + per, last))),
        ]
    whole = lambda shape: pl.BlockSpec(shape, lambda i, blocks, start: (0, 0))
    row_parts = two_parts(band(rows, rows + 2 * HALO, HALO))
    col_parts = two_parts(band(TILE, TILE + 2 * SIDE, SIDE).T)
    parts = [jnp.asarray(p) for p in row_parts + col_parts]
    flops = 6 * rows * (rows + 2 * HALO) * (share + 2 * SIDE) + 6 * rows * share * (TILE + 2 * SIDE)
    return pl.pallas_call(
        functools.partial(smooth_kernel, plan, width, count),
        grid_spec=pltpu.PrefetchScalarGridSpec(
            num_scalar_prefetch=2,
            grid=(len(plan),),
            in_specs=specs + [whole(p.shape) for p in parts] + [whole((rows, share))] * count,
            out_specs=[whole((rows, share))] * count,
        ),
        out_shape=[jax.ShapeDtypeStruct((rows, share), F32)] * count,
        compiler_params=pltpu.CompilerParams(vmem_limit_bytes=VMEM),
        cost_estimate=pl.CostEstimate(
            flops=flops * len(plan), bytes_accessed=rows * share * len(plan) * 14, transcendentals=0
        ),
        name="smoothed_terms",
    )(blocks, start, *([above] * 3 + [frame] * 3 + [below] * 3), *parts, *weights)


def contract_last(left, right):
    return lax.dot_general(left, right, (((1,), (1,)), ((), ())), precision=HIGH, preferred_element_type=F32)


def moments_kernel(image_ref, weight_ref, basis_ref, out_ref):
    image, weight = image_ref[...], weight_ref[...]
    count = image.shape[0]
    pairs, diffs = [], []
    for apart in range(1, count // 2 + 1):
        other_w = jnp.concatenate([weight[apart:], weight[:apart]], axis=0)
        other_i = jnp.concatenate([image[apart:], image[:apart]], axis=0)
        joint = weight * other_w / (weight + other_w + 1.0)
        pairs.append(joint)
        diffs.append(joint * (image - other_i))
    basis = basis_ref[...]
    out_ref[...] = jnp.concatenate(
        [
            contract_last(basis, jnp.concatenate(pairs, axis=0)),
            contract_last(basis, jnp.concatenate(diffs, axis=0)),
        ],
        axis=0,
    )


def solve_kernel(moments_ref, owner_ref, out_ref):
    owner = owner_ref[...].astype(F32)
    count = owner.shape[0]
    lanes = moments_ref.shape[1]
    exposure = lax.broadcasted_iota(jnp.int32, (count, lanes), 0)
    lane = lax.broadcasted_iota(jnp.int32, (count, lanes), 1)
    mine = lane % count
    apart = lane // count + 1
    is_i = (exposure == mine).astype(F32)
    is_j = (exposure == (mine + apart) % count).astype(F32)
    both = owner + owner.T
    listed = jnp.sum(is_i * jnp.dot(both, is_j, precision=HIGH, preferred_element_type=F32), axis=0, keepdims=True)
    lane_row = lax.broadcasted_iota(jnp.int32, (1, lanes), 1)
    once = (lane_row // count + 1 < count // 2) | (lane_row % count < count // 2)
    listed = jnp.where(once, listed, 0.0)
    held = listed > 0.0
    moment = [[moments_ref[5 * a + b : 5 * a + b + 1, :] for b in range(5)] for a in range(5)]

    def entry(k, l):
        (u, v), (s, t) = divmod(k, 3), divmod(l, 3)
        total = 0.0
        for a in (u + s, abs(u - s)):
            for b in (v + t, abs(v - t)):
                total = total + moment[a][b]
        return jnp.where(held, 0.25 * total, 1.0 if k == l else 0.0)

    factor = [[None] * 9 for _ in range(9)]
    scale = [None] * 9
    for k in range(9):
        for l in range(k, 9):
            value = entry(l, k)
            for m in range(k):
                value = value - factor[l][m] * factor[k][m]
            if l == k:
                scale[k] = 1.0 / jnp.sqrt(value)
            else:
                factor[l][k] = value * scale[k]
    half = [None] * 9
    for k in range(9):
        at = 32 + 5 * (k // 3) + k % 3
        value = moments_ref[at : at + 1, :]
        for m in range(k):
            value = value - factor[k][m] * half[m]
        half[k] = value * scale[k]
    fit = [None] * 9
    for k in reversed(range(9)):
        value = half[k]
        for m in range(k + 1, 9):
            value = value - factor[m][k] * fit[m]
        fit[k] = value * scale[k]
    fits = jnp.concatenate([jnp.where(held, f, 0.0) for f in fit] + [jnp.zeros((7, lanes), F32)], axis=0)
    right = contract_last((is_i - is_j) * listed, fits)
    row = lax.broadcasted_iota(jnp.int32, (count, count), 0)
    column = lax.broadcasted_iota(jnp.int32, (count, count), 1)
    degree = jnp.sum(both, axis=1, keepdims=True) + LAMBDA_REG
    system = jnp.where(row == column, degree, 0.0) - both
    for k in range(count):
        inverse = 1.0 / system[k : k + 1, k : k + 1]
        pivot_s, pivot_r = system[k : k + 1, :] * inverse, right[k : k + 1, :] * inverse
        lead = system[:, k : k + 1]
        chosen = row[:, :1] == k
        system = jnp.where(chosen, pivot_s, system - lead * pivot_s)
        right = jnp.where(chosen, pivot_r, right - lead * pivot_r)
    out_ref[...] = right[:, :9]


def per_device(image, variance, mask, foot_start, pair_owner):
    frame, spread, blocks = image[0], variance[0], mask[0]
    rows, cols = frame.shape
    bins_row, bins_col = blocks.shape
    exposures, sky_count = lax.axis_size("exp"), lax.axis_size("sky")
    member, strip = lax.axis_index("exp"), lax.axis_index("sky")
    share = cols // exposures
    width = 3 * cols // 4
    places = exposures // 2
    quarter = places // 4
    place, side = member // 2, member % 2
    own_start = lax.dynamic_slice_in_dim(foot_start, member, 1)
    mate_start = lax.dynamic_slice_in_dim(foot_start, member + 1 - 2 * side, 1)

    order = np.zeros((places, places), np.int32)
    for z in range(places):
        down = z < places // 2
        ends = range(quarter)
        middle = list(range(quarter, places - quarter))
        listed = []
        for q in ends:
            low = quarter - 1 - q if down else q
            listed += [low, low + places - quarter]
        order[z] = listed + (middle[::-1] if down else middle)
    middle_count = places - 2 * quarter
    my_order = lax.dynamic_index_in_dim(jnp.asarray(order), place, 0, keepdims=False)
    sent_blocks = 2 * my_order + (1 - side)
    kept_blocks = 2 * my_order + side
    folded = [(i // 2, i % 2 == 0) for i in range(2 * quarter)]
    folded += [(quarter + i, True) for i in range(middle_count)]
    plain = [(i, True) for i in range(places)]
    units = quarter + middle_count

    up = [(i, i + 1) for i in range(sky_count - 1)]
    down = [(j, i) for i, j in up]
    above = lax.ppermute(frame[rows - HALO :], "sky", up)
    below = lax.ppermute(frame[:HALO], "sky", down)

    swap = [(i, i ^ 1) for i in range(exposures)]
    bins_a, *den_sent = pixel_weights(folded, units, sent_blocks, own_start, frame, spread, blocks, share, width)
    den_got = [lax.ppermute(d, "exp", swap) for d in den_sent]
    bins_b, *den_kept = pixel_weights(plain, places, kept_blocks, own_start, frame, spread, blocks, share, width)

    bins = (bins_a + bins_b).reshape(2, bins_row, bins_col)
    cell = jnp.arange(bins_col)
    inside_bins = (cell >= own_start) & (cell < own_start + width // BIN)
    keep = jnp.where(inside_bins[None, :], blocks, 0).astype(F32)
    both = jnp.stack([bins[0] / (BIN * BIN), bins[1] * keep])
    part_rows = bins_row // exposures
    both = both.reshape(2, exposures, part_rows, bins_col).swapaxes(0, 1)
    spread_bins = lax.all_to_all(both, "exp", 0, 0)
    per_exposure = spread_bins.reshape(exposures, 2, part_rows * bins_col)
    ty = chebyshev(centers(jnp.arange(part_rows) + (strip * bins_row + member * part_rows), bins_row * sky_count), 5)
    tx = chebyshev(centers(jnp.arange(bins_col), bins_col), 5)
    basis = (ty[:, None, :, None] * tx[None, :, None, :]).reshape(25, part_rows * bins_col)
    basis = jnp.concatenate([basis, jnp.zeros((7, part_rows * bins_col), F32)])
    moments = pl.pallas_call(
        moments_kernel,
        out_shape=jax.ShapeDtypeStruct((64, exposures * exposures // 2), F32),
        cost_estimate=pl.CostEstimate(flops=10**7, bytes_accessed=3 * 10**5, transcendentals=0),
        name="pair_moments",
    )(per_exposure[:, 0], per_exposure[:, 1], basis)
    for axis, size in (("sky", sky_count), ("exp", exposures)):
        bit = 1
        while bit < size:
            moments = moments + lax.ppermute(moments, axis, [(i, i ^ bit) for i in range(size)])
            bit *= 2
    offsets = pl.pallas_call(
        solve_kernel,
        out_shape=jax.ShapeDtypeStruct((exposures, 9), F32),
        cost_estimate=pl.CostEstimate(flops=10**6, bytes_accessed=10**5, transcendentals=0),
        name="offsets",
    )(moments, pair_owner)

    taps = tap_values().astype(np.float32)
    row_at = jnp.arange(-RADIUS, rows + RADIUS) + strip * rows
    ty = chebyshev(centers(row_at, rows * sky_count))
    ty = jnp.where((row_at >= 0) & (row_at < rows * sky_count), ty, 0.0)
    rows_part = sum(float(taps[t]) * ty[:, t : t + rows] for t in range(2 * RADIUS + 1))
    col_at = jnp.arange(-RADIUS, cols + RADIUS)
    tx = chebyshev(centers(col_at, cols))

    def columns_part(start):
        masked = jnp.where((col_at >= start * BIN) & (col_at < start * BIN + width), tx, 0.0)
        return sum(float(taps[t]) * masked[:, t : t + cols] for t in range(2 * RADIUS + 1))

    def coefficients(which, start):
        coeffs = lax.dynamic_index_in_dim(offsets, which, 0, keepdims=False).reshape(3, 3)
        return jnp.sum(coeffs[:, :, None] * columns_part(start)[None], axis=1)

    own_back = coefficients(member, own_start)
    mate_back = coefficients(member + 1 - 2 * side, mate_start)

    num_sent = smoothed_terms(folded, den_sent, sent_blocks, own_start, frame, above, below, share, width)
    num_got = [lax.ppermute(d, "exp", swap) for d in num_sent]
    num_kept = smoothed_terms(plain, den_kept, kept_blocks, own_start, frame, above, below, share, width)

    def background(back, at):
        cut = lax.dynamic_slice_in_dim(back, at * share, share, 1)
        return sum(rows_part[u][:, None] * cut[u][None, :] for u in range(3))

    unit_of = [out for out, fresh in folded]
    den_sum, num_sum = [], []
    for k in range(places):
        at = kept_blocks[k]
        got_den, got_num = den_got[unit_of[k]], num_got[unit_of[k]]
        if k < 2 * quarter:
            col = jnp.arange(share) + at * share
            inside = ((col >= mate_start * BIN) & (col < mate_start * BIN + width))[None, :]
            got_den = jnp.where(inside, got_den, 0.0)
            got_num = jnp.where(inside, got_num, 0.0)
        den_sum.append(den_kept[k] + got_den)
        num_sum.append(
            (num_kept[k] - den_kept[k] * background(own_back, at)) + (got_num - got_den * background(mate_back, at))
        )

    position = np.zeros((places, places), np.int32)
    for z in range(places):
        position[z, order[z]] = np.arange(places)

    def pick(parts, wanted):
        value = None
        for at in sorted(set(wanted.values())):
            if value is None:
                value = parts[at]
                continue
            here = functools.reduce(jnp.logical_or, [place == z for z, w in wanted.items() if w == at])
            value = jnp.where(here, parts[at], value)
        return value

    def along_places(parts):
        rightward = leftward = None
        for step in range(1, places):
            senders = {z: position[z, z + places - step] for z in range(places) if z + places - step < places}
            value = pick(parts, senders)
            value = value if rightward is None else value + rightward
            rightward = lax.ppermute(
                value, "exp", [(2 * z + s, 2 * z + 2 + s) for z in senders for s in range(2)]
            )
            senders = {z: position[z, z - places + step] for z in range(places) if z - places + step >= 0}
            value = pick(parts, senders)
            value = value if leftward is None else value + leftward
            leftward = lax.ppermute(
                value, "exp", [(2 * z + s, 2 * z - 2 + s) for z in senders for s in range(2)]
            )
        return pick(parts, {z: position[z, z] for z in range(places)}) + rightward + leftward

    total_den = along_places(den_sum)
    total_num = along_places(num_sum)
    return (total_num / (PRIOR + total_den), offsets)


def solution(mesh):
    placed = (P("exp", "sky", None), P("exp", "sky", None), P("exp", "sky", None), P(), P())
    return jax.shard_map(
        per_device, mesh=mesh, in_specs=placed, out_specs=(P("sky", "exp"), P()), check_vma=False
    )
```

```python
import functools

import jax
import jax.numpy as jnp
import ml_dtypes
import numpy as np
from jax import lax
from jax.experimental import pallas as pl
from jax.experimental.pallas import tpu as pltpu
from jax.sharding import PartitionSpec as P

BIN = 16
RADIUS = 10
HALO = 16
SIDE = 128
TILE = 256

HIGH = lax.Precision.HIGHEST
LAMBDA_REG = 0.25
PRIOR = 1.0
VMEM = 56 * 1024 * 1024
BF16 = jnp.bfloat16
F32 = jnp.float32
SMALL = pl.CostEstimate(flops=1000, bytes_accessed=1000, transcendentals=0)


def tap_values():
    offs = np.arange(-RADIUS, RADIUS + 1).astype(np.float64)
    taps = np.exp(-offs * offs / 50.0)
    return taps / taps.sum()


def band(out, width, lead):
    taps = tap_values()
    full = np.zeros((out, width), np.float64)
    for shift in range(-RADIUS, RADIUS + 1):
        rows = np.arange(out)
        full[rows, rows + lead + shift] = taps[shift + RADIUS]
    return full


def two_parts(full):
    high = full.astype(np.float32).astype(ml_dtypes.bfloat16)
    low = (full - high.astype(np.float64)).astype(np.float32).astype(ml_dtypes.bfloat16)
    return high, low


def chebyshev(coord, count=3):
    terms = [jnp.ones_like(coord), coord]
    while len(terms) < count:
        terms.append(2.0 * coord * terms[-1] - terms[-2])
    return jnp.stack(terms)


def centers(index, total):
    return (2.0 * index.astype(F32) + 1.0) / total - 1.0


def split_high_low(value):
    high = value.astype(BF16)
    return high, (value - high.astype(F32)).astype(BF16)


def mm(left, right):
    return jnp.dot(left, right, preferred_element_type=F32)


def weights_kernel(plan, units, width, blocks_ref, start_ref, frame_ref, spread_ref, mask_ref, *refs):
    outs, (scatter, gather) = refs[:-2], refs[-2:]
    bins_ref, weights = outs[-1], outs[:-1]
    step = pl.program_id(1)
    block = blocks_ref[step]
    rows, share = frame_ref.shape
    bins_row, bins_col = mask_ref.shape
    per = share // BIN

    @pl.when((pl.program_id(0) == 0) & (step == 0))
    def _():
        cell = lax.broadcasted_iota(jnp.int32, (SIDE, share), 1) >> 4
        scatter[...] = (cell == lax.broadcasted_iota(jnp.int32, (SIDE, share), 0)).astype(BF16)
        cell = lax.broadcasted_iota(jnp.int32, (share, SIDE), 0) >> 4
        gather[...] = (cell == lax.broadcasted_iota(jnp.int32, (share, SIDE), 1)).astype(BF16)

    inverse = 1.0 / spread_ref[...]
    blocks_here = pltpu.roll(mask_ref[...].astype(F32), lax.rem(bins_col - block * per, bins_col), 1)[:, :SIDE]
    kept = mm(blocks_here.astype(BF16), scatter[...])
    first = start_ref[0] * BIN
    col = lax.broadcasted_iota(jnp.int32, (1, share), 1) + block * share
    kept = jnp.where((col >= first) & (col < first + width), kept, 0.0)
    weight = inverse * jnp.broadcast_to(kept[:, None, :], (bins_row, BIN, share)).reshape(rows, share)
    for at, (out, fresh) in enumerate(plan):
        @pl.when(step == at)
        def _(out=out, fresh=fresh):
            if out >= units:
                weights[-1][0] = weight
            elif fresh:
                weights[out][...] = weight
            else:
                weights[out][...] += weight

    def halved(value):
        return value.reshape(bins_row, 2, 8, share).sum(axis=1).reshape(bins_row * 8, share)

    sums = jnp.concatenate([halved(frame_ref[...]), halved(inverse)], axis=0)
    top, rest = split_high_low(sums)
    last = ((sums - top.astype(F32)) - rest.astype(F32)).astype(BF16)
    part = mm(top, gather[...]) + (mm(rest, gather[...]) + mm(last, gather[...]))
    if bins_col > SIDE:
        part = jnp.concatenate([part, jnp.zeros((part.shape[0], bins_col - SIDE), F32)], axis=1)
    part = pltpu.roll(part, block * per, 1)

    @pl.when(step == 0)
    def _():
        bins_ref[0] = part

    @pl.when(step > 0)
    def _():
        bins_ref[0] += part


ANY = pl.BlockSpec(memory_space=pl.ANY)


def rows_of_chunk(rows):
    return min(SIDE, rows)


def pixel_weights(plan, units, blocks, start, frame, spread, mask, share, width, after=()):
    rows = frame.shape[0]
    chunk = rows_of_chunk(rows)
    bins_col = mask.shape[1]
    kept = sum(out >= units for out, fresh in plan)
    lead = len(plan) - kept
    tile = pl.BlockSpec((chunk, share), lambda r, i, blocks, start: (r, blocks[i]))
    out_specs = [pl.BlockSpec((chunk, share), lambda r, i, blocks, start: (r, 0))] * units
    out_shape = [jax.ShapeDtypeStruct((rows, share), F32)] * units
    if kept:
        out_specs.append(
            pl.BlockSpec((1, chunk, share), lambda r, i, blocks, start: (jnp.maximum(i - lead, 0), r, 0))
        )
        out_shape.append(jax.ShapeDtypeStruct((kept, rows, share), F32))
    out_specs.append(pl.BlockSpec((1, chunk, bins_col), lambda r, i, blocks, start: (r, 0, 0)))
    out_shape.append(jax.ShapeDtypeStruct((rows // chunk, chunk, bins_col), F32))

    def body(blocks_ref, start_ref, frame_ref, spread_ref, mask_ref, *refs):
        weights_kernel(plan, units, width, blocks_ref, start_ref, frame_ref, spread_ref, mask_ref, *refs[len(after) :])

    return pl.pallas_call(
        body,
        grid_spec=pltpu.PrefetchScalarGridSpec(
            num_scalar_prefetch=2,
            grid=(rows // chunk, len(plan)),
            in_specs=[
                tile,
                tile,
                pl.BlockSpec((chunk // BIN, bins_col), lambda r, i, blocks, start: (r, 0)),
            ] + [ANY] * len(after),
            out_specs=out_specs,
            scratch_shapes=[pltpu.VMEM((SIDE, share), BF16), pltpu.VMEM((share, SIDE), BF16)],
        ),
        out_shape=out_shape,
        compiler_params=pltpu.CompilerParams(vmem_limit_bytes=VMEM),
        cost_estimate=SMALL,
        name="pixel_weights",
    )(blocks, start, frame, spread, mask, *after)


def smooth_kernel(plan, width, stacked, blocks_ref, start_ref, *refs):
    step = pl.program_id(0)
    images, (col_hi, col_lo, row_hi, row_lo, up_hi, up_lo, down_hi, down_lo) = refs[:9], refs[9:17]
    refs = refs[17:]
    weights, outs = refs[: len(refs) // 2], refs[len(refs) // 2 :]
    block = blocks_ref[step]
    rows, share = images[4].shape
    window = share + 2 * SIDE
    field = jnp.concatenate(
        [jnp.concatenate([images[3 * i + j][...] for j in range(3)], axis=1) for i in range(3)], axis=0
    )
    first = start_ref[0] * BIN
    col = lax.broadcasted_iota(jnp.int32, (1, window), 1) + (block * share - SIDE)
    field = jnp.where((col >= first) & (col < first + width), field, 0.0)
    high, low = split_high_low(field)

    def three(a_hi, a_lo, b_hi, b_lo):
        return mm(a_hi, b_hi) + (mm(a_lo, b_hi) + mm(a_hi, b_lo))

    tiles = []
    for tile in range(share // TILE):
        lanes = slice(tile * TILE, (tile + 1) * TILE + 2 * SIDE)
        tiles.append(three(high[:, lanes], low[:, lanes], col_hi[...], col_lo[...]))
    across = tiles[0] if len(tiles) == 1 else jnp.concatenate(tiles, axis=1)
    high, low = split_high_low(across)
    height = row_hi.shape[0]
    tiles = []
    for tile in range(rows // height):
        top = tile * height
        mid = slice(top + HALO, top + HALO + height)
        upper = slice(top, top + HALO)
        lower = slice(top + HALO + height, top + 2 * HALO + height)
        main = three(row_hi[...], row_lo[...], high[mid], low[mid])
        tiles += [
            main[:HALO] + three(up_hi[...], up_lo[...], high[upper], low[upper]),
            main[HALO : height - HALO],
            main[height - HALO :] + three(down_hi[...], down_lo[...], high[lower], low[lower]),
        ]
    smoothed = jnp.concatenate(tiles, axis=0)
    col = lax.broadcasted_iota(jnp.int32, (1, share), 1) + block * share
    smoothed = jnp.where((col >= first) & (col < first + width), smoothed, 0.0)
    if stacked:
        outs[0][0] = weights[0][0] * smoothed
        return
    for at, (out, fresh) in enumerate(plan):
        @pl.when(step == at)
        def _(out=out, fresh=fresh):
            term = weights[out][...] * smoothed
            outs[out][...] = term if fresh else outs[out][...] + term


def smoothed_terms(plan, weights, blocks, start, frame, above, below, share, width, after=()):
    rows, cols = frame.shape
    stacked = weights[0].ndim == 3
    count = len(weights)
    per = share // SIDE
    last = cols // SIDE - 1
    specs = []
    for height in (HALO, rows, HALO):
        specs += [
            pl.BlockSpec((height, SIDE), lambda i, blocks, start: (0, jnp.maximum(blocks[i] * per - 1, 0))),
            pl.BlockSpec((height, share), lambda i, blocks, start: (0, blocks[i])),
            pl.BlockSpec((height, SIDE), lambda i, blocks, start: (0, jnp.minimum(blocks[i] * per + per, last))),
        ]
    whole = lambda shape: pl.BlockSpec(shape, lambda i, blocks, start: (0, 0))
    if stacked:
        parts_spec = pl.BlockSpec((1, rows, share), lambda i, blocks, start: (i, 0, 0))
    else:
        parts_spec = whole((rows, share))
    height = min(TILE, rows)
    full = band(height, height + 2 * HALO, HALO)
    bands = [
        band(TILE, TILE + 2 * SIDE, SIDE).T,
        full[:, HALO : HALO + height],
        full[:HALO, :HALO],
        full[height - HALO :, HALO + height :],
    ]
    parts = [jnp.asarray(p) for matrix in bands for p in two_parts(matrix)]

    def body(*refs):
        lead = 2 + 9 + len(parts) + count
        smooth_kernel(plan, width, stacked, *refs[:lead], *refs[lead + len(after) :])

    return pl.pallas_call(
        body,
        grid_spec=pltpu.PrefetchScalarGridSpec(
            num_scalar_prefetch=2,
            grid=(len(plan),),
            in_specs=specs + [whole(p.shape) for p in parts] + [parts_spec] * count + [ANY] * len(after),
            out_specs=[parts_spec] * count,
        ),
        out_shape=[jax.ShapeDtypeStruct(w.shape, F32) for w in weights],
        compiler_params=pltpu.CompilerParams(vmem_limit_bytes=VMEM),
        cost_estimate=SMALL,
        name="smoothed_terms",
    )(blocks, start, *([above] * 3 + [frame] * 3 + [below] * 3), *parts, *weights, *after)


def held_until(values, after):
    def body(*refs):
        del refs

    return pl.pallas_call(
        body,
        in_specs=[ANY] * (len(values) + len(after)),
        out_specs=[ANY] * len(values),
        out_shape=[jax.ShapeDtypeStruct(v.shape, v.dtype) for v in values],
        input_output_aliases={i: i for i in range(len(values))},
        compiler_params=pltpu.CompilerParams(vmem_limit_bytes=VMEM),
        cost_estimate=SMALL,
        name="held",
    )(*values, *after)


def contract_last(left, right):
    return lax.dot_general(left, right, (((1,), (1,)), ((), ())), precision=HIGH, preferred_element_type=F32)


def contract_last_three(left, right):
    def one(a, b):
        return lax.dot_general(a, b, (((1,), (1,)), ((), ())), preferred_element_type=F32)

    (l_hi, l_lo), (r_hi, r_lo) = split_high_low(left), split_high_low(right)
    return one(l_hi, r_hi) + (one(l_lo, r_hi) + one(l_hi, r_lo))


def moments_kernel(places, strips, strip_ref, bins_ref, out_ref):
    count, _, rows, cols = bins_ref.shape
    at = [places.index(e) for e in range(count)]
    image = [bins_ref[at[e], 0] for e in range(count)]
    weight = [bins_ref[at[e], 1] for e in range(count)]
    x = centers(lax.broadcasted_iota(jnp.int32, (1, cols), 1), cols)
    tx = [jnp.ones_like(x), x]
    while len(tx) < 5:
        tx.append(2.0 * x * tx[-1] - tx[-2])
    tx = jnp.concatenate(tx + [jnp.zeros((3, cols), F32)], axis=0)
    joint, diffs = [], []
    for apart in range(1, count // 2 + 1):
        group, group_d = [], []
        for i in range(count):
            j = (i + apart) % count
            w = weight[i] * weight[j] / (weight[i] + weight[j] + 1.0)
            group.append(w)
            group_d.append(w * (image[i] - image[j]))
        joint.append(contract_last_three(tx, jnp.concatenate(group, axis=0)))
        diffs.append(contract_last_three(tx, jnp.concatenate(group_d, axis=0)))
    along = jnp.concatenate([jnp.concatenate(joint, axis=1), jnp.concatenate(diffs, axis=1)], axis=0)
    total = along.shape[1]
    row = lax.broadcasted_iota(jnp.int32, (total, SIDE), 0)
    lane = lax.broadcasted_iota(jnp.int32, (total, SIDE), 1)
    mine = row // rows == lane
    y = centers(row % rows + strip_ref[0] * rows, rows * strips)
    a_hi, a_lo = split_high_low(along)
    ty = [jnp.ones_like(y), y]
    for a in range(5):
        if a > 1:
            ty.append(2.0 * y * ty[-1] - ty[-2])
        b_hi, b_lo = split_high_low(jnp.where(mine, ty[a], 0.0))
        out_ref[:, a * SIDE : (a + 1) * SIDE] = mm(a_hi, b_hi) + (mm(a_lo, b_hi) + mm(a_hi, b_lo))


def solve_kernel(moments_ref, owner_ref, out_ref):
    owner = owner_ref[...].astype(F32)
    count = owner.shape[0]
    lanes = count * count // 2
    exposure = lax.broadcasted_iota(jnp.int32, (count, lanes), 0)
    lane = lax.broadcasted_iota(jnp.int32, (count, lanes), 1)
    mine = lane % count
    apart = lane // count + 1
    is_i = (exposure == mine).astype(F32)
    is_j = (exposure == (mine + apart) % count).astype(F32)
    both = owner + owner.T
    listed = jnp.sum(is_i * jnp.dot(both, is_j, precision=HIGH, preferred_element_type=F32), axis=0, keepdims=True)
    lane_row = lax.broadcasted_iota(jnp.int32, (1, lanes), 1)
    once = (lane_row // count + 1 < count // 2) | (lane_row % count < count // 2)
    listed = jnp.where(once, listed, 0.0)
    held = listed > 0.0
    moment = [[moments_ref[b : b + 1, a * SIDE : a * SIDE + lanes] for b in range(5)] for a in range(5)]

    def entry(k, l):
        (u, v), (s, t) = divmod(k, 3), divmod(l, 3)
        total = 0.0
        for a in (u + s, abs(u - s)):
            for b in (v + t, abs(v - t)):
                total = total + moment[a][b]
        return jnp.where(held, 0.25 * total, 1.0 if k == l else 0.0)

    factor = [[None] * 9 for _ in range(9)]
    scale = [None] * 9
    for k in range(9):
        for l in range(k, 9):
            value = entry(l, k)
            for m in range(k):
                value = value - factor[l][m] * factor[k][m]
            if l == k:
                scale[k] = 1.0 / jnp.sqrt(value)
            else:
                factor[l][k] = value * scale[k]
    half = [None] * 9
    for k in range(9):
        a, b = divmod(k, 3)
        value = moments_ref[8 + b : 9 + b, a * SIDE : a * SIDE + lanes]
        for m in range(k):
            value = value - factor[k][m] * half[m]
        half[k] = value * scale[k]
    fit = [None] * 9
    for k in reversed(range(9)):
        value = half[k]
        for m in range(k + 1, 9):
            value = value - factor[m][k] * fit[m]
        fit[k] = value * scale[k]
    fits = jnp.concatenate([jnp.where(held, f, 0.0) for f in fit] + [jnp.zeros((7, lanes), F32)], axis=0)
    right = contract_last((is_i - is_j) * listed, fits)
    row = lax.broadcasted_iota(jnp.int32, (count, count), 0)
    column = lax.broadcasted_iota(jnp.int32, (count, count), 1)
    degree = jnp.sum(both, axis=1, keepdims=True) + LAMBDA_REG
    system = jnp.where(row == column, degree, 0.0) - both
    for k in range(count):
        inverse = 1.0 / system[k : k + 1, k : k + 1]
        pivot_s, pivot_r = system[k : k + 1, :] * inverse, right[k : k + 1, :] * inverse
        lead = system[:, k : k + 1]
        chosen = row[:, :1] == k
        system = jnp.where(chosen, pivot_s, system - lead * pivot_s)
        right = jnp.where(chosen, pivot_r, right - lead * pivot_r)
    out_ref[...] = right[:, :9]


def per_device(image, variance, mask, foot_start, pair_owner):
    frame, spread, blocks = image[0], variance[0], mask[0]
    rows, cols = frame.shape
    bins_row, bins_col = blocks.shape
    exposures, sky_count = lax.axis_size("exp"), lax.axis_size("sky")
    member, strip = lax.axis_index("exp"), lax.axis_index("sky")
    share = cols // exposures
    width = 3 * cols // 4
    places = exposures // 2
    quarter = places // 4
    place, side = member // 2, member % 2
    own_start = lax.dynamic_slice_in_dim(foot_start, member, 1)
    mate_start = lax.dynamic_slice_in_dim(foot_start, member + 1 - 2 * side, 1)

    order = np.zeros((places, places), np.int32)
    for z in range(places):
        down = z < places // 2
        ends = range(quarter)
        middle = list(range(quarter, places - quarter))
        listed = []
        for q in ends:
            low = quarter - 1 - q if down else q
            listed += [low, low + places - quarter]
        order[z] = listed + (middle[::-1] if down else middle)
    middle_count = places - 2 * quarter
    my_order = lax.dynamic_index_in_dim(jnp.asarray(order), place, 0, keepdims=False)
    sent_blocks = 2 * my_order + (1 - side)
    kept_blocks = 2 * my_order + side
    ends = 2 * quarter
    folded = [(i // 2, i % 2 == 0) for i in range(ends)]
    middle = [(i, True) for i in range(middle_count)]
    plain = [(middle_count + i, True) for i in range(places)]

    up = [(i, i + 1) for i in range(sky_count - 1)]
    down = [(j, i) for i, j in up]
    above = lax.ppermute(frame[rows - HALO :], "sky", up)
    below = lax.ppermute(frame[:HALO], "sky", down)

    swap = [(i, i ^ 1) for i in range(exposures)]

    def swapped(parts):
        return [lax.ppermute(part, "exp", swap) for part in parts]

    *den_ends, bins_a = pixel_weights(
        folded, quarter, sent_blocks[:ends], own_start, frame, spread, blocks, share, width
    )
    got_ends = swapped(den_ends)
    *den_middle, den_kept, bins_b = pixel_weights(
        middle + plain,
        middle_count,
        jnp.concatenate([sent_blocks[ends:], kept_blocks]),
        own_start,
        frame,
        spread,
        blocks,
        share,
        width,
        after=(bins_a,),
    )

    bins = (bins_a + bins_b).reshape(-1, 2, bins_row * rows_of_chunk(rows) // rows, 8, bins_col).sum(axis=3)
    bins = bins.swapaxes(0, 1).reshape(2, bins_row, bins_col)
    cell = jnp.arange(bins_col)
    inside_bins = (cell >= own_start) & (cell < own_start + width // BIN)
    keep = jnp.where(inside_bins[None, :], blocks, 0).astype(F32)
    gathered = jnp.stack([bins[0] / (BIN * BIN), bins[1] * keep])[None]
    smooth = functools.partial(
        smoothed_terms, start=own_start, frame=frame, above=above, below=below, share=share, width=width
    )
    held = [0]
    bits = [1 << k for k in range(exposures.bit_length() - 1)]

    def gather_along(gathered, bit):
        other = lax.ppermute(gathered, "exp", [(i, i ^ bit) for i in range(exposures)])
        low = (member & bit) == 0
        held.extend([e | bit for e in held])
        return jnp.concatenate([jnp.where(low, gathered, other), jnp.where(low, other, gathered)])

    num_ends = smooth(folded, den_ends, sent_blocks[:ends], after=(bins_b,))
    gathered = gather_along(gathered, bits[1])
    (gathered,) = held_until([gathered], num_ends)
    for bit in bits[2:]:
        gathered = gather_along(gathered, bit)
    num_middle = smooth(middle, den_middle, sent_blocks[ends:], after=num_ends)
    gathered, *den_middle = held_until([gathered, *den_middle], num_middle)
    gathered = gather_along(gathered, bits[0])
    got_middle = swapped(den_middle)
    den_got = got_ends + got_middle
    num_got = []
    for k, part in enumerate(num_ends + num_middle):
        num_got += swapped(held_until([part], [(got_middle + num_got)[k]]))

    position = np.zeros((places, places), np.int32)
    for z in range(places):
        position[z, order[z]] = np.arange(places)

    def by_place(values):
        table = np.zeros((places,), np.int32)
        for z, value in values.items():
            table[z] = value
        return lax.dynamic_index_in_dim(jnp.asarray(table), place, 0, keepdims=False)

    def pick(parts, wanted):
        unit = {z: (at // 2 if at < ends else at - quarter) for z, at in wanted.items()}
        value = None
        for u in sorted(set(unit.values())):
            if value is None:
                value = parts[u]
                continue
            here = functools.reduce(jnp.logical_or, [place == z for z, w in unit.items() if w == u])
            value = jnp.where(here, parts[u], value)
        return value

    def own_and_mate(wanted, *arrays):
        at = by_place(wanted)
        block = kept_blocks[at]
        col = jnp.arange(share) + block * share
        inside = ((col >= mate_start * BIN) & (col < mate_start * BIN + width))[None, :]
        out = []
        for own, got in arrays:
            out.append(lax.dynamic_index_in_dim(own, at, 0, keepdims=False))
            out.append(jnp.where(inside, pick(got, wanted), 0.0))
        return block, out

    def along_places(term):
        rightward = leftward = None
        values = []

        def shift(value, rights, lefts):
            pairs = [(2 * z + s, 2 * z + 2 + s) for z in rights for s in range(2)]
            pairs += [(2 * z + s, 2 * z - 2 + s) for z in lefts for s in range(2)]
            return lax.ppermute(value, "exp", pairs)

        for step in range(1, places):
            rights = {z: position[z, z + places - step] for z in range(step)}
            lefts = {z: position[z, z - places + step] for z in range(places - step, places)}
            if step < places - 1 - step:
                value = term(rights | lefts)
                if rightward is not None:
                    value = value + jnp.where(place < places // 2, rightward, leftward)
                values.append(value)
                both = shift(value, rights, lefts)
                rightward = jnp.where(place <= step, both, 0.0)
                leftward = jnp.where(place >= places - 1 - step, both, 0.0)
                continue
            value = term(rights)
            value = value if rightward is None else value + rightward
            back = term(lefts)
            back = back if leftward is None else back + leftward
            values += [value, back]
            rightward = shift(value, rights, [])
            leftward = shift(back, [], lefts)
        return term({z: position[z, z] for z in range(places)}) + rightward + leftward, values

    def den_term(wanted):
        block, (own, mate) = own_and_mate(wanted, (den_kept, den_got))
        return own + mate

    total_den, den_values = along_places(den_term)
    (num_kept,) = smooth(
        [(i, True) for i in range(places)], [den_kept], kept_blocks, after=(den_values[0], *num_middle)
    )

    (gathered,) = held_until([gathered], [num_kept])
    moments = pl.pallas_call(
        functools.partial(moments_kernel, held, sky_count),
        in_specs=[pl.BlockSpec(memory_space=pltpu.SMEM), pl.BlockSpec(memory_space=pltpu.VMEM)],
        out_shape=jax.ShapeDtypeStruct((16, 5 * SIDE), F32),
        compiler_params=pltpu.CompilerParams(vmem_limit_bytes=VMEM),
        cost_estimate=SMALL,
        name="pair_moments",
    )(strip[None], gathered)
    bit = 1
    while bit < sky_count:
        moments = moments + lax.ppermute(moments, "sky", [(i, i ^ bit) for i in range(sky_count)])
        bit *= 2
    offsets = pl.pallas_call(
        solve_kernel,
        out_shape=jax.ShapeDtypeStruct((exposures, 9), F32),
        cost_estimate=SMALL,
        name="offsets",
    )(moments, pair_owner)

    taps = tap_values().astype(np.float32)
    row_at = jnp.arange(-RADIUS, rows + RADIUS) + strip * rows
    ty = chebyshev(centers(row_at, rows * sky_count))
    ty = jnp.where((row_at >= 0) & (row_at < rows * sky_count), ty, 0.0)
    rows_part = sum(float(taps[t]) * ty[:, t : t + rows] for t in range(2 * RADIUS + 1))
    col_at = jnp.arange(-RADIUS, cols + RADIUS)
    tx = chebyshev(centers(col_at, cols))

    def columns_part(start):
        masked = jnp.where((col_at >= start * BIN) & (col_at < start * BIN + width), tx, 0.0)
        return sum(float(taps[t]) * masked[:, t : t + cols] for t in range(2 * RADIUS + 1))

    def coefficients(which, start):
        coeffs = lax.dynamic_index_in_dim(offsets, which, 0, keepdims=False).reshape(3, 3)
        return jnp.sum(coeffs[:, :, None] * columns_part(start)[None], axis=1)

    own_back = coefficients(member, own_start)
    mate_back = coefficients(member + 1 - 2 * side, mate_start)

    def background(back, block):
        cut = lax.dynamic_slice_in_dim(back, block * share, share, 1)
        return sum(rows_part[u][:, None] * cut[u][None, :] for u in range(3))

    def num_term(wanted):
        block, (own, mate, own_den, mate_den) = own_and_mate(wanted, (num_kept, num_got), (den_kept, den_got))
        return (own - own_den * background(own_back, block)) + (mate - mate_den * background(mate_back, block))

    total_num, _ = along_places(num_term)
    return (total_num / (PRIOR + total_den), offsets)


def solution(mesh):
    placed = (P("exp", "sky", None), P("exp", "sky", None), P("exp", "sky", None), P(), P())
    return jax.shard_map(
        per_device, mesh=mesh, in_specs=placed, out_specs=(P("sky", "exp"), P()), check_vma=False
    )
```

```python
import functools

import jax
import jax.numpy as jnp
import numpy as np
from jax import lax
from jax.experimental import pallas as pl
from jax.experimental.pallas import tpu as pltpu
from jax.sharding import PartitionSpec as P

BIN = 16
RADIUS = 10
HALO = 16
SIDE = 128
TILE = 256

HIGH = lax.Precision.HIGHEST
LAMBDA_REG = 0.25
PRIOR = 1.0
VMEM = 56 * 1024 * 1024
BF16 = jnp.bfloat16
F32 = jnp.float32
SMALL = pl.CostEstimate(flops=1000, bytes_accessed=1000, transcendentals=0)


def tap_values():
    offs = np.arange(-RADIUS, RADIUS + 1).astype(np.float64)
    taps = np.exp(-offs * offs / 50.0)
    return taps / taps.sum()


def band(out, width, lead):
    taps = tap_values()
    full = np.zeros((out, width), np.float64)
    for shift in range(-RADIUS, RADIUS + 1):
        rows = np.arange(out)
        full[rows, rows + lead + shift] = taps[shift + RADIUS]
    return full


def centers(index, total):
    return (2.0 * index.astype(F32) + 1.0) / total - 1.0


def split_high_low(value):
    high = value.astype(BF16)
    return high, (value - high.astype(F32)).astype(BF16)


def mm(left, right):
    return jnp.dot(left, right, preferred_element_type=F32)


def choose(condition, left, right):
    if isinstance(condition, (bool, np.bool_)):
        return left if condition else right
    return jnp.where(condition, left, right)


class Places:
    def __init__(self, exposures, cols):
        self.share = cols // exposures
        self.places = exposures // 2
        self.quarter = self.places // 4
        self.ends = 2 * self.quarter
        self.middle = self.places - self.ends

    def place_of(self, at, place):
        down = place < self.places // 2
        pair = at // 2
        end = choose(down, self.quarter - 1 - pair, pair) + (at % 2) * (self.places - self.quarter)
        turn = at - self.ends
        mid = choose(down, self.places - self.quarter - 1 - turn, self.quarter + turn)
        return choose(at < self.ends, end, mid)

    def position_of(self, wanted, place):
        down = place < self.places // 2
        right = wanted >= self.places - self.quarter
        low = choose(right, wanted - (self.places - self.quarter), wanted)
        pair = choose(down, self.quarter - 1 - low, low)
        turn = choose(down, self.places - self.quarter - 1 - wanted, wanted - self.quarter)
        is_end = right | (wanted < self.quarter)
        at = choose(is_end, 2 * pair + choose(right, 1, 0), self.ends + turn)
        return at, choose(is_end, pair, self.quarter + turn)

    def sent_block(self, at, meta):
        return 2 * self.place_of(at, meta[0] // 2) + 1 - meta[0] % 2

    def kept_block(self, at, meta):
        return 2 * self.place_of(at, meta[0] // 2) + meta[0] % 2


def inside(col, start, width):
    return (col >= start * BIN) & (col < start * BIN + width)


def columns(block, share, width=None, lead=0):
    return lax.broadcasted_iota(jnp.int32, (1, width or share), 1) + (block * share - lead)


def weights_kernel(block_of, plan, units, width, meta_ref, start_ref, frame_ref, spread_ref, mask_ref, *refs):
    weights, (bins_ref, total, scatter, gather) = refs[:-4], refs[-4:]
    step = pl.program_id(0)
    block = block_of(step, meta_ref)
    start = start_ref[meta_ref[0]]
    rows, share = frame_ref.shape
    bins_row, bins_col = mask_ref.shape
    per = share // BIN

    @pl.when(step == 0)
    def _():
        cell = lax.broadcasted_iota(jnp.int32, (SIDE, share), 1) >> 4
        scatter[...] = (cell == lax.broadcasted_iota(jnp.int32, (SIDE, share), 0)).astype(BF16)
        cell = lax.broadcasted_iota(jnp.int32, (share, SIDE), 0) >> 4
        gather[...] = (cell == lax.broadcasted_iota(jnp.int32, (share, SIDE), 1)).astype(BF16)
        total[...] = jnp.zeros_like(total)

    inverse = 1.0 / spread_ref[...]
    blocks_here = pltpu.roll(mask_ref[...].astype(F32), lax.rem(bins_col - block * per, bins_col), 1)[:, :SIDE]
    kept = mm(blocks_here.astype(BF16), scatter[...])
    kept = jnp.where(inside(columns(block, share), start, width), kept, 0.0)
    weight = inverse * jnp.broadcast_to(kept[:, None, :], (bins_row, BIN, share)).reshape(rows, share)
    for at, (out, fresh) in enumerate(plan):
        @pl.when(step == at)
        def _(out=out, fresh=fresh):
            if out >= units:
                weights[-1][0] = weight
            elif fresh:
                weights[out][...] = weight
            else:
                weights[out][...] += weight

    def halved(value):
        return value.reshape(bins_row, 2, 8, share).sum(axis=1).reshape(bins_row * 8, share)

    sums = jnp.concatenate([halved(frame_ref[...]), halved(inverse)], axis=0)
    top, rest = split_high_low(sums)
    last = ((sums - top.astype(F32)) - rest.astype(F32)).astype(BF16)
    part = mm(top, gather[...]) + (mm(rest, gather[...]) + mm(last, gather[...]))
    if bins_col > SIDE:
        part = jnp.concatenate([part, jnp.zeros((part.shape[0], bins_col - SIDE), F32)], axis=1)
    total[...] += pltpu.roll(part, block * per, 1)

    @pl.when(step == len(plan) - 1)
    def _():
        bins = total[...].reshape(2 * bins_row, 8, bins_col).sum(axis=1)
        cell = lax.broadcasted_iota(jnp.int32, (1, bins_col), 1) * BIN
        keep = jnp.where(inside(cell, start, width), mask_ref[...].astype(F32), 0.0)
        bins_ref[0, 0] = bins[:bins_row] / (BIN * BIN)
        bins_ref[0, 1] = bins[bins_row:] * keep


ANY = pl.BlockSpec(memory_space=pl.ANY)


def whole(shape):
    return pl.BlockSpec(shape, lambda *_: (0,) * len(shape))


def pixel_weights(block_of, plan, units, meta, starts, frame, spread, mask, share, width):
    rows = frame.shape[0]
    bins_row, bins_col = mask.shape
    kept = sum(out >= units for out, fresh in plan)
    lead = len(plan) - kept
    tile = pl.BlockSpec((rows, share), lambda i, meta, starts: (0, block_of(i, meta)))
    bins = (1, 2, bins_row, bins_col)
    return pl.pallas_call(
        functools.partial(weights_kernel, block_of, plan, units, width),
        grid_spec=pltpu.PrefetchScalarGridSpec(
            num_scalar_prefetch=2,
            grid=(len(plan),),
            in_specs=[tile, tile, whole(mask.shape)],
            out_specs=[whole((rows, share))] * units
            + [pl.BlockSpec((1, rows, share), lambda i, meta, starts: (jnp.maximum(i - lead, 0), 0, 0)), whole(bins)],
            scratch_shapes=[
                pltpu.VMEM((rows, bins_col), F32), pltpu.VMEM((SIDE, share), BF16), pltpu.VMEM((share, SIDE), BF16)
            ],
        ),
        out_shape=[pltpu.HBM((rows, share), F32)] * units
        + [pltpu.HBM((kept, rows, share), F32), jax.ShapeDtypeStruct(bins, F32)],
        compiler_params=pltpu.CompilerParams(vmem_limit_bytes=VMEM),
        cost_estimate=SMALL,
        name="pixel_weights",
    )(meta, starts, frame, spread, mask)


def smooth_kernel(block_of, plan, width, stacked, meta_ref, start_ref, *refs):
    step = pl.program_id(0)
    images, bands, scratch = refs[:9], refs[9:13], refs[-8:]
    refs = refs[13:-8]
    weights, outs = refs[: len(refs) // 2], refs[len(refs) // 2 :]

    @pl.when(step == 0)
    def _():
        for k, matrix in enumerate(bands):
            scratch[2 * k][...], scratch[2 * k + 1][...] = split_high_low(matrix[...])

    col_hi, col_lo, row_hi, row_lo, up_hi, up_lo, down_hi, down_lo = scratch
    block = block_of(step, meta_ref)
    start = start_ref[meta_ref[0]]
    rows, share = images[4].shape
    window = share + 2 * SIDE
    field = jnp.concatenate(
        [jnp.concatenate([images[3 * i + j][...] for j in range(3)], axis=1) for i in range(3)], axis=0
    )
    field = jnp.where(inside(columns(block, share, window, SIDE), start, width), field, 0.0)
    high, low = split_high_low(field)

    def three(a_hi, a_lo, b_hi, b_lo):
        return mm(a_hi, b_hi) + (mm(a_lo, b_hi) + mm(a_hi, b_lo))

    tiles = []
    for tile in range(share // TILE):
        lanes = slice(tile * TILE, (tile + 1) * TILE + 2 * SIDE)
        tiles.append(three(high[:, lanes], low[:, lanes], col_hi[...], col_lo[...]))
    across = tiles[0] if len(tiles) == 1 else jnp.concatenate(tiles, axis=1)
    high, low = split_high_low(across)
    height = row_hi.shape[0]
    tiles = []
    for tile in range(rows // height):
        top = tile * height
        mid = slice(top + HALO, top + HALO + height)
        upper = slice(top, top + HALO)
        lower = slice(top + HALO + height, top + 2 * HALO + height)
        main = three(row_hi[...], row_lo[...], high[mid], low[mid])
        tiles += [
            main[:HALO] + three(up_hi[...], up_lo[...], high[upper], low[upper]),
            main[HALO : height - HALO],
            main[height - HALO :] + three(down_hi[...], down_lo[...], high[lower], low[lower]),
        ]
    smoothed = jnp.concatenate(tiles, axis=0)
    smoothed = jnp.where(inside(columns(block, share), start, width), smoothed, 0.0)
    if stacked:
        outs[0][0] = weights[0][0] * smoothed
        return
    for at, (out, fresh) in enumerate(plan):
        @pl.when(step == at)
        def _(out=out, fresh=fresh):
            term = weights[out][...] * smoothed
            outs[out][...] = term if fresh else outs[out][...] + term


def smoothed_terms(block_of, plan, weights, meta, starts, frame, above, below, share, width, after=()):
    rows, cols = frame.shape
    stacked = weights[0].ndim == 3
    count = len(weights)
    per = share // SIDE
    last = cols // SIDE - 1
    specs = []
    for height in (HALO, rows, HALO):
        specs += [
            pl.BlockSpec((height, SIDE), lambda i, m, s: (0, jnp.maximum(block_of(i, m) * per - 1, 0))),
            pl.BlockSpec((height, share), lambda i, m, s: (0, block_of(i, m))),
            pl.BlockSpec((height, SIDE), lambda i, m, s: (0, jnp.minimum(block_of(i, m) * per + per, last))),
        ]
    if stacked:
        parts_spec = pl.BlockSpec((1, rows, share), lambda i, m, s: (i, 0, 0))
    else:
        parts_spec = whole((rows, share))
    height = min(TILE, rows)
    full = band(height, height + 2 * HALO, HALO)
    bands = [
        band(TILE, TILE + 2 * SIDE, SIDE).T,
        full[:, HALO : HALO + height],
        full[:HALO, :HALO],
        full[height - HALO :, HALO + height :],
    ]
    parts = [jnp.asarray(matrix.astype(np.float32)) for matrix in bands]

    def body(*refs):
        lead = 2 + 9 + len(parts) + count
        smooth_kernel(block_of, plan, width, stacked, *refs[:lead], *refs[lead + len(after) :])

    return pl.pallas_call(
        body,
        grid_spec=pltpu.PrefetchScalarGridSpec(
            num_scalar_prefetch=2,
            grid=(len(plan),),
            in_specs=specs + [whole(p.shape) for p in parts] + [parts_spec] * count + [ANY] * len(after),
            out_specs=[parts_spec] * count,
            scratch_shapes=[pltpu.VMEM(p.shape, BF16) for p in parts for _ in range(2)],
        ),
        out_shape=[pltpu.HBM(w.shape, F32) for w in weights],
        compiler_params=pltpu.CompilerParams(vmem_limit_bytes=VMEM),
        cost_estimate=SMALL,
        name="smoothed_terms",
    )(meta, starts, *([above] * 3 + [frame] * 3 + [below] * 3), *parts, *weights, *after)


def term_kernel(layout, width, wanted, units, received, numerator, meta_ref, start_ref, *refs):
    place = meta_ref[0] // 2
    block = 2 * wanted(place) + meta_ref[0] % 2
    _, unit = layout.position_of(wanted(place), place)
    mate_start = start_ref[meta_ref[0] + 1 - 2 * (meta_ref[0] % 2)]
    in_mate = inside(columns(block, layout.share), mate_start, width)
    *refs, out_ref = refs

    def pair():
        own = refs.pop(0)[0]
        got = refs.pop(0)[...]
        for u in units[1:]:
            got = jnp.where(unit == u, refs.pop(0)[...], got)
        return own, got

    def added(own, got, names):
        value = own + jnp.where(in_mate, got, 0.0)
        for _ in range(names):
            value = value + refs.pop(0)[...]
        return value

    if not numerator:
        out_ref[...] = added(*pair(), received)
        return
    own_den, mate_den = pair()
    own, mate = pair()
    rows_part, back = refs.pop(0)[...], refs.pop(0)[...]
    own_back = sum(rows_part[:, u : u + 1] * back[u : u + 1, :] for u in range(3))
    mate_back = sum(rows_part[:, u : u + 1] * back[3 + u : 4 + u, :] for u in range(3))
    top = added(own - own_den * own_back, mate - mate_den * mate_back, received)
    if numerator == "quotient":
        out_ref[...] = top / (PRIOR + added(own_den, mate_den, received))
    else:
        out_ref[...] = top


def block_term(layout, width, wanted, senders, meta, starts, parts, received, numerator=None, tables=(), after=()):
    kept = parts[0][0]
    rows, share = kept.shape[1:]
    chunk = min(SIDE, rows)

    def at_unit(place):
        return layout.position_of(wanted(place), place)

    units = sorted({int(at_unit(z)[1]) for z in senders})
    flat = pl.BlockSpec((chunk, share), lambda r, m, s: (r, 0))
    specs, args = [], []
    for own, got in parts:
        specs.append(pl.BlockSpec((1, chunk, share), lambda r, m, s: (at_unit(m[0] // 2)[0], r, 0)))
        args.append(own)
        for u in units:
            specs.append(
                flat
                if len(units) == 1
                else pl.BlockSpec(
                    (chunk, share), lambda r, m, s, u=u: (jnp.where(at_unit(m[0] // 2)[1] == u, r, 0), 0)
                )
            )
            args.append(got[u])
    if numerator:
        rows_part, back = tables
        strips = rows // chunk
        specs.append(pl.BlockSpec((chunk, rows_part.shape[1]), lambda r, m, s: (m[1] * strips + r, 0)))
        specs.append(
            pl.BlockSpec((back.shape[0], share), lambda r, m, s: (0, 2 * wanted(m[0] // 2) + m[0] % 2))
        )
        args += [rows_part, back]
    for sums in received:
        specs += [flat] * len(sums)
        args += list(sums)
    lead = 2 + len(args)
    body = functools.partial(term_kernel, layout, width, wanted, units, len(received[0]), numerator)
    return pl.pallas_call(
        lambda *refs: body(*refs[:lead], refs[-1]),
        grid_spec=pltpu.PrefetchScalarGridSpec(
            num_scalar_prefetch=2, grid=(rows // chunk,), in_specs=specs + [ANY] * len(after), out_specs=flat
        ),
        out_shape=jax.ShapeDtypeStruct((rows, share), F32)
        if numerator == "quotient"
        else pltpu.HBM((rows, share), F32),
        compiler_params=pltpu.CompilerParams(vmem_limit_bytes=VMEM),
        cost_estimate=SMALL,
        name="block_term",
    )(meta, starts, *args, *after)


def held_until(values, after):
    def body(*refs):
        del refs

    return pl.pallas_call(
        body,
        in_specs=[ANY] * (len(values) + len(after)),
        out_specs=[ANY] * len(values),
        out_shape=[jax.ShapeDtypeStruct(v.shape, v.dtype) for v in values],
        input_output_aliases={i: i for i in range(len(values))},
        compiler_params=pltpu.CompilerParams(vmem_limit_bytes=VMEM),
        cost_estimate=SMALL,
        name="held",
    )(*values, *after)


def contract_last(left, right):
    return lax.dot_general(left, right, (((1,), (1,)), ((), ())), precision=HIGH, preferred_element_type=F32)


def contract_last_three(left, right):
    def one(a, b):
        return lax.dot_general(a, b, (((1,), (1,)), ((), ())), preferred_element_type=F32)

    (l_hi, l_lo), (r_hi, r_lo) = split_high_low(left), split_high_low(right)
    return one(l_hi, r_hi) + (one(l_lo, r_hi) + one(l_hi, r_lo))


def moments_kernel(places, strips, meta_ref, bins_ref, out_ref):
    count, _, rows, cols = bins_ref.shape
    at = [places.index(e) for e in range(count)]
    image = [bins_ref[at[e], 0] for e in range(count)]
    weight = [bins_ref[at[e], 1] for e in range(count)]
    x = centers(lax.broadcasted_iota(jnp.int32, (1, cols), 1), cols)
    tx = [jnp.ones_like(x), x]
    while len(tx) < 5:
        tx.append(2.0 * x * tx[-1] - tx[-2])
    tx = jnp.concatenate(tx + [jnp.zeros((3, cols), F32)], axis=0)
    joint, diffs = [], []
    for apart in range(1, count // 2 + 1):
        group, group_d = [], []
        for i in range(count):
            j = (i + apart) % count
            w = weight[i] * weight[j] / (weight[i] + weight[j] + 1.0)
            group.append(w)
            group_d.append(w * (image[i] - image[j]))
        joint.append(contract_last_three(tx, jnp.concatenate(group, axis=0)))
        diffs.append(contract_last_three(tx, jnp.concatenate(group_d, axis=0)))
    along = jnp.concatenate([jnp.concatenate(joint, axis=1), jnp.concatenate(diffs, axis=1)], axis=0)
    total = along.shape[1]
    row = lax.broadcasted_iota(jnp.int32, (total, SIDE), 0)
    lane = lax.broadcasted_iota(jnp.int32, (total, SIDE), 1)
    mine = row // rows == lane
    y = centers(row % rows + meta_ref[1] * rows, rows * strips)
    a_hi, a_lo = split_high_low(along)
    ty = [jnp.ones_like(y), y]
    for a in range(5):
        if a > 1:
            ty.append(2.0 * y * ty[-1] - ty[-2])
        b_hi, b_lo = split_high_low(jnp.where(mine, ty[a], 0.0))
        out_ref[:, a * SIDE : (a + 1) * SIDE] = mm(a_hi, b_hi) + (mm(a_lo, b_hi) + mm(a_hi, b_lo))


def solve_kernel(width, meta_ref, start_ref, moments_ref, owner_ref, out_ref, back_ref):
    owner = owner_ref[...].astype(F32)
    count = owner.shape[0]
    lanes = count * count // 2
    exposure = lax.broadcasted_iota(jnp.int32, (count, lanes), 0)
    lane = lax.broadcasted_iota(jnp.int32, (count, lanes), 1)
    mine = lane % count
    apart = lane // count + 1
    is_i = (exposure == mine).astype(F32)
    is_j = (exposure == (mine + apart) % count).astype(F32)
    both = owner + owner.T
    listed = jnp.sum(is_i * jnp.dot(both, is_j, precision=HIGH, preferred_element_type=F32), axis=0, keepdims=True)
    lane_row = lax.broadcasted_iota(jnp.int32, (1, lanes), 1)
    once = (lane_row // count + 1 < count // 2) | (lane_row % count < count // 2)
    listed = jnp.where(once, listed, 0.0)
    held = listed > 0.0
    moment = [[moments_ref[b : b + 1, a * SIDE : a * SIDE + lanes] for b in range(5)] for a in range(5)]

    def entry(k, l):
        (u, v), (s, t) = divmod(k, 3), divmod(l, 3)
        total = 0.0
        for a in (u + s, abs(u - s)):
            for b in (v + t, abs(v - t)):
                total = total + moment[a][b]
        return jnp.where(held, 0.25 * total, 1.0 if k == l else 0.0)

    factor = [[None] * 9 for _ in range(9)]
    scale = [None] * 9
    for k in range(9):
        for l in range(k, 9):
            value = entry(l, k)
            for m in range(k):
                value = value - factor[l][m] * factor[k][m]
            if l == k:
                scale[k] = 1.0 / jnp.sqrt(value)
            else:
                factor[l][k] = value * scale[k]
    half = [None] * 9
    for k in range(9):
        a, b = divmod(k, 3)
        value = moments_ref[8 + b : 9 + b, a * SIDE : a * SIDE + lanes]
        for m in range(k):
            value = value - factor[k][m] * half[m]
        half[k] = value * scale[k]
    fit = [None] * 9
    for k in reversed(range(9)):
        value = half[k]
        for m in range(k + 1, 9):
            value = value - factor[m][k] * fit[m]
        fit[k] = value * scale[k]
    fits = jnp.concatenate([jnp.where(held, f, 0.0) for f in fit] + [jnp.zeros((7, lanes), F32)], axis=0)
    right = contract_last((is_i - is_j) * listed, fits)
    row = lax.broadcasted_iota(jnp.int32, (count, count), 0)
    column = lax.broadcasted_iota(jnp.int32, (count, count), 1)
    degree = jnp.sum(both, axis=1, keepdims=True) + LAMBDA_REG
    system = jnp.where(row == column, degree, 0.0) - both
    for k in range(count):
        inverse = 1.0 / system[k : k + 1, k : k + 1]
        pivot_s, pivot_r = system[k : k + 1, :] * inverse, right[k : k + 1, :] * inverse
        lead = system[:, k : k + 1]
        chosen = row[:, :1] == k
        system = jnp.where(chosen, pivot_s, system - lead * pivot_s)
        right = jnp.where(chosen, pivot_r, right - lead * pivot_r)
    out_ref[...] = right[:, :9]
    member = meta_ref[0]
    mate = member + 1 - 2 * (member % 2)
    cols = back_ref.shape[1]
    padded = cols + 2 * SIDE
    col = lax.broadcasted_iota(jnp.int32, (1, padded), 1) - SIDE
    x = centers(col, cols)
    terms = [jnp.ones_like(x), x, 2.0 * x * x - 1.0]
    fields = [jnp.where(inside(col, start_ref[e], width), t, 0.0) for e in (member, mate) for t in terms]
    fields = jnp.concatenate(fields + [jnp.zeros((2, padded), F32)], axis=0)
    taps = tap_values()
    total = float(taps[RADIUS]) * fields
    for shift in range(1, RADIUS + 1):
        both = pltpu.roll(fields, shift, 1) + pltpu.roll(fields, padded - shift, 1)
        total = total + float(taps[RADIUS + shift]) * both
    total = total[:, SIDE : SIDE + cols]
    rows = lax.broadcasted_iota(jnp.int32, (count, 16), 0)
    for k, which in enumerate((member, mate)):
        mine = jnp.sum(jnp.where(rows == which, right, 0.0), axis=0, keepdims=True)
        for u in range(3):
            back_ref[3 * k + u : 3 * k + u + 1, :] = sum(
                mine[:, 3 * u + v : 3 * u + v + 1] * total[3 * k + v : 3 * k + v + 1, :] for v in range(3)
            )
    back_ref[6:8, :] = jnp.zeros((2, cols), F32)


def filtered_rows(total_rows):
    y = (2.0 * np.arange(total_rows) + 1.0) / total_rows - 1.0
    terms = np.stack([np.ones_like(y), y, 2.0 * y * y - 1.0])
    padded = np.pad(terms, ((0, 0), (RADIUS, RADIUS)))
    taps = tap_values()
    return sum(taps[t] * padded[:, t : t + total_rows] for t in range(2 * RADIUS + 1)).T.astype(np.float32)


def per_device(image, variance, mask, foot_start, pair_owner):
    frame, spread, blocks = image[0], variance[0], mask[0]
    rows, cols = frame.shape
    exposures, sky_count = lax.axis_size("exp"), lax.axis_size("sky")
    member = lax.axis_index("exp")
    meta = jnp.stack([member, lax.axis_index("sky")])
    width = 3 * cols // 4
    layout = Places(exposures, cols)
    share, places, quarter = layout.share, layout.places, layout.quarter
    ends, middle_count = layout.ends, layout.middle
    units = quarter + middle_count
    sent = [(i // 2, i % 2 == 0) for i in range(ends)] + [(quarter + i, True) for i in range(middle_count)]
    kept = [(units + i, True) for i in range(places)]

    def sent_then_kept(i, meta):
        return jnp.where(i < places, layout.sent_block(i, meta), layout.kept_block(i - places, meta))

    swap = [(i, i ^ 1) for i in range(exposures)]

    def swapped(parts):
        return [lax.ppermute(part, "exp", swap) for part in parts]

    *den_sent, den_kept, gathered = pixel_weights(
        sent_then_kept, sent + kept, units, meta, foot_start, frame, spread, blocks, share, width
    )

    held = [0]
    bit = 1
    while bit < exposures:
        other = lax.ppermute(gathered, "exp", [(i, i ^ bit) for i in range(exposures)])
        low = (member & bit) == 0
        held = held + [e | bit for e in held]
        gathered = jnp.concatenate([jnp.where(low, gathered, other), jnp.where(low, other, gathered)])
        bit *= 2

    up = [(i, i + 1) for i in range(sky_count - 1)]
    down = [(j, i) for i, j in up]
    above = lax.ppermute(frame[rows - HALO :], "sky", up)
    below = lax.ppermute(frame[:HALO], "sky", down)
    den_got = swapped(den_sent)
    smooth = functools.partial(
        smoothed_terms, meta=meta, starts=foot_start, frame=frame, above=above, below=below, share=share, width=width
    )
    num_sent = smooth(layout.sent_block, sent, den_sent)
    num_got = swapped(num_sent)

    def to_right(step):
        return lambda z: choose(z < step, z + places - step, places - 1)

    def to_left(step):
        return lambda z: choose(z >= places - step, z - places + step, 0)

    def outward(step):
        return lambda z: choose(z < places // 2, to_right(step)(z), to_left(step)(z))

    def shift(value, rights, lefts):
        pairs = [(2 * z + s, 2 * z + 2 + s) for z in rights for s in range(2)]
        pairs += [(2 * z + s, 2 * z - 2 + s) for z in lefts for s in range(2)]
        return lax.ppermute(value, "exp", pairs)

    def along_places(step, term, sums, after):
        rights, lefts = range(step), range(places - step, places)
        if step <= places // 2:
            value = term(outward(step), [*rights, *lefts], sums, after)
            if step < places // 2:
                return (shift(value, rights, lefts),), (value,)
            return (shift(value, rights, []), shift(value, [], lefts)), (value,)
        right = term(to_right(step), rights, sums[:1], after)
        left = term(to_left(step), lefts, sums[1:], after)
        return (shift(right, rights, []), shift(left, [], lefts)), (right, left)

    def den_term(wanted, senders, sums, after):
        parts = [(den_kept, den_got)]
        return block_term(layout, width, wanted, senders, meta, foot_start, parts, [sums], after=after)

    den_sums, den_values = along_places(1, den_term, (), ())
    (num_kept,) = smooth(layout.kept_block, kept, [den_kept], after=num_sent)

    (gathered,) = held_until([gathered], [*num_sent, *den_values])
    scalars = pl.BlockSpec(memory_space=pltpu.SMEM)
    vmem = pl.BlockSpec(memory_space=pltpu.VMEM)
    moments = pl.pallas_call(
        functools.partial(moments_kernel, held, sky_count),
        in_specs=[scalars, vmem],
        out_shape=jax.ShapeDtypeStruct((16, 5 * SIDE), F32),
        compiler_params=pltpu.CompilerParams(vmem_limit_bytes=VMEM),
        cost_estimate=SMALL,
        name="pair_moments",
    )(meta, gathered)
    bit = 1
    while bit < sky_count:
        moments = moments + lax.ppermute(moments, "sky", [(i, i ^ bit) for i in range(sky_count)])
        if bit == 1:
            (moments,) = held_until([moments], [num_kept])
        bit *= 2
    offsets, back = pl.pallas_call(
        functools.partial(solve_kernel, width),
        in_specs=[scalars, scalars, vmem, vmem],
        out_shape=[jax.ShapeDtypeStruct((exposures, 9), F32), jax.ShapeDtypeStruct((8, cols), F32)],
        compiler_params=pltpu.CompilerParams(vmem_limit_bytes=VMEM),
        cost_estimate=SMALL,
        name="offsets",
    )(meta, foot_start, moments, pair_owner)

    tables = (jnp.asarray(filtered_rows(rows * sky_count)), back)
    parts = [(den_kept, den_got), (num_kept, num_got)]

    def num_term(wanted, senders, sums, after):
        return block_term(
            layout, width, wanted, senders, meta, foot_start, parts, [sums], "terms", tables, after
        )

    num_sums, num_values = along_places(1, num_term, (), den_values)
    for step in range(2, places):
        den_sums, den_values = along_places(step, den_term, den_sums, num_values)
        num_sums, num_values = along_places(step, num_term, num_sums, den_values)
    coadd = block_term(
        layout,
        width,
        lambda z: z,
        range(places),
        meta,
        foot_start,
        parts,
        [num_sums, den_sums],
        "quotient",
        tables,
    )
    return (coadd, offsets)


def solution(mesh):
    placed = (P("exp", "sky", None), P("exp", "sky", None), P("exp", "sky", None), P(), P())
    return jax.shard_map(
        per_device, mesh=mesh, in_specs=placed, out_specs=(P("sky", "exp"), P()), check_vma=False
    )
```

```python
import functools

import jax
import jax.numpy as jnp
import numpy as np
from jax import lax
from jax.experimental import pallas as pl
from jax.experimental.pallas import tpu as pltpu
from jax.sharding import PartitionSpec as P

BIN = 16
RADIUS = 10
HALO = 16
SIDE = 128
TOKEN = (8, 128)
TILE = 256

HIGH = lax.Precision.HIGHEST
LAMBDA_REG = 0.25
PRIOR = 1.0
VMEM = 127 * 512 * 1024
SOME = 24 * 1024 * 1024
BF16 = jnp.bfloat16
F32 = jnp.float32
SMALL = pl.CostEstimate(flops=1000, bytes_accessed=1000, transcendentals=0)


def tap_values():
    offs = np.arange(-RADIUS, RADIUS + 1).astype(np.float64)
    taps = np.exp(-offs * offs / 50.0)
    return taps / taps.sum()


def band(out, width, lead):
    taps = tap_values()
    full = np.zeros((out, width), np.float64)
    for shift in range(-RADIUS, RADIUS + 1):
        rows = np.arange(out)
        full[rows, rows + lead + shift] = taps[shift + RADIUS]
    return full


def centers(index, total):
    return (2.0 * index.astype(F32) + 1.0) / total - 1.0


def split_high_low(value):
    high = value.astype(BF16)
    return high, (value - high.astype(F32)).astype(BF16)


def mm(left, right):
    return jnp.dot(left, right, preferred_element_type=F32)


def choose(condition, left, right):
    if isinstance(condition, (bool, np.bool_)):
        return left if condition else right
    return jnp.where(condition, left, right)


class Places:
    def __init__(self, exposures, cols):
        self.share = cols // exposures
        self.places = exposures // 2
        self.quarter = self.places // 4
        self.ends = 2 * self.quarter
        self.middle = self.places - self.ends

    def place_of(self, at, place):
        down = place < self.places // 2
        pair = at // 2
        end = choose(down, self.quarter - 1 - pair, pair) + (at % 2) * (self.places - self.quarter)
        turn = at - self.ends
        mid = choose(down, self.places - self.quarter - 1 - turn, self.quarter + turn)
        return choose(at < self.ends, end, mid)

    def position_of(self, wanted, place):
        down = place < self.places // 2
        right = wanted >= self.places - self.quarter
        low = choose(right, wanted - (self.places - self.quarter), wanted)
        pair = choose(down, self.quarter - 1 - low, low)
        turn = choose(down, self.places - self.quarter - 1 - wanted, wanted - self.quarter)
        is_end = right | (wanted < self.quarter)
        at = choose(is_end, 2 * pair + choose(right, 1, 0), self.ends + turn)
        return at, choose(is_end, pair, self.quarter + turn)

    def sent_block(self, at, meta):
        return 2 * self.place_of(at, meta[0] // 2) + 1 - meta[0] % 2

    def kept_block(self, at, meta):
        return 2 * self.place_of(at, meta[0] // 2) + meta[0] % 2


def inside(col, start, width):
    return (col >= start * BIN) & (col < start * BIN + width)


def columns(block, share, width=None, lead=0):
    return lax.broadcasted_iota(jnp.int32, (1, width or share), 1) + (block * share - lead)


def weights_kernel(block_of, plan, units, width, meta_ref, start_ref, *refs):
    binned = len(refs) > 4 + units
    frame_ref, refs = (refs[0], refs[1:]) if binned else (None, refs)
    spread_ref, mask_ref, *refs = refs
    weights, scratch = (refs[:-4], refs[-4:]) if binned else (refs[:-1], refs[-1:])
    scatter = scratch[-1]
    step = pl.program_id(0)
    block = block_of(step, meta_ref)
    start = start_ref[meta_ref[0]]
    rows, share = spread_ref.shape
    bins_row, bins_col = mask_ref.shape
    per = share // BIN

    @pl.when(step == 0)
    def _():
        cell = lax.broadcasted_iota(jnp.int32, (SIDE, share), 1) >> 4
        scatter[...] = (cell == lax.broadcasted_iota(jnp.int32, (SIDE, share), 0)).astype(BF16)

    inverse = 1.0 / spread_ref[...]
    blocks_here = pltpu.roll(mask_ref[...].astype(F32), lax.rem(bins_col - block * per, bins_col), 1)[:, :SIDE]
    kept = mm(blocks_here.astype(BF16), scatter[...])
    kept = jnp.where(inside(columns(block, share), start, width), kept, 0.0)
    weight = inverse * jnp.broadcast_to(kept[:, None, :], (bins_row, BIN, share)).reshape(rows, share)
    for at, part in enumerate(plan):
        if part is None:
            continue

        @pl.when(step == at)
        def _(out=part[0], fresh=part[1]):
            if out >= units:
                weights[-1][0] = weight
            elif fresh:
                weights[out][...] = weight
            else:
                weights[out][...] += weight

    if not binned:
        return
    bins_ref, total, gather, _ = scratch

    @pl.when(step == 0)
    def _():
        cell = lax.broadcasted_iota(jnp.int32, (share, SIDE), 0) >> 4
        gather[...] = (cell == lax.broadcasted_iota(jnp.int32, (share, SIDE), 1)).astype(BF16)
        total[...] = jnp.zeros_like(total)

    def halved(value):
        return value.reshape(bins_row, 2, 8, share).sum(axis=1).reshape(bins_row * 8, share)

    def gathered(value, parts):
        result = None
        for _ in range(parts):
            rounded = value.astype(BF16)
            value = value - rounded.astype(F32)
            product = mm(rounded, gather[...])
            result = product if result is None else result + product
        if bins_col > SIDE:
            result = jnp.concatenate([result, jnp.zeros((result.shape[0], bins_col - SIDE), F32)], axis=1)
        return pltpu.roll(result, block * per, 1)

    half = bins_row * 8
    total[:half] += gathered(halved(frame_ref[...]), 3)
    total[half:] += gathered(halved(inverse), 2)

    @pl.when(step == len(plan) - 1)
    def _():
        bins = total[...].reshape(2 * bins_row, 8, bins_col).sum(axis=1)
        cell = lax.broadcasted_iota(jnp.int32, (1, bins_col), 1) * BIN
        keep = jnp.where(inside(cell, start, width), mask_ref[...].astype(F32), 0.0)
        bins_ref[0, 0] = bins[:bins_row] / (BIN * BIN)
        bins_ref[0, 1] = bins[bins_row:] * keep


ANY = pl.BlockSpec(memory_space=pl.ANY)


def whole(shape):
    return pl.BlockSpec(shape, lambda *_: (0,) * len(shape))


def pixel_weights(block_of, plan, units, meta, starts, frame, spread, mask, share, width, after=()):
    rows = spread.shape[0]
    bins_row, bins_col = mask.shape
    kept = sum(part is not None and part[0] >= units for part in plan)
    lead = len(plan) - kept
    tile = pl.BlockSpec((rows, share), lambda i, meta, starts: (0, block_of(i, meta)))
    out_specs = [whole((rows, share))] * units
    out_shape = [pltpu.HBM((rows, share), F32)] * units
    scratch = [pltpu.VMEM((SIDE, share), BF16)]
    images = []
    if frame is not None:
        images = [frame]
        bins = (1, 2, bins_row, bins_col)
        out_specs += [
            pl.BlockSpec((1, rows, share), lambda i, meta, starts: (jnp.maximum(i - lead, 0), 0, 0)), whole(bins)
        ]
        out_shape += [pltpu.HBM((kept, rows, share), F32), jax.ShapeDtypeStruct(bins, F32)]
        scratch = [pltpu.VMEM((rows, bins_col), F32), pltpu.VMEM((share, SIDE), BF16)] + scratch
    given = 2 + len(images) + 2
    kernel = functools.partial(weights_kernel, block_of, plan, units, width)
    return pl.pallas_call(
        lambda *refs: kernel(*refs[:given], *refs[given + len(after) :]),
        grid_spec=pltpu.PrefetchScalarGridSpec(
            num_scalar_prefetch=2,
            grid=(len(plan),),
            in_specs=[tile] * len(images) + [tile, whole(mask.shape)] + [ANY] * len(after),
            out_specs=out_specs,
            scratch_shapes=scratch,
        ),
        out_shape=out_shape,
        compiler_params=pltpu.CompilerParams(vmem_limit_bytes=VMEM),
        cost_estimate=SMALL,
        name="pixel_weights",
    )(meta, starts, *images, spread, mask, *after)


def smooth_kernel(block_of, plan, width, stacked, meta_ref, start_ref, *refs):
    step = pl.program_id(0)
    images, bands, scratch = refs[:9], refs[9:13], refs[-8:]
    refs = refs[13:-8]
    weights, outs = refs[: len(refs) // 2], refs[len(refs) // 2 :]

    @pl.when(step == 0)
    def _():
        for k, matrix in enumerate(bands):
            scratch[2 * k][...], scratch[2 * k + 1][...] = split_high_low(matrix[...])

    col_hi, col_lo, row_hi, row_lo, up_hi, up_lo, down_hi, down_lo = scratch
    block = block_of(step, meta_ref)
    start = start_ref[meta_ref[0]]
    rows, share = images[4].shape
    window = share + 2 * SIDE
    field = jnp.concatenate(
        [jnp.concatenate([images[3 * i + j][...] for j in range(3)], axis=1) for i in range(3)], axis=0
    )
    field = jnp.where(inside(columns(block, share, window, SIDE), start, width), field, 0.0)
    high, low = split_high_low(field)

    def three(a_hi, a_lo, b_hi, b_lo):
        return mm(a_hi, b_hi) + (mm(a_lo, b_hi) + mm(a_hi, b_lo))

    tiles = []
    for tile in range(share // TILE):
        lanes = slice(tile * TILE, (tile + 1) * TILE + 2 * SIDE)
        tiles.append(three(high[:, lanes], low[:, lanes], col_hi[...], col_lo[...]))
    across = tiles[0] if len(tiles) == 1 else jnp.concatenate(tiles, axis=1)
    high, low = split_high_low(across)
    height = row_hi.shape[0]
    tiles = []
    for tile in range(rows // height):
        top = tile * height
        mid = slice(top + HALO, top + HALO + height)
        upper = slice(top, top + HALO)
        lower = slice(top + HALO + height, top + 2 * HALO + height)
        main = three(row_hi[...], row_lo[...], high[mid], low[mid])
        tiles += [
            main[:HALO] + three(up_hi[...], up_lo[...], high[upper], low[upper]),
            main[HALO : height - HALO],
            main[height - HALO :] + three(down_hi[...], down_lo[...], high[lower], low[lower]),
        ]
    smoothed = jnp.concatenate(tiles, axis=0)
    smoothed = jnp.where(inside(columns(block, share), start, width), smoothed, 0.0)
    if stacked:
        outs[0][0] = weights[0][0] * smoothed
        return
    for at, (out, fresh) in enumerate(plan):
        @pl.when(step == at)
        def _(out=out, fresh=fresh):
            term = weights[out][...] * smoothed
            outs[out][...] = term if fresh else outs[out][...] + term


def smoothed_terms(block_of, plan, weights, meta, starts, frame, above, below, share, width, after=()):
    rows, cols = frame.shape
    stacked = weights[0].ndim == 3
    count = len(weights)
    per = share // SIDE
    last = cols // SIDE - 1
    specs = []
    for height in (HALO, rows, HALO):
        specs += [
            pl.BlockSpec((height, SIDE), lambda i, m, s: (0, jnp.maximum(block_of(i, m) * per - 1, 0))),
            pl.BlockSpec((height, share), lambda i, m, s: (0, block_of(i, m))),
            pl.BlockSpec((height, SIDE), lambda i, m, s: (0, jnp.minimum(block_of(i, m) * per + per, last))),
        ]
    if stacked:
        parts_spec = pl.BlockSpec((1, rows, share), lambda i, m, s: (i, 0, 0))
    else:
        parts_spec = whole((rows, share))
    height = min(TILE, rows)
    full = band(height, height + 2 * HALO, HALO)
    bands = [
        band(TILE, TILE + 2 * SIDE, SIDE).T,
        full[:, HALO : HALO + height],
        full[:HALO, :HALO],
        full[height - HALO :, HALO + height :],
    ]
    parts = [jnp.asarray(matrix.astype(np.float32)) for matrix in bands]

    def body(*refs):
        lead = 2 + 9 + len(parts) + count
        smooth_kernel(block_of, plan, width, stacked, *refs[:lead], *refs[lead + len(after) :])

    return pl.pallas_call(
        body,
        grid_spec=pltpu.PrefetchScalarGridSpec(
            num_scalar_prefetch=2,
            grid=(len(plan),),
            in_specs=specs + [whole(p.shape) for p in parts] + [parts_spec] * count + [ANY] * len(after),
            out_specs=[parts_spec] * count,
            scratch_shapes=[pltpu.VMEM(p.shape, BF16) for p in parts for _ in range(2)],
        ),
        out_shape=[pltpu.HBM(w.shape, F32) for w in weights],
        compiler_params=pltpu.CompilerParams(vmem_limit_bytes=VMEM),
        cost_estimate=SMALL,
        name="smoothed_terms",
    )(meta, starts, *([above] * 3 + [frame] * 3 + [below] * 3), *parts, *weights, *after)


def term_kernel(layout, width, wanted, units, received, numerator, meta_ref, start_ref, *refs):
    place = meta_ref[0] // 2
    block = 2 * wanted(place) + meta_ref[0] % 2
    _, unit = layout.position_of(wanted(place), place)
    mate_start = start_ref[meta_ref[0] + 1 - 2 * (meta_ref[0] % 2)]
    in_mate = inside(columns(block, layout.share), mate_start, width)
    *refs, out_ref, token_ref = refs
    token_ref[...] = jnp.zeros_like(token_ref)

    def pair():
        own = refs.pop(0)[0]
        got = refs.pop(0)[...]
        for u in units[1:]:
            got = jnp.where(unit == u, refs.pop(0)[...], got)
        return own, got

    def added(own, got, names):
        value = own + jnp.where(in_mate, got, 0.0)
        for _ in range(names):
            value = value + refs.pop(0)[...]
        return value

    if not numerator:
        out_ref[...] = added(*pair(), received)
        return
    own_den, mate_den = pair()
    own, mate = pair()
    rows_part, back = refs.pop(0)[...], refs.pop(0)[...]
    own_back = sum(rows_part[:, u : u + 1] * back[u : u + 1, :] for u in range(3))
    mate_back = sum(rows_part[:, u : u + 1] * back[3 + u : 4 + u, :] for u in range(3))
    top = added(own - own_den * own_back, mate - mate_den * mate_back, received)
    if numerator == "quotient":
        out_ref[...] = top / (PRIOR + added(own_den, mate_den, received))
    else:
        out_ref[...] = top


def block_term(layout, width, wanted, senders, meta, starts, parts, received, numerator=None, tables=(), after=()):
    kept = parts[0][0]
    rows, share = kept.shape[1:]
    chunk = min(TILE, rows)

    def at_unit(place):
        return layout.position_of(wanted(place), place)

    units = sorted({int(at_unit(z)[1]) for z in senders})
    flat = pl.BlockSpec((chunk, share), lambda r, m, s: (r, 0))
    specs, args = [], []
    for own, got in parts:
        specs.append(pl.BlockSpec((1, chunk, share), lambda r, m, s: (at_unit(m[0] // 2)[0], r, 0)))
        args.append(own)
        for u in units:
            specs.append(
                flat
                if len(units) == 1
                else pl.BlockSpec(
                    (chunk, share), lambda r, m, s, u=u: (jnp.where(at_unit(m[0] // 2)[1] == u, r, 0), 0)
                )
            )
            args.append(got[u])
    if numerator:
        rows_part, back = tables
        strips = rows // chunk
        specs.append(pl.BlockSpec((chunk, rows_part.shape[1]), lambda r, m, s: (m[1] * strips + r, 0)))
        specs.append(
            pl.BlockSpec((back.shape[0], share), lambda r, m, s: (0, 2 * wanted(m[0] // 2) + m[0] % 2))
        )
        args += [rows_part, back]
    for sums in received:
        specs += [flat] * len(sums)
        args += list(sums)
    lead = 2 + len(args)
    body = functools.partial(term_kernel, layout, width, wanted, units, len(received[0]), numerator)
    return pl.pallas_call(
        lambda *refs: body(*refs[:lead], *refs[-2:]),
        grid_spec=pltpu.PrefetchScalarGridSpec(
            num_scalar_prefetch=2, grid=(rows // chunk,), in_specs=specs + [ANY] * len(after), out_specs=[flat, whole(TOKEN)]
        ),
        out_shape=[jax.ShapeDtypeStruct((rows, share), F32), jax.ShapeDtypeStruct(TOKEN, F32)],
        compiler_params=pltpu.CompilerParams(vmem_limit_bytes=SOME),
        cost_estimate=SMALL,
        name="block_term",
    )(meta, starts, *args, *after)


def held_until(values, after):
    def body(*refs):
        del refs

    return pl.pallas_call(
        body,
        in_specs=[ANY] * (len(values) + len(after)),
        out_specs=[ANY] * len(values),
        out_shape=[jax.ShapeDtypeStruct(v.shape, v.dtype) for v in values],
        input_output_aliases={i: i for i in range(len(values))},
        compiler_params=pltpu.CompilerParams(vmem_limit_bytes=VMEM),
        cost_estimate=SMALL,
        name="held",
    )(*values, *after)


def arrived(values):
    def body(*refs):
        refs[-1][...] = jnp.zeros_like(refs[-1])

    return pl.pallas_call(
        body,
        in_specs=[ANY] * len(values),
        out_shape=jax.ShapeDtypeStruct(TOKEN, F32),
        compiler_params=pltpu.CompilerParams(vmem_limit_bytes=SOME),
        cost_estimate=pl.CostEstimate(flops=1000, bytes_accessed=8 * 10**6, transcendentals=0),
        name="arrived",
    )(*values)


def contract_last(left, right):
    return lax.dot_general(left, right, (((1,), (1,)), ((), ())), precision=HIGH, preferred_element_type=F32)


def contract_last_three(left, right):
    def one(a, b):
        return lax.dot_general(a, b, (((1,), (1,)), ((), ())), preferred_element_type=F32)

    (l_hi, l_lo), (r_hi, r_lo) = split_high_low(left), split_high_low(right)
    return one(l_hi, r_hi) + (one(l_lo, r_hi) + one(l_hi, r_lo))


def moments_kernel(places, strips, meta_ref, bins_ref, out_ref):
    count, _, rows, cols = bins_ref.shape
    at = [places.index(e) for e in range(count)]
    image = [bins_ref[at[e], 0] for e in range(count)]
    weight = [bins_ref[at[e], 1] for e in range(count)]
    x = centers(lax.broadcasted_iota(jnp.int32, (1, cols), 1), cols)
    tx = [jnp.ones_like(x), x]
    while len(tx) < 5:
        tx.append(2.0 * x * tx[-1] - tx[-2])
    tx = jnp.concatenate(tx + [jnp.zeros((3, cols), F32)], axis=0)
    joint, diffs = [], []
    for apart in range(1, count // 2 + 1):
        group, group_d = [], []
        for i in range(count):
            j = (i + apart) % count
            w = weight[i] * weight[j] / (weight[i] + weight[j] + 1.0)
            group.append(w)
            group_d.append(w * (image[i] - image[j]))
        joint.append(contract_last_three(tx, jnp.concatenate(group, axis=0)))
        diffs.append(contract_last_three(tx, jnp.concatenate(group_d, axis=0)))
    along = jnp.concatenate([jnp.concatenate(joint, axis=1), jnp.concatenate(diffs, axis=1)], axis=0)
    total = along.shape[1]
    row = lax.broadcasted_iota(jnp.int32, (total, SIDE), 0)
    lane = lax.broadcasted_iota(jnp.int32, (total, SIDE), 1)
    mine = row // rows == lane
    y = centers(row % rows + meta_ref[1] * rows, rows * strips)
    a_hi, a_lo = split_high_low(along)
    ty = [jnp.ones_like(y), y]
    for a in range(5):
        if a > 1:
            ty.append(2.0 * y * ty[-1] - ty[-2])
        b_hi, b_lo = split_high_low(jnp.where(mine, ty[a], 0.0))
        out_ref[:, a * SIDE : (a + 1) * SIDE] = mm(a_hi, b_hi) + (mm(a_lo, b_hi) + mm(a_hi, b_lo))


def solve_kernel(width, meta_ref, start_ref, moments_ref, owner_ref, out_ref, back_ref):
    owner = owner_ref[...].astype(F32)
    count = owner.shape[0]
    lanes = count * count // 2
    exposure = lax.broadcasted_iota(jnp.int32, (count, lanes), 0)
    lane = lax.broadcasted_iota(jnp.int32, (count, lanes), 1)
    mine = lane % count
    apart = lane // count + 1
    is_i = (exposure == mine).astype(F32)
    is_j = (exposure == (mine + apart) % count).astype(F32)
    both = owner + owner.T
    listed = jnp.sum(is_i * jnp.dot(both, is_j, precision=HIGH, preferred_element_type=F32), axis=0, keepdims=True)
    lane_row = lax.broadcasted_iota(jnp.int32, (1, lanes), 1)
    once = (lane_row // count + 1 < count // 2) | (lane_row % count < count // 2)
    listed = jnp.where(once, listed, 0.0)
    held = listed > 0.0
    moment = [[moments_ref[b : b + 1, a * SIDE : a * SIDE + lanes] for b in range(5)] for a in range(5)]

    def entry(k, l):
        (u, v), (s, t) = divmod(k, 3), divmod(l, 3)
        total = 0.0
        for a in (u + s, abs(u - s)):
            for b in (v + t, abs(v - t)):
                total = total + moment[a][b]
        return jnp.where(held, 0.25 * total, 1.0 if k == l else 0.0)

    factor = [[None] * 9 for _ in range(9)]
    scale = [None] * 9
    for k in range(9):
        for l in range(k, 9):
            value = entry(l, k)
            for m in range(k):
                value = value - factor[l][m] * factor[k][m]
            if l == k:
                scale[k] = 1.0 / jnp.sqrt(value)
            else:
                factor[l][k] = value * scale[k]
    half = [None] * 9
    for k in range(9):
        a, b = divmod(k, 3)
        value = moments_ref[8 + b : 9 + b, a * SIDE : a * SIDE + lanes]
        for m in range(k):
            value = value - factor[k][m] * half[m]
        half[k] = value * scale[k]
    fit = [None] * 9
    for k in reversed(range(9)):
        value = half[k]
        for m in range(k + 1, 9):
            value = value - factor[m][k] * fit[m]
        fit[k] = value * scale[k]
    fits = jnp.concatenate([jnp.where(held, f, 0.0) for f in fit] + [jnp.zeros((7, lanes), F32)], axis=0)
    right = contract_last((is_i - is_j) * listed, fits)
    row = lax.broadcasted_iota(jnp.int32, (count, count), 0)
    column = lax.broadcasted_iota(jnp.int32, (count, count), 1)
    degree = jnp.sum(both, axis=1, keepdims=True) + LAMBDA_REG
    system = jnp.where(row == column, degree, 0.0) - both
    for k in range(count):
        inverse = 1.0 / system[k : k + 1, k : k + 1]
        pivot_s, pivot_r = system[k : k + 1, :] * inverse, right[k : k + 1, :] * inverse
        lead = system[:, k : k + 1]
        chosen = row[:, :1] == k
        system = jnp.where(chosen, pivot_s, system - lead * pivot_s)
        right = jnp.where(chosen, pivot_r, right - lead * pivot_r)
    out_ref[...] = right[:, :9]
    member = meta_ref[0]
    mate = member + 1 - 2 * (member % 2)
    cols = back_ref.shape[1]
    padded = cols + 2 * SIDE
    col = lax.broadcasted_iota(jnp.int32, (1, padded), 1) - SIDE
    x = centers(col, cols)
    terms = [jnp.ones_like(x), x, 2.0 * x * x - 1.0]
    fields = [jnp.where(inside(col, start_ref[e], width), t, 0.0) for e in (member, mate) for t in terms]
    fields = jnp.concatenate(fields + [jnp.zeros((2, padded), F32)], axis=0)
    taps = tap_values()
    total = float(taps[RADIUS]) * fields
    for shift in range(1, RADIUS + 1):
        both = pltpu.roll(fields, shift, 1) + pltpu.roll(fields, padded - shift, 1)
        total = total + float(taps[RADIUS + shift]) * both
    total = total[:, SIDE : SIDE + cols]
    rows = lax.broadcasted_iota(jnp.int32, (count, 16), 0)
    for k, which in enumerate((member, mate)):
        mine = jnp.sum(jnp.where(rows == which, right, 0.0), axis=0, keepdims=True)
        for u in range(3):
            back_ref[3 * k + u : 3 * k + u + 1, :] = sum(
                mine[:, 3 * u + v : 3 * u + v + 1] * total[3 * k + v : 3 * k + v + 1, :] for v in range(3)
            )
    back_ref[6:8, :] = jnp.zeros((2, cols), F32)


def filtered_rows(total_rows):
    y = (2.0 * np.arange(total_rows) + 1.0) / total_rows - 1.0
    terms = np.stack([np.ones_like(y), y, 2.0 * y * y - 1.0])
    padded = np.pad(terms, ((0, 0), (RADIUS, RADIUS)))
    taps = tap_values()
    return sum(taps[t] * padded[:, t : t + total_rows] for t in range(2 * RADIUS + 1)).T.astype(np.float32)


def per_device(image, variance, mask, foot_start, pair_owner):
    frame, spread, blocks = image[0], variance[0], mask[0]
    rows, cols = frame.shape
    exposures, sky_count = lax.axis_size("exp"), lax.axis_size("sky")
    member = lax.axis_index("exp")
    meta = jnp.stack([member, lax.axis_index("sky")])
    width = 3 * cols // 4
    layout = Places(exposures, cols)
    share, places, quarter = layout.share, layout.places, layout.quarter
    ends, middle_count = layout.ends, layout.middle
    units = quarter + middle_count
    folded = [(i // 2, i % 2 == 0) for i in range(ends)]
    sent = folded + [(quarter + i, True) for i in range(middle_count)]
    rest = [None] * ends + [(i, True) for i in range(middle_count + places)]

    def sent_then_kept(i, meta):
        return jnp.where(i < places, layout.sent_block(i, meta), layout.kept_block(i - places, meta))

    swap = [(i, i ^ 1) for i in range(exposures)]

    def swapped(parts):
        return [lax.ppermute(part, "exp", swap) for part in parts]

    den_ends = pixel_weights(
        layout.sent_block, folded, quarter, meta, foot_start, None, spread, blocks, share, width
    )
    *den_middle, den_kept, gathered = pixel_weights(
        sent_then_kept, rest, middle_count, meta, foot_start, frame, spread, blocks, share, width, after=den_ends
    )
    got_ends = swapped(den_ends)

    held = [0]
    bits = [1 << k for k in range(exposures.bit_length() - 1)]
    for bit in bits[1:] + bits[:1]:
        if bit == 1:
            (gathered,) = held_until([gathered], got_ends)
        other = lax.ppermute(gathered, "exp", [(i, i ^ bit) for i in range(exposures)])
        low = (member & bit) == 0
        held = held + [e | bit for e in held]
        gathered = jnp.concatenate([jnp.where(low, gathered, other), jnp.where(low, other, gathered)])
    up = [(i, i + 1) for i in range(sky_count - 1)]
    down = [(j, i) for i, j in up]
    above = lax.ppermute(frame[rows - HALO :], "sky", up)
    below = lax.ppermute(frame[:HALO], "sky", down)
    smooth = functools.partial(
        smoothed_terms, meta=meta, starts=foot_start, frame=frame, above=above, below=below, share=share, width=width
    )
    def to_right(step):
        return lambda z: choose(z < step, z + places - step, places - 1)

    def to_left(step):
        return lambda z: choose(z >= places - step, z - places + step, 0)

    def outward(step):
        return lambda z: choose(z < places // 2, to_right(step)(z), to_left(step)(z))

    def shift(value, rights, lefts):
        pairs = [(2 * z + s, 2 * z + 2 + s) for z in rights for s in range(2)]
        pairs += [(2 * z + s, 2 * z - 2 + s) for z in lefts for s in range(2)]
        return lax.ppermute(value, "exp", pairs)

    def along_places(step, term, sums, after, after_left=()):
        rights, lefts = range(step), range(places - step, places)
        if step <= places // 2:
            value, token = term(outward(step), [*rights, *lefts], sums, after)
            if step < places // 2:
                return (shift(value, rights, lefts),), (token,)
            return (shift(value, rights, []), shift(value, [], lefts)), (token,)
        right, token = term(to_right(step), rights, sums[:1], (*after, sums[1]))
        left, token_left = term(to_left(step), lefts, sums[1:], after_left or after)
        return (shift(right, rights, []), shift(left, [], lefts)), (token, token_left)

    def den_term(wanted, senders, sums, after):
        parts = [(den_kept, got_ends + got_middle)]
        return block_term(layout, width, wanted, senders, meta, foot_start, parts, [sums], after=after)

    got_middle = []
    den_sums, den_values = along_places(1, den_term, (), ())
    den_middle = held_until(den_middle, den_values)
    got_middle = swapped(den_middle)
    den_got = got_ends + got_middle
    num_sent = smooth(layout.sent_block, sent, [*den_ends, *den_middle], after=[gathered])
    num_got = swapped(num_sent)
    (num_kept,) = smooth(layout.kept_block, [(i, True) for i in range(places)], [den_kept], after=num_sent)

    scalars = pl.BlockSpec(memory_space=pltpu.SMEM)
    vmem = pl.BlockSpec(memory_space=pltpu.VMEM)
    moments = pl.pallas_call(
        functools.partial(moments_kernel, held, sky_count),
        in_specs=[scalars, vmem],
        out_shape=jax.ShapeDtypeStruct((16, 5 * SIDE), F32),
        compiler_params=pltpu.CompilerParams(vmem_limit_bytes=SOME),
        cost_estimate=SMALL,
        name="pair_moments",
    )(meta, gathered)
    bit = 1
    while bit < sky_count:
        moments = moments + lax.ppermute(moments, "sky", [(i, i ^ bit) for i in range(sky_count)])
        bit *= 2
    offsets, back = pl.pallas_call(
        functools.partial(solve_kernel, width),
        in_specs=[scalars, scalars, vmem, vmem],
        out_shape=[jax.ShapeDtypeStruct((exposures, 9), F32), jax.ShapeDtypeStruct((8, cols), F32)],
        compiler_params=pltpu.CompilerParams(vmem_limit_bytes=SOME),
        cost_estimate=SMALL,
        name="offsets",
    )(meta, foot_start, moments, pair_owner)

    tables = (jnp.asarray(filtered_rows(rows * sky_count)), back)
    parts = [(den_kept, den_got), (num_kept, num_got)]

    def num_term(wanted, senders, sums, after):
        return block_term(
            layout, width, wanted, senders, meta, foot_start, parts, [sums], "terms", tables, after
        )

    den_sums, den_values = along_places(2, den_term, den_sums, ())
    num_sums, num_values = along_places(1, num_term, (), den_values)
    num_sums, num_values = along_places(2, num_term, num_sums, [arrived(den_sums)])
    for step in range(3, places):
        den_sums, den_values = along_places(step, den_term, den_sums, num_values)
        num_sums, num_values = along_places(step, num_term, num_sums, den_values, [arrived(den_sums)])
    coadd, _ = block_term(
        layout,
        width,
        lambda z: z,
        range(places),
        meta,
        foot_start,
        parts,
        [num_sums, den_sums],
        "quotient",
        tables,
    )
    return (coadd, offsets)


def solution(mesh):
    placed = (P("exp", "sky", None), P("exp", "sky", None), P("exp", "sky", None), P(), P())
    return jax.shard_map(
        per_device, mesh=mesh, in_specs=placed, out_specs=(P("sky", "exp"), P()), check_vma=False
    )
```

```python
import functools

import jax
import jax.numpy as jnp
import numpy as np
from jax import lax
from jax.experimental import pallas as pl
from jax.experimental.pallas import tpu as pltpu
from jax.sharding import PartitionSpec as P

BIN = 16
RADIUS = 10
HALO = 16
SIDE = 128
TOKEN = (8, 128)
TILE = 256
CHUNK = 64

HIGH = lax.Precision.HIGHEST
LAMBDA_REG = 0.25
PRIOR = 1.0
VMEM = 127 * 512 * 1024
SOME = 24 * 1024 * 1024
BF16 = jnp.bfloat16
F32 = jnp.float32
SMALL = pl.CostEstimate(flops=1000, bytes_accessed=1000, transcendentals=0)


def tap_values():
    offs = np.arange(-RADIUS, RADIUS + 1).astype(np.float64)
    taps = np.exp(-offs * offs / 50.0)
    return taps / taps.sum()


def band(out, width, lead):
    taps = tap_values()
    full = np.zeros((out, width), np.float64)
    for shift in range(-RADIUS, RADIUS + 1):
        rows = np.arange(out)
        full[rows, rows + lead + shift] = taps[shift + RADIUS]
    return full


def centers(index, total):
    return (2.0 * index.astype(F32) + 1.0) / total - 1.0


def split_high_low(value):
    high = value.astype(BF16)
    return high, (value - high.astype(F32)).astype(BF16)


def mm(left, right):
    return jnp.dot(left, right, preferred_element_type=F32)


def choose(condition, left, right):
    if isinstance(condition, (bool, np.bool_)):
        return left if condition else right
    return jnp.where(condition, left, right)


class Places:
    def __init__(self, exposures, cols):
        self.share = cols // exposures
        self.places = exposures // 2
        self.quarter = self.places // 4
        self.ends = 2 * self.quarter
        self.middle = self.places - self.ends

    def place_of(self, at, place):
        down = place < self.places // 2
        pair = at // 2
        end = choose(down, self.quarter - 1 - pair, pair) + (at % 2) * (self.places - self.quarter)
        turn = at - self.ends
        mid = choose(down, self.places - self.quarter - 1 - turn, self.quarter + turn)
        return choose(at < self.ends, end, mid)

    def position_of(self, wanted, place):
        down = place < self.places // 2
        right = wanted >= self.places - self.quarter
        low = choose(right, wanted - (self.places - self.quarter), wanted)
        pair = choose(down, self.quarter - 1 - low, low)
        turn = choose(down, self.places - self.quarter - 1 - wanted, wanted - self.quarter)
        is_end = right | (wanted < self.quarter)
        at = choose(is_end, 2 * pair + choose(right, 1, 0), self.ends + turn)
        return at, choose(is_end, pair, self.quarter + turn)

    def sent_block(self, at, meta):
        return 2 * self.place_of(at, meta[0] // 2) + 1 - meta[0] % 2

    def kept_block(self, at, meta):
        return 2 * self.place_of(at, meta[0] // 2) + meta[0] % 2


def inside(col, start, width):
    return (col >= start * BIN) & (col < start * BIN + width)


def columns(block, share, width=None, lead=0):
    return lax.broadcasted_iota(jnp.int32, (1, width or share), 1) + (block * share - lead)


def reciprocal(value):
    rough = pl.reciprocal(value, approx=True)
    rough = rough * (2.0 - value * rough)
    return rough * (2.0 - value * rough)


def weights_kernel(block_of, plan, units, width, meta_ref, start_ref, *refs):
    binned = len(refs) > 5 + units
    frame_ref, refs = (refs[0], refs[1:]) if binned else (None, refs)
    spread_ref, mask_ref, *refs = refs
    weights, scratch = (refs[:-10], refs[-10:]) if binned else (refs[:-2], refs[-2:])
    *scratch, scatter, weight = scratch
    if binned:
        bins_ref, total, gather, *splits = scratch
        image_parts, weight_parts = splits[:3], splits[3:]
    step = pl.program_id(0)
    block = block_of(step, meta_ref)
    start = start_ref[meta_ref[0]]
    rows, share = spread_ref.shape
    bins_row, bins_col = mask_ref.shape
    per = share // BIN

    @pl.when(step == 0)
    def _():
        cell = lax.broadcasted_iota(jnp.int32, (SIDE, share), 1) >> 4
        scatter[...] = (cell == lax.broadcasted_iota(jnp.int32, (SIDE, share), 0)).astype(BF16)

    blocks_here = pltpu.roll(mask_ref[...].astype(F32), lax.rem(bins_col - block * per, bins_col), 1)[:, :SIDE]
    kept = mm(blocks_here.astype(BF16), scatter[...])
    kept = jnp.where(inside(columns(block, share), start, width), kept, 0.0)
    for top in range(0, rows, CHUNK):
        here = slice(top, top + CHUNK)
        inverse = reciprocal(spread_ref[here])
        bins_here = slice(top // BIN, (top + CHUNK) // BIN)
        factor = jnp.broadcast_to(kept[bins_here][:, None, :], (CHUNK // BIN, BIN, share)).reshape(CHUNK, share)
        weight[here] = inverse * factor
        if binned:
            for value, splits in ((frame_ref[here], image_parts), (inverse, weight_parts)):
                value = value.reshape(CHUNK // BIN, 2, 8, share).sum(axis=1).reshape(CHUNK // 2, share)
                for split in splits:
                    rounded = value.astype(BF16)
                    split[top // 2 : (top + CHUNK) // 2] = rounded
                    value = value - rounded.astype(F32)
    for at, part in enumerate(plan):
        if part is None:
            continue

        @pl.when(step == at)
        def _(out=part[0], fresh=part[1]):
            if out >= units:
                weights[-1][0] = weight[...]
            elif fresh:
                weights[out][...] = weight[...]
            else:
                weights[out][...] += weight[...]

    if not binned:
        return

    @pl.when(step == 0)
    def _():
        cell = lax.broadcasted_iota(jnp.int32, (share, SIDE), 0) >> 4
        gather[...] = (cell == lax.broadcasted_iota(jnp.int32, (share, SIDE), 1)).astype(BF16)
        total[...] = jnp.zeros_like(total)

    def gathered(splits):
        result = None
        for split in splits:
            product = mm(split[...], gather[...])
            result = product if result is None else result + product
        if bins_col > SIDE:
            result = jnp.concatenate([result, jnp.zeros((result.shape[0], bins_col - SIDE), F32)], axis=1)
        return pltpu.roll(result, block * per, 1)

    half = bins_row * 8
    total[:half] += gathered(image_parts)
    total[half:] += gathered(weight_parts)

    @pl.when(step == len(plan) - 1)
    def _():
        bins = total[...].reshape(2 * bins_row, 8, bins_col).sum(axis=1)
        cell = lax.broadcasted_iota(jnp.int32, (1, bins_col), 1) * BIN
        keep = jnp.where(inside(cell, start, width), mask_ref[...].astype(F32), 0.0)
        bins_ref[0, 0] = bins[:bins_row] / (BIN * BIN)
        bins_ref[0, 1] = bins[bins_row:] * keep


ANY = pl.BlockSpec(memory_space=pl.ANY)


def whole(shape):
    return pl.BlockSpec(shape, lambda *_: (0,) * len(shape))


def pixel_weights(block_of, plan, units, meta, starts, frame, spread, mask, share, width, after=()):
    rows = spread.shape[0]
    bins_row, bins_col = mask.shape
    kept = sum(part is not None and part[0] >= units for part in plan)
    lead = len(plan) - kept
    tile = pl.BlockSpec((rows, share), lambda i, meta, starts: (0, block_of(i, meta)))
    out_specs = [whole((rows, share))] * units
    out_shape = [pltpu.HBM((rows, share), F32)] * units
    scratch = [pltpu.VMEM((SIDE, share), BF16), pltpu.VMEM((rows, share), F32)]
    images = []
    if frame is not None:
        images = [frame]
        bins = (1, 2, bins_row, bins_col)
        out_specs += [
            pl.BlockSpec((1, rows, share), lambda i, meta, starts: (jnp.maximum(i - lead, 0), 0, 0)), whole(bins)
        ]
        out_shape += [pltpu.HBM((kept, rows, share), F32), jax.ShapeDtypeStruct(bins, F32)]
        splits = [pltpu.VMEM((rows // 2, share), BF16)] * 5
        scratch = [pltpu.VMEM((rows, bins_col), F32), pltpu.VMEM((share, SIDE), BF16), *splits, *scratch]
    given = 2 + len(images) + 2
    kernel = functools.partial(weights_kernel, block_of, plan, units, width)
    return pl.pallas_call(
        lambda *refs: kernel(*refs[:given], *refs[given + len(after) :]),
        grid_spec=pltpu.PrefetchScalarGridSpec(
            num_scalar_prefetch=2,
            grid=(len(plan),),
            in_specs=[tile] * len(images) + [tile, whole(mask.shape)] + [ANY] * len(after),
            out_specs=out_specs,
            scratch_shapes=scratch,
        ),
        out_shape=out_shape,
        compiler_params=pltpu.CompilerParams(vmem_limit_bytes=VMEM),
        cost_estimate=SMALL,
        name="pixel_weights",
    )(meta, starts, *images, spread, mask, *after)


def smooth_kernel(block_of, plan, width, stacked, meta_ref, start_ref, *refs):
    step = pl.program_id(0)
    images, bands, scratch = refs[:9], refs[9:13], refs[-8:]
    refs = refs[13:-8]
    *refs, token_ref = refs
    token_ref[...] = jnp.zeros_like(token_ref)
    weights, outs = refs[: len(refs) // 2], refs[len(refs) // 2 :]

    @pl.when(step == 0)
    def _():
        for k, matrix in enumerate(bands):
            scratch[2 * k][...], scratch[2 * k + 1][...] = split_high_low(matrix[...])

    col_hi, col_lo, row_hi, row_lo, up_hi, up_lo, down_hi, down_lo = scratch
    block = block_of(step, meta_ref)
    start = start_ref[meta_ref[0]]
    rows, share = images[4].shape
    window = share + 2 * SIDE
    field = jnp.concatenate(
        [jnp.concatenate([images[3 * i + j][...] for j in range(3)], axis=1) for i in range(3)], axis=0
    )
    field = jnp.where(inside(columns(block, share, window, SIDE), start, width), field, 0.0)
    high, low = split_high_low(field)

    def three(a_hi, a_lo, b_hi, b_lo):
        return mm(a_hi, b_hi) + (mm(a_lo, b_hi) + mm(a_hi, b_lo))

    tiles = []
    for tile in range(share // TILE):
        lanes = slice(tile * TILE, (tile + 1) * TILE + 2 * SIDE)
        tiles.append(three(high[:, lanes], low[:, lanes], col_hi[...], col_lo[...]))
    across = tiles[0] if len(tiles) == 1 else jnp.concatenate(tiles, axis=1)
    high, low = split_high_low(across)
    height = row_hi.shape[0]
    tiles = []
    for tile in range(rows // height):
        top = tile * height
        mid = slice(top + HALO, top + HALO + height)
        upper = slice(top, top + HALO)
        lower = slice(top + HALO + height, top + 2 * HALO + height)
        main = three(row_hi[...], row_lo[...], high[mid], low[mid])
        tiles += [
            main[:HALO] + three(up_hi[...], up_lo[...], high[upper], low[upper]),
            main[HALO : height - HALO],
            main[height - HALO :] + three(down_hi[...], down_lo[...], high[lower], low[lower]),
        ]
    smoothed = jnp.concatenate(tiles, axis=0)
    smoothed = jnp.where(inside(columns(block, share), start, width), smoothed, 0.0)
    if stacked:
        outs[0][0] = weights[0][0] * smoothed
        return
    for at, (out, fresh) in enumerate(plan):
        @pl.when(step == at)
        def _(out=out, fresh=fresh):
            term = weights[out][...] * smoothed
            outs[out][...] = term if fresh else outs[out][...] + term


def smoothed_terms(block_of, plan, weights, meta, starts, frame, above, below, share, width, after=()):
    rows, cols = frame.shape
    stacked = weights[0].ndim == 3
    count = len(weights)
    per = share // SIDE
    last = cols // SIDE - 1
    specs = []
    for height in (HALO, rows, HALO):
        specs += [
            pl.BlockSpec((height, SIDE), lambda i, m, s: (0, jnp.maximum(block_of(i, m) * per - 1, 0))),
            pl.BlockSpec((height, share), lambda i, m, s: (0, block_of(i, m))),
            pl.BlockSpec((height, SIDE), lambda i, m, s: (0, jnp.minimum(block_of(i, m) * per + per, last))),
        ]
    if stacked:
        parts_spec = pl.BlockSpec((1, rows, share), lambda i, m, s: (i, 0, 0))
    else:
        parts_spec = whole((rows, share))
    height = min(TILE, rows)
    full = band(height, height + 2 * HALO, HALO)
    bands = [
        band(TILE, TILE + 2 * SIDE, SIDE).T,
        full[:, HALO : HALO + height],
        full[:HALO, :HALO],
        full[height - HALO :, HALO + height :],
    ]
    parts = [jnp.asarray(matrix.astype(np.float32)) for matrix in bands]

    def body(*refs):
        lead = 2 + 9 + len(parts) + count
        smooth_kernel(block_of, plan, width, stacked, *refs[:lead], *refs[lead + len(after) :])

    return pl.pallas_call(
        body,
        grid_spec=pltpu.PrefetchScalarGridSpec(
            num_scalar_prefetch=2,
            grid=(len(plan),),
            in_specs=specs + [whole(p.shape) for p in parts] + [parts_spec] * count + [ANY] * len(after),
            out_specs=[parts_spec] * count + [whole(TOKEN)],
            scratch_shapes=[pltpu.VMEM(p.shape, BF16) for p in parts for _ in range(2)],
        ),
        out_shape=[pltpu.HBM(w.shape, F32) for w in weights] + [jax.ShapeDtypeStruct(TOKEN, F32)],
        compiler_params=pltpu.CompilerParams(vmem_limit_bytes=VMEM),
        cost_estimate=SMALL,
        name="smoothed_terms",
    )(meta, starts, *([above] * 3 + [frame] * 3 + [below] * 3), *parts, *weights, *after)


def term_kernel(layout, width, wanted, units, received, numerator, meta_ref, start_ref, *refs):
    place = meta_ref[0] // 2
    block = 2 * wanted(place) + meta_ref[0] % 2
    _, unit = layout.position_of(wanted(place), place)
    mate_start = start_ref[meta_ref[0] + 1 - 2 * (meta_ref[0] % 2)]
    in_mate = inside(columns(block, layout.share), mate_start, width)
    *refs, out_ref, token_ref = refs
    token_ref[...] = jnp.zeros_like(token_ref)

    def pair():
        own = refs.pop(0)[0]
        got = refs.pop(0)[...]
        for u in units[1:]:
            got = jnp.where(unit == u, refs.pop(0)[...], got)
        return own, got

    def added(own, got, names):
        value = own + jnp.where(in_mate, got, 0.0)
        for _ in range(names):
            value = value + refs.pop(0)[...]
        return value

    if not numerator:
        out_ref[...] = added(*pair(), received)
        return
    own_den, mate_den = pair()
    own, mate = pair()
    rows_part, back = refs.pop(0)[...], refs.pop(0)[...]
    own_back = sum(rows_part[:, u : u + 1] * back[u : u + 1, :] for u in range(3))
    mate_back = sum(rows_part[:, u : u + 1] * back[3 + u : 4 + u, :] for u in range(3))
    top = added(own - own_den * own_back, mate - mate_den * mate_back, received)
    if numerator == "quotient":
        out_ref[...] = top / (PRIOR + added(own_den, mate_den, received))
    else:
        out_ref[...] = top


def block_term(layout, width, wanted, senders, meta, starts, parts, received, numerator=None, tables=(), after=()):
    kept = parts[0][0]
    rows, share = kept.shape[1:]
    chunk = min(TILE, rows)

    def at_unit(place):
        return layout.position_of(wanted(place), place)

    units = sorted({int(at_unit(z)[1]) for z in senders})
    flat = pl.BlockSpec((chunk, share), lambda r, m, s: (r, 0))
    specs, args = [], []
    for own, got in parts:
        specs.append(pl.BlockSpec((1, chunk, share), lambda r, m, s: (at_unit(m[0] // 2)[0], r, 0)))
        args.append(pltpu.with_memory_space_constraint(own, pltpu.HBM))
        for u in units:
            specs.append(
                flat
                if len(units) == 1
                else pl.BlockSpec(
                    (chunk, share), lambda r, m, s, u=u: (jnp.where(at_unit(m[0] // 2)[1] == u, r, 0), 0)
                )
            )
            args.append(got[u])
    if numerator:
        rows_part, back = tables
        strips = rows // chunk
        specs.append(pl.BlockSpec((chunk, rows_part.shape[1]), lambda r, m, s: (m[1] * strips + r, 0)))
        specs.append(
            pl.BlockSpec((back.shape[0], share), lambda r, m, s: (0, 2 * wanted(m[0] // 2) + m[0] % 2))
        )
        args += [rows_part, back]
    for sums in received:
        specs += [flat] * len(sums)
        args += list(sums)
    lead = 2 + len(args)
    body = functools.partial(term_kernel, layout, width, wanted, units, len(received[0]), numerator)
    return pl.pallas_call(
        lambda *refs: body(*refs[:lead], *refs[-2:]),
        grid_spec=pltpu.PrefetchScalarGridSpec(
            num_scalar_prefetch=2, grid=(rows // chunk,), in_specs=specs + [ANY] * len(after), out_specs=[flat, whole(TOKEN)]
        ),
        out_shape=[jax.ShapeDtypeStruct((rows, share), F32), jax.ShapeDtypeStruct(TOKEN, F32)],
        compiler_params=pltpu.CompilerParams(vmem_limit_bytes=SOME),
        cost_estimate=SMALL,
        name="block_term",
    )(meta, starts, *args, *after)


def held_until(values, after):
    def body(*refs):
        del refs

    return pl.pallas_call(
        body,
        in_specs=[ANY] * (len(values) + len(after)),
        out_specs=[ANY] * len(values),
        out_shape=[jax.ShapeDtypeStruct(v.shape, v.dtype) for v in values],
        input_output_aliases={i: i for i in range(len(values))},
        compiler_params=pltpu.CompilerParams(vmem_limit_bytes=VMEM),
        cost_estimate=SMALL,
        name="held",
    )(*values, *after)


def arrived(values):
    def body(*refs):
        refs[-1][...] = jnp.zeros_like(refs[-1])

    return pl.pallas_call(
        body,
        in_specs=[ANY] * len(values),
        out_shape=jax.ShapeDtypeStruct(TOKEN, F32),
        compiler_params=pltpu.CompilerParams(vmem_limit_bytes=SOME),
        cost_estimate=pl.CostEstimate(flops=1000, bytes_accessed=8 * 10**6, transcendentals=0),
        name="arrived",
    )(*values)


def contract_last(left, right):
    return lax.dot_general(left, right, (((1,), (1,)), ((), ())), precision=HIGH, preferred_element_type=F32)


def contract_last_three(left, right):
    def one(a, b):
        return lax.dot_general(a, b, (((1,), (1,)), ((), ())), preferred_element_type=F32)

    (l_hi, l_lo), (r_hi, r_lo) = split_high_low(left), split_high_low(right)
    return one(l_hi, r_hi) + (one(l_lo, r_hi) + one(l_hi, r_lo))


def moments_kernel(places, strips, meta_ref, bins_ref, out_ref):
    count, _, rows, cols = bins_ref.shape
    at = [places.index(e) for e in range(count)]
    image = [bins_ref[at[e], 0] for e in range(count)]
    weight = [bins_ref[at[e], 1] for e in range(count)]
    x = centers(lax.broadcasted_iota(jnp.int32, (1, cols), 1), cols)
    tx = [jnp.ones_like(x), x]
    while len(tx) < 5:
        tx.append(2.0 * x * tx[-1] - tx[-2])
    tx = jnp.concatenate(tx + [jnp.zeros((3, cols), F32)], axis=0)
    joint, diffs = [], []
    for apart in range(1, count // 2 + 1):
        group, group_d = [], []
        for i in range(count):
            j = (i + apart) % count
            w = weight[i] * weight[j] / (weight[i] + weight[j] + 1.0)
            group.append(w)
            group_d.append(w * (image[i] - image[j]))
        joint.append(contract_last_three(tx, jnp.concatenate(group, axis=0)))
        diffs.append(contract_last_three(tx, jnp.concatenate(group_d, axis=0)))
    along = jnp.concatenate([jnp.concatenate(joint, axis=1), jnp.concatenate(diffs, axis=1)], axis=0)
    total = along.shape[1]
    row = lax.broadcasted_iota(jnp.int32, (total, SIDE), 0)
    lane = lax.broadcasted_iota(jnp.int32, (total, SIDE), 1)
    mine = row // rows == lane
    y = centers(row % rows + meta_ref[1] * rows, rows * strips)
    a_hi, a_lo = split_high_low(along)
    ty = [jnp.ones_like(y), y]
    for a in range(5):
        if a > 1:
            ty.append(2.0 * y * ty[-1] - ty[-2])
        b_hi, b_lo = split_high_low(jnp.where(mine, ty[a], 0.0))
        out_ref[:, a * SIDE : (a + 1) * SIDE] = mm(a_hi, b_hi) + (mm(a_lo, b_hi) + mm(a_hi, b_lo))


def solve_kernel(width, meta_ref, start_ref, moments_ref, owner_ref, out_ref, back_ref):
    owner = owner_ref[...].astype(F32)
    count = owner.shape[0]
    lanes = count * count // 2
    exposure = lax.broadcasted_iota(jnp.int32, (count, lanes), 0)
    lane = lax.broadcasted_iota(jnp.int32, (count, lanes), 1)
    mine = lane % count
    apart = lane // count + 1
    is_i = (exposure == mine).astype(F32)
    is_j = (exposure == (mine + apart) % count).astype(F32)
    both = owner + owner.T
    listed = jnp.sum(is_i * jnp.dot(both, is_j, precision=HIGH, preferred_element_type=F32), axis=0, keepdims=True)
    lane_row = lax.broadcasted_iota(jnp.int32, (1, lanes), 1)
    once = (lane_row // count + 1 < count // 2) | (lane_row % count < count // 2)
    listed = jnp.where(once, listed, 0.0)
    held = listed > 0.0
    moment = [[moments_ref[b : b + 1, a * SIDE : a * SIDE + lanes] for b in range(5)] for a in range(5)]

    def entry(k, l):
        (u, v), (s, t) = divmod(k, 3), divmod(l, 3)
        total = 0.0
        for a in (u + s, abs(u - s)):
            for b in (v + t, abs(v - t)):
                total = total + moment[a][b]
        return jnp.where(held, 0.25 * total, 1.0 if k == l else 0.0)

    factor = [[None] * 9 for _ in range(9)]
    scale = [None] * 9
    for k in range(9):
        for l in range(k, 9):
            value = entry(l, k)
            for m in range(k):
                value = value - factor[l][m] * factor[k][m]
            if l == k:
                scale[k] = 1.0 / jnp.sqrt(value)
            else:
                factor[l][k] = value * scale[k]
    half = [None] * 9
    for k in range(9):
        a, b = divmod(k, 3)
        value = moments_ref[8 + b : 9 + b, a * SIDE : a * SIDE + lanes]
        for m in range(k):
            value = value - factor[k][m] * half[m]
        half[k] = value * scale[k]
    fit = [None] * 9
    for k in reversed(range(9)):
        value = half[k]
        for m in range(k + 1, 9):
            value = value - factor[m][k] * fit[m]
        fit[k] = value * scale[k]
    fits = jnp.concatenate([jnp.where(held, f, 0.0) for f in fit] + [jnp.zeros((7, lanes), F32)], axis=0)
    right = contract_last((is_i - is_j) * listed, fits)
    row = lax.broadcasted_iota(jnp.int32, (count, count), 0)
    column = lax.broadcasted_iota(jnp.int32, (count, count), 1)
    degree = jnp.sum(both, axis=1, keepdims=True) + LAMBDA_REG
    system = jnp.where(row == column, degree, 0.0) - both
    for k in range(count):
        inverse = 1.0 / system[k : k + 1, k : k + 1]
        pivot_s, pivot_r = system[k : k + 1, :] * inverse, right[k : k + 1, :] * inverse
        lead = system[:, k : k + 1]
        chosen = row[:, :1] == k
        system = jnp.where(chosen, pivot_s, system - lead * pivot_s)
        right = jnp.where(chosen, pivot_r, right - lead * pivot_r)
    out_ref[...] = right[:, :9]
    member = meta_ref[0]
    mate = member + 1 - 2 * (member % 2)
    cols = back_ref.shape[1]
    padded = cols + 2 * SIDE
    col = lax.broadcasted_iota(jnp.int32, (1, padded), 1) - SIDE
    x = centers(col, cols)
    terms = [jnp.ones_like(x), x, 2.0 * x * x - 1.0]
    fields = [jnp.where(inside(col, start_ref[e], width), t, 0.0) for e in (member, mate) for t in terms]
    fields = jnp.concatenate(fields + [jnp.zeros((2, padded), F32)], axis=0)
    taps = tap_values()
    total = float(taps[RADIUS]) * fields
    for shift in range(1, RADIUS + 1):
        both = pltpu.roll(fields, shift, 1) + pltpu.roll(fields, padded - shift, 1)
        total = total + float(taps[RADIUS + shift]) * both
    total = total[:, SIDE : SIDE + cols]
    rows = lax.broadcasted_iota(jnp.int32, (count, 16), 0)
    for k, which in enumerate((member, mate)):
        mine = jnp.sum(jnp.where(rows == which, right, 0.0), axis=0, keepdims=True)
        for u in range(3):
            back_ref[3 * k + u : 3 * k + u + 1, :] = sum(
                mine[:, 3 * u + v : 3 * u + v + 1] * total[3 * k + v : 3 * k + v + 1, :] for v in range(3)
            )
    back_ref[6:8, :] = jnp.zeros((2, cols), F32)


def filtered_rows(total_rows):
    y = (2.0 * np.arange(total_rows) + 1.0) / total_rows - 1.0
    terms = np.stack([np.ones_like(y), y, 2.0 * y * y - 1.0])
    padded = np.pad(terms, ((0, 0), (RADIUS, RADIUS)))
    taps = tap_values()
    return sum(taps[t] * padded[:, t : t + total_rows] for t in range(2 * RADIUS + 1)).T.astype(np.float32)


def per_device(image, variance, mask, foot_start, pair_owner):
    frame, spread, blocks = image[0], variance[0], mask[0]
    rows, cols = frame.shape
    exposures, sky_count = lax.axis_size("exp"), lax.axis_size("sky")
    member = lax.axis_index("exp")
    meta = jnp.stack([member, lax.axis_index("sky")])
    width = 3 * cols // 4
    layout = Places(exposures, cols)
    share, places, quarter = layout.share, layout.places, layout.quarter
    ends, middle_count = layout.ends, layout.middle
    units = quarter + middle_count
    folded = [(i // 2, i % 2 == 0) for i in range(ends)]
    sent = folded + [(quarter + i, True) for i in range(middle_count)]
    rest = [None] * ends + [(i, True) for i in range(middle_count + places)]

    def sent_then_kept(i, meta):
        return jnp.where(i < places, layout.sent_block(i, meta), layout.kept_block(i - places, meta))

    swap = [(i, i ^ 1) for i in range(exposures)]

    def swapped(parts):
        return [lax.ppermute(part, "exp", swap) for part in parts]

    den_ends = pixel_weights(
        layout.sent_block, folded, quarter, meta, foot_start, None, spread, blocks, share, width
    )
    *den_middle, den_kept, gathered = pixel_weights(
        sent_then_kept, rest, middle_count, meta, foot_start, frame, spread, blocks, share, width, after=den_ends
    )
    got_ends = swapped(den_ends)
    got_middle = swapped(den_middle)
    den_got = got_ends + got_middle

    up = [(i, i + 1) for i in range(sky_count - 1)]
    down = [(j, i) for i, j in up]
    above = lax.ppermute(frame[rows - HALO :], "sky", up)
    below = lax.ppermute(frame[:HALO], "sky", down)
    smooth = functools.partial(
        smoothed_terms, meta=meta, starts=foot_start, frame=frame, above=above, below=below, share=share, width=width
    )

    held = [0]
    bits = [1 << k for k in range(exposures.bit_length() - 1)]

    def gather_along(gathered, bit):
        other = lax.ppermute(gathered, "exp", [(i, i ^ bit) for i in range(exposures)])
        low = (member & bit) == 0
        held.extend([e | bit for e in held])
        return jnp.concatenate([jnp.where(low, gathered, other), jnp.where(low, other, gathered)])

    gathered = gather_along(gathered, bits[1])
    (gathered,) = held_until([gathered], [above, below])
    for bit in bits[2:]:
        gathered = gather_along(gathered, bit)

    def to_right(step):
        return lambda z: choose(z < step, z + places - step, places - 1)

    def to_left(step):
        return lambda z: choose(z >= places - step, z - places + step, 0)

    def outward(step):
        return lambda z: choose(z < places // 2, to_right(step)(z), to_left(step)(z))

    def shift(value, rights, lefts):
        pairs = [(2 * z + s, 2 * z + 2 + s) for z in rights for s in range(2)]
        pairs += [(2 * z + s, 2 * z - 2 + s) for z in lefts for s in range(2)]
        return lax.ppermute(value, "exp", pairs)

    def along_places(step, term, sums, after, after_left=()):
        rights, lefts = range(step), range(places - step, places)
        if step <= places // 2:
            value, token = term(outward(step), [*rights, *lefts], sums, after)
            if step < places // 2:
                return (shift(value, rights, lefts),), (token,)
            return (shift(value, rights, []), shift(value, [], lefts)), (token,)
        right, token = term(to_right(step), rights, sums[:1], (*after, sums[1]))
        left, token_left = term(to_left(step), lefts, sums[1:], after_left or after)
        return (shift(right, rights, []), shift(left, [], lefts)), (token, token_left)

    def den_term(wanted, senders, sums, after):
        parts = [(den_kept, den_got)]
        return block_term(layout, width, wanted, senders, meta, foot_start, parts, [sums], after=after)

    den_sums, den_values = along_places(1, den_term, (), ())
    *num_sent, token = smooth(layout.sent_block, sent, [*den_ends, *den_middle], after=den_values)
    num_got = swapped(num_sent)
    (gathered,) = held_until([gathered], [token])
    gathered = gather_along(gathered, bits[0])
    num_kept, token = smooth(layout.kept_block, [(i, True) for i in range(places)], [den_kept], after=[token])
    den_sums, den_values = along_places(2, den_term, den_sums, [token])

    (gathered,) = held_until([gathered], den_values)
    scalars = pl.BlockSpec(memory_space=pltpu.SMEM)
    vmem = pl.BlockSpec(memory_space=pltpu.VMEM)
    moments = pl.pallas_call(
        functools.partial(moments_kernel, held, sky_count),
        in_specs=[scalars, vmem],
        out_shape=jax.ShapeDtypeStruct((16, 5 * SIDE), F32),
        compiler_params=pltpu.CompilerParams(vmem_limit_bytes=SOME),
        cost_estimate=SMALL,
        name="pair_moments",
    )(meta, gathered)
    bit = 1
    while bit < sky_count:
        moments = moments + lax.ppermute(moments, "sky", [(i, i ^ bit) for i in range(sky_count)])
        bit *= 2
    offsets, back = pl.pallas_call(
        functools.partial(solve_kernel, width),
        in_specs=[scalars, scalars, vmem, vmem],
        out_shape=[jax.ShapeDtypeStruct((exposures, 9), F32), jax.ShapeDtypeStruct((8, cols), F32)],
        compiler_params=pltpu.CompilerParams(vmem_limit_bytes=SOME),
        cost_estimate=SMALL,
        name="offsets",
    )(meta, foot_start, moments, pair_owner)

    tables = (jnp.asarray(filtered_rows(rows * sky_count)), back)
    parts = [(den_kept, den_got), (num_kept, num_got)]

    def num_term(wanted, senders, sums, after):
        return block_term(
            layout, width, wanted, senders, meta, foot_start, parts, [sums], "terms", tables, after
        )

    num_sums, num_values = along_places(1, num_term, (), den_values)
    for step in range(3, places):
        den_sums, den_values = along_places(step, den_term, den_sums, num_values)
        num_sums, num_values = along_places(step - 1, num_term, num_sums, den_values)
    num_sums, num_values = along_places(places - 1, num_term, num_sums, num_values, [arrived(den_sums)])
    coadd, _ = block_term(
        layout,
        width,
        lambda z: z,
        range(places),
        meta,
        foot_start,
        parts,
        [num_sums, den_sums],
        "quotient",
        tables,
    )
    return (coadd, offsets)


def solution(mesh):
    placed = (P("exp", "sky", None), P("exp", "sky", None), P("exp", "sky", None), P(), P())
    return jax.shard_map(
        per_device, mesh=mesh, in_specs=placed, out_specs=(P("sky", "exp"), P()), check_vma=False
    )
```

```python
import functools

import jax
import jax.numpy as jnp
import numpy as np
from jax import lax
from jax.experimental import pallas as pl
from jax.experimental.pallas import tpu as pltpu
from jax.sharding import PartitionSpec as P

BIN = 16
RADIUS = 10
HALO = 16
SIDE = 128
TOKEN = (8, 128)
TILE = 256
CHUNK = 64

HIGH = lax.Precision.HIGHEST
LAMBDA_REG = 0.25
PRIOR = 1.0
VMEM = 127 * 512 * 1024
SOME = 24 * 1024 * 1024
BF16 = jnp.bfloat16
F32 = jnp.float32
SMALL = pl.CostEstimate(flops=1000, bytes_accessed=1000, transcendentals=0)


def tap_values():
    offs = np.arange(-RADIUS, RADIUS + 1).astype(np.float64)
    taps = np.exp(-offs * offs / 50.0)
    return taps / taps.sum()


def band(out, width, lead):
    taps = tap_values()
    full = np.zeros((out, width), np.float64)
    for shift in range(-RADIUS, RADIUS + 1):
        rows = np.arange(out)
        full[rows, rows + lead + shift] = taps[shift + RADIUS]
    return full


def centers(index, total):
    return (2.0 * index.astype(F32) + 1.0) / total - 1.0


def split_high_low(value):
    high = value.astype(BF16)
    return high, (value - high.astype(F32)).astype(BF16)


def mm(left, right):
    return jnp.dot(left, right, preferred_element_type=F32)


def choose(condition, left, right):
    if isinstance(condition, (bool, np.bool_)):
        return left if condition else right
    return jnp.where(condition, left, right)


class Places:
    def __init__(self, exposures, cols):
        self.share = cols // exposures
        self.places = exposures // 2
        self.quarter = self.places // 4
        self.ends = 2 * self.quarter
        self.middle = self.places - self.ends

    def place_of(self, at, place):
        down = place < self.places // 2
        pair = at // 2
        end = choose(down, self.quarter - 1 - pair, pair) + (at % 2) * (self.places - self.quarter)
        turn = at - self.ends
        mid = choose(down, self.places - self.quarter - 1 - turn, self.quarter + turn)
        return choose(at < self.ends, end, mid)

    def position_of(self, wanted, place):
        down = place < self.places // 2
        right = wanted >= self.places - self.quarter
        low = choose(right, wanted - (self.places - self.quarter), wanted)
        pair = choose(down, self.quarter - 1 - low, low)
        turn = choose(down, self.places - self.quarter - 1 - wanted, wanted - self.quarter)
        is_end = right | (wanted < self.quarter)
        at = choose(is_end, 2 * pair + choose(right, 1, 0), self.ends + turn)
        return at, choose(is_end, pair, self.quarter + turn)

    def sent_block(self, at, meta):
        return 2 * self.place_of(at, meta[0] // 2) + 1 - meta[0] % 2

    def kept_block(self, at, meta):
        return 2 * self.place_of(at, meta[0] // 2) + meta[0] % 2


def inside(col, start, width):
    return (col >= start * BIN) & (col < start * BIN + width)


def columns(block, share, width=None, lead=0):
    return lax.broadcasted_iota(jnp.int32, (1, width or share), 1) + (block * share - lead)


def reciprocal(value):
    rough = pl.reciprocal(value, approx=True)
    rough = rough * (2.0 - value * rough)
    return rough * (2.0 - value * rough)


def weights_kernel(block_of, plan, units, width, meta_ref, start_ref, *refs):
    binned = len(refs) > 5 + units
    frame_ref, refs = (refs[0], refs[1:]) if binned else (None, refs)
    spread_ref, mask_ref, *refs = refs
    weights, scratch = (refs[:-10], refs[-10:]) if binned else (refs[:-2], refs[-2:])
    *scratch, scatter, weight = scratch
    if binned:
        bins_ref, total, gather, *splits = scratch
        image_parts, weight_parts = splits[:3], splits[3:]
    step = pl.program_id(0)
    block = block_of(step, meta_ref)
    start = start_ref[meta_ref[0]]
    rows, share = spread_ref.shape
    bins_row, bins_col = mask_ref.shape
    per = share // BIN

    @pl.when(step == 0)
    def _():
        cell = lax.broadcasted_iota(jnp.int32, (SIDE, share), 1) >> 4
        scatter[...] = (cell == lax.broadcasted_iota(jnp.int32, (SIDE, share), 0)).astype(BF16)

    blocks_here = pltpu.roll(mask_ref[...].astype(F32), lax.rem(bins_col - block * per, bins_col), 1)[:, :SIDE]
    kept = mm(blocks_here.astype(BF16), scatter[...])
    kept = jnp.where(inside(columns(block, share), start, width), kept, 0.0)
    for top in range(0, rows, CHUNK):
        here = slice(top, top + CHUNK)
        inverse = reciprocal(spread_ref[here])
        bins_here = slice(top // BIN, (top + CHUNK) // BIN)
        factor = jnp.broadcast_to(kept[bins_here][:, None, :], (CHUNK // BIN, BIN, share)).reshape(CHUNK, share)
        weight[here] = inverse * factor
        if binned:
            for value, splits in ((frame_ref[here], image_parts), (inverse, weight_parts)):
                value = value.reshape(CHUNK // BIN, 2, 8, share).sum(axis=1).reshape(CHUNK // 2, share)
                for split in splits:
                    rounded = value.astype(BF16)
                    split[top // 2 : (top + CHUNK) // 2] = rounded
                    value = value - rounded.astype(F32)
    for at, part in enumerate(plan):
        if part is None:
            continue

        @pl.when(step == at)
        def _(out=part[0], fresh=part[1]):
            if out >= units:
                weights[-1][0] = weight[...]
            elif fresh:
                weights[out][...] = weight[...]
            else:
                weights[out][...] += weight[...]

    if not binned:
        return

    @pl.when(step == 0)
    def _():
        cell = lax.broadcasted_iota(jnp.int32, (share, SIDE), 0) >> 4
        gather[...] = (cell == lax.broadcasted_iota(jnp.int32, (share, SIDE), 1)).astype(BF16)
        total[...] = jnp.zeros_like(total)

    def gathered(splits):
        result = None
        for split in splits:
            product = mm(split[...], gather[...])
            result = product if result is None else result + product
        if bins_col > SIDE:
            result = jnp.concatenate([result, jnp.zeros((result.shape[0], bins_col - SIDE), F32)], axis=1)
        return pltpu.roll(result, block * per, 1)

    half = bins_row * 8
    total[:half] += gathered(image_parts)
    total[half:] += gathered(weight_parts)

    @pl.when(step == len(plan) - 1)
    def _():
        bins = total[...].reshape(2 * bins_row, 8, bins_col).sum(axis=1)
        cell = lax.broadcasted_iota(jnp.int32, (1, bins_col), 1) * BIN
        keep = jnp.where(inside(cell, start, width), mask_ref[...].astype(F32), 0.0)
        bins_ref[0, 0] = bins[:bins_row] / (BIN * BIN)
        bins_ref[0, 1] = bins[bins_row:] * keep


ANY = pl.BlockSpec(memory_space=pl.ANY)


def whole(shape):
    return pl.BlockSpec(shape, lambda *_: (0,) * len(shape))


def pixel_weights(block_of, plan, units, meta, starts, frame, spread, mask, share, width, after=()):
    rows = spread.shape[0]
    bins_row, bins_col = mask.shape
    kept = sum(part is not None and part[0] >= units for part in plan)
    lead = len(plan) - kept
    tile = pl.BlockSpec((rows, share), lambda i, meta, starts: (0, block_of(i, meta)))
    out_specs = [whole((rows, share))] * units
    out_shape = [pltpu.HBM((rows, share), F32)] * units
    scratch = [pltpu.VMEM((SIDE, share), BF16), pltpu.VMEM((rows, share), F32)]
    images = []
    if frame is not None:
        images = [frame]
        bins = (1, 2, bins_row, bins_col)
        out_specs += [
            pl.BlockSpec((1, rows, share), lambda i, meta, starts: (jnp.maximum(i - lead, 0), 0, 0)), whole(bins)
        ]
        out_shape += [pltpu.HBM((kept, rows, share), F32), jax.ShapeDtypeStruct(bins, F32)]
        splits = [pltpu.VMEM((rows // 2, share), BF16)] * 5
        scratch = [pltpu.VMEM((rows, bins_col), F32), pltpu.VMEM((share, SIDE), BF16), *splits, *scratch]
    given = 2 + len(images) + 2
    kernel = functools.partial(weights_kernel, block_of, plan, units, width)
    return pl.pallas_call(
        lambda *refs: kernel(*refs[:given], *refs[given + len(after) :]),
        grid_spec=pltpu.PrefetchScalarGridSpec(
            num_scalar_prefetch=2,
            grid=(len(plan),),
            in_specs=[tile] * len(images) + [tile, whole(mask.shape)] + [ANY] * len(after),
            out_specs=out_specs,
            scratch_shapes=scratch,
        ),
        out_shape=out_shape,
        compiler_params=pltpu.CompilerParams(vmem_limit_bytes=VMEM),
        cost_estimate=SMALL,
        name="pixel_weights",
    )(meta, starts, *images, spread, mask, *after)


def smooth_kernel(block_of, plan, width, stacked, meta_ref, start_ref, *refs):
    step = pl.program_id(0)
    images, bands, scratch = refs[:9], refs[9:13], refs[-8:]
    refs = refs[13:-8]
    *refs, token_ref = refs
    token_ref[...] = jnp.zeros_like(token_ref)
    weights, outs = refs[: len(refs) // 2], refs[len(refs) // 2 :]

    @pl.when(step == 0)
    def _():
        for k, matrix in enumerate(bands):
            scratch[2 * k][...], scratch[2 * k + 1][...] = split_high_low(matrix[...])

    col_hi, col_lo, row_hi, row_lo, up_hi, up_lo, down_hi, down_lo = scratch
    block = block_of(step, meta_ref)
    start = start_ref[meta_ref[0]]
    rows, share = images[4].shape
    window = share + 2 * SIDE
    field = jnp.concatenate(
        [jnp.concatenate([images[3 * i + j][...] for j in range(3)], axis=1) for i in range(3)], axis=0
    )
    field = jnp.where(inside(columns(block, share, window, SIDE), start, width), field, 0.0)
    high, low = split_high_low(field)

    def three(a_hi, a_lo, b_hi, b_lo):
        return mm(a_hi, b_hi) + (mm(a_lo, b_hi) + mm(a_hi, b_lo))

    tiles = []
    for tile in range(share // TILE):
        lanes = slice(tile * TILE, (tile + 1) * TILE + 2 * SIDE)
        tiles.append(three(high[:, lanes], low[:, lanes], col_hi[...], col_lo[...]))
    across = tiles[0] if len(tiles) == 1 else jnp.concatenate(tiles, axis=1)
    high, low = split_high_low(across)
    height = row_hi.shape[0]
    tiles = []
    for tile in range(rows // height):
        top = tile * height
        mid = slice(top + HALO, top + HALO + height)
        upper = slice(top, top + HALO)
        lower = slice(top + HALO + height, top + 2 * HALO + height)
        main = three(row_hi[...], row_lo[...], high[mid], low[mid])
        tiles += [
            main[:HALO] + three(up_hi[...], up_lo[...], high[upper], low[upper]),
            main[HALO : height - HALO],
            main[height - HALO :] + three(down_hi[...], down_lo[...], high[lower], low[lower]),
        ]
    smoothed = jnp.concatenate(tiles, axis=0)
    smoothed = jnp.where(inside(columns(block, share), start, width), smoothed, 0.0)
    if stacked:
        outs[0][0] = weights[0][0] * smoothed
        return
    for at, (out, fresh) in enumerate(plan):
        @pl.when(step == at)
        def _(out=out, fresh=fresh):
            term = weights[out][...] * smoothed
            outs[out][...] = term if fresh else outs[out][...] + term


def smoothed_terms(block_of, plan, weights, meta, starts, frame, above, below, share, width, after=()):
    rows, cols = frame.shape
    stacked = weights[0].ndim == 3
    count = len(weights)
    per = share // SIDE
    last = cols // SIDE - 1
    specs = []
    for height in (HALO, rows, HALO):
        specs += [
            pl.BlockSpec((height, SIDE), lambda i, m, s: (0, jnp.maximum(block_of(i, m) * per - 1, 0))),
            pl.BlockSpec((height, share), lambda i, m, s: (0, block_of(i, m))),
            pl.BlockSpec((height, SIDE), lambda i, m, s: (0, jnp.minimum(block_of(i, m) * per + per, last))),
        ]
    if stacked:
        parts_spec = pl.BlockSpec((1, rows, share), lambda i, m, s: (i, 0, 0))
    else:
        parts_spec = whole((rows, share))
    height = min(TILE, rows)
    full = band(height, height + 2 * HALO, HALO)
    bands = [
        band(TILE, TILE + 2 * SIDE, SIDE).T,
        full[:, HALO : HALO + height],
        full[:HALO, :HALO],
        full[height - HALO :, HALO + height :],
    ]
    parts = [jnp.asarray(matrix.astype(np.float32)) for matrix in bands]

    def body(*refs):
        lead = 2 + 9 + len(parts) + count
        smooth_kernel(block_of, plan, width, stacked, *refs[:lead], *refs[lead + len(after) :])

    return pl.pallas_call(
        body,
        grid_spec=pltpu.PrefetchScalarGridSpec(
            num_scalar_prefetch=2,
            grid=(len(plan),),
            in_specs=specs + [whole(p.shape) for p in parts] + [parts_spec] * count + [ANY] * len(after),
            out_specs=[parts_spec] * count + [whole(TOKEN)],
            scratch_shapes=[pltpu.VMEM(p.shape, BF16) for p in parts for _ in range(2)],
        ),
        out_shape=[pltpu.HBM(w.shape, F32) for w in weights] + [jax.ShapeDtypeStruct(TOKEN, F32)],
        compiler_params=pltpu.CompilerParams(vmem_limit_bytes=VMEM),
        cost_estimate=SMALL,
        name="smoothed_terms",
    )(meta, starts, *([above] * 3 + [frame] * 3 + [below] * 3), *parts, *weights, *after)


def term_kernel(layout, width, wanted, units, received, numerator, meta_ref, start_ref, *refs):
    place = meta_ref[0] // 2
    block = 2 * wanted(place) + meta_ref[0] % 2
    _, unit = layout.position_of(wanted(place), place)
    mate_start = start_ref[meta_ref[0] + 1 - 2 * (meta_ref[0] % 2)]
    in_mate = inside(columns(block, layout.share), mate_start, width)
    *refs, out_ref, token_ref = refs
    token_ref[...] = jnp.zeros_like(token_ref)

    def pair():
        own = refs.pop(0)[0]
        got = refs.pop(0)[...]
        for u in units[1:]:
            got = jnp.where(unit == u, refs.pop(0)[...], got)
        return own, got

    def added(own, got, names):
        value = own + jnp.where(in_mate, got, 0.0)
        for _ in range(names):
            value = value + refs.pop(0)[...]
        return value

    if not numerator:
        out_ref[...] = added(*pair(), received)
        return
    own_den, mate_den = pair()
    own, mate = pair()
    rows_part, back = refs.pop(0)[...], refs.pop(0)[...]
    own_back = sum(rows_part[:, u : u + 1] * back[u : u + 1, :] for u in range(3))
    mate_back = sum(rows_part[:, u : u + 1] * back[3 + u : 4 + u, :] for u in range(3))
    top = added(own - own_den * own_back, mate - mate_den * mate_back, received)
    out_ref[...] = top


def block_term(layout, width, wanted, senders, meta, starts, parts, received, tables=(), after=()):
    kept = parts[0][0]
    rows, share = kept.shape[1:]
    chunk = min(TILE, rows)

    def at_unit(place):
        return layout.position_of(wanted(place), place)

    units = sorted({int(at_unit(z)[1]) for z in senders})
    flat = pl.BlockSpec((chunk, share), lambda r, m, s: (r, 0))
    specs, args = [], []
    for own, got in parts:
        specs.append(pl.BlockSpec((1, chunk, share), lambda r, m, s: (at_unit(m[0] // 2)[0], r, 0)))
        args.append(pltpu.with_memory_space_constraint(own, pltpu.HBM))
        for u in units:
            specs.append(
                flat
                if len(units) == 1
                else pl.BlockSpec(
                    (chunk, share), lambda r, m, s, u=u: (jnp.where(at_unit(m[0] // 2)[1] == u, r, 0), 0)
                )
            )
            args.append(got[u])
    if tables:
        rows_part, back = tables
        strips = rows // chunk
        specs.append(pl.BlockSpec((chunk, rows_part.shape[1]), lambda r, m, s: (m[1] * strips + r, 0)))
        specs.append(
            pl.BlockSpec((back.shape[0], share), lambda r, m, s: (0, 2 * wanted(m[0] // 2) + m[0] % 2))
        )
        args += [rows_part, back]
    specs += [flat] * len(received)
    args += list(received)
    lead = 2 + len(args)
    body = functools.partial(term_kernel, layout, width, wanted, units, len(received), bool(tables))
    return pl.pallas_call(
        lambda *refs: body(*refs[:lead], *refs[-2:]),
        grid_spec=pltpu.PrefetchScalarGridSpec(
            num_scalar_prefetch=2, grid=(rows // chunk,), in_specs=specs + [ANY] * len(after), out_specs=[flat, whole(TOKEN)]
        ),
        out_shape=[jax.ShapeDtypeStruct((rows, share), F32), jax.ShapeDtypeStruct(TOKEN, F32)],
        compiler_params=pltpu.CompilerParams(vmem_limit_bytes=SOME),
        cost_estimate=SMALL,
        name="block_term",
    )(meta, starts, *args, *after)


def held_until(values, after):
    def body(*refs):
        del refs

    return pl.pallas_call(
        body,
        in_specs=[ANY] * (len(values) + len(after)),
        out_specs=[ANY] * len(values),
        out_shape=[jax.ShapeDtypeStruct(v.shape, v.dtype) for v in values],
        input_output_aliases={i: i for i in range(len(values))},
        compiler_params=pltpu.CompilerParams(vmem_limit_bytes=VMEM),
        cost_estimate=SMALL,
        name="held",
    )(*values, *after)


def arrived(values):
    def body(*refs):
        refs[-1][...] = jnp.zeros_like(refs[-1])

    return pl.pallas_call(
        body,
        in_specs=[ANY] * len(values),
        out_shape=jax.ShapeDtypeStruct(TOKEN, F32),
        compiler_params=pltpu.CompilerParams(vmem_limit_bytes=SOME),
        cost_estimate=pl.CostEstimate(flops=1000, bytes_accessed=8 * 10**6, transcendentals=0),
        name="arrived",
    )(*values)


def contract_last(left, right):
    return lax.dot_general(left, right, (((1,), (1,)), ((), ())), precision=HIGH, preferred_element_type=F32)


def contract_last_three(left, right):
    def one(a, b):
        return lax.dot_general(a, b, (((1,), (1,)), ((), ())), preferred_element_type=F32)

    (l_hi, l_lo), (r_hi, r_lo) = split_high_low(left), split_high_low(right)
    return one(l_hi, r_hi) + (one(l_lo, r_hi) + one(l_hi, r_lo))


def moments_kernel(places, strips, meta_ref, bins_ref, out_ref):
    count, _, rows, cols = bins_ref.shape
    at = [places.index(e) for e in range(count)]
    image = [bins_ref[at[e], 0] for e in range(count)]
    weight = [bins_ref[at[e], 1] for e in range(count)]
    x = centers(lax.broadcasted_iota(jnp.int32, (1, cols), 1), cols)
    tx = [jnp.ones_like(x), x]
    while len(tx) < 5:
        tx.append(2.0 * x * tx[-1] - tx[-2])
    tx = jnp.concatenate(tx + [jnp.zeros((3, cols), F32)], axis=0)
    joint, diffs = [], []
    for apart in range(1, count // 2 + 1):
        group, group_d = [], []
        for i in range(count):
            j = (i + apart) % count
            w = weight[i] * weight[j] / (weight[i] + weight[j] + 1.0)
            group.append(w)
            group_d.append(w * (image[i] - image[j]))
        joint.append(contract_last_three(tx, jnp.concatenate(group, axis=0)))
        diffs.append(contract_last_three(tx, jnp.concatenate(group_d, axis=0)))
    along = jnp.concatenate([jnp.concatenate(joint, axis=1), jnp.concatenate(diffs, axis=1)], axis=0)
    total = along.shape[1]
    row = lax.broadcasted_iota(jnp.int32, (total, SIDE), 0)
    lane = lax.broadcasted_iota(jnp.int32, (total, SIDE), 1)
    mine = row // rows == lane
    y = centers(row % rows + meta_ref[1] * rows, rows * strips)
    a_hi, a_lo = split_high_low(along)
    ty = [jnp.ones_like(y), y]
    for a in range(5):
        if a > 1:
            ty.append(2.0 * y * ty[-1] - ty[-2])
        b_hi, b_lo = split_high_low(jnp.where(mine, ty[a], 0.0))
        out_ref[:, a * SIDE : (a + 1) * SIDE] = mm(a_hi, b_hi) + (mm(a_lo, b_hi) + mm(a_hi, b_lo))


def solve_kernel(width, meta_ref, start_ref, moments_ref, owner_ref, out_ref, back_ref):
    owner = owner_ref[...].astype(F32)
    count = owner.shape[0]
    lanes = count * count // 2
    exposure = lax.broadcasted_iota(jnp.int32, (count, lanes), 0)
    lane = lax.broadcasted_iota(jnp.int32, (count, lanes), 1)
    mine = lane % count
    apart = lane // count + 1
    is_i = (exposure == mine).astype(F32)
    is_j = (exposure == (mine + apart) % count).astype(F32)
    both = owner + owner.T
    listed = jnp.sum(is_i * jnp.dot(both, is_j, precision=HIGH, preferred_element_type=F32), axis=0, keepdims=True)
    lane_row = lax.broadcasted_iota(jnp.int32, (1, lanes), 1)
    once = (lane_row // count + 1 < count // 2) | (lane_row % count < count // 2)
    listed = jnp.where(once, listed, 0.0)
    held = listed > 0.0
    moment = [[moments_ref[b : b + 1, a * SIDE : a * SIDE + lanes] for b in range(5)] for a in range(5)]

    def entry(k, l):
        (u, v), (s, t) = divmod(k, 3), divmod(l, 3)
        total = 0.0
        for a in (u + s, abs(u - s)):
            for b in (v + t, abs(v - t)):
                total = total + moment[a][b]
        return jnp.where(held, 0.25 * total, 1.0 if k == l else 0.0)

    factor = [[None] * 9 for _ in range(9)]
    scale = [None] * 9
    for k in range(9):
        for l in range(k, 9):
            value = entry(l, k)
            for m in range(k):
                value = value - factor[l][m] * factor[k][m]
            if l == k:
                scale[k] = 1.0 / jnp.sqrt(value)
            else:
                factor[l][k] = value * scale[k]
    half = [None] * 9
    for k in range(9):
        a, b = divmod(k, 3)
        value = moments_ref[8 + b : 9 + b, a * SIDE : a * SIDE + lanes]
        for m in range(k):
            value = value - factor[k][m] * half[m]
        half[k] = value * scale[k]
    fit = [None] * 9
    for k in reversed(range(9)):
        value = half[k]
        for m in range(k + 1, 9):
            value = value - factor[m][k] * fit[m]
        fit[k] = value * scale[k]
    fits = jnp.concatenate([jnp.where(held, f, 0.0) for f in fit] + [jnp.zeros((7, lanes), F32)], axis=0)
    right = contract_last((is_i - is_j) * listed, fits)
    row = lax.broadcasted_iota(jnp.int32, (count, count), 0)
    column = lax.broadcasted_iota(jnp.int32, (count, count), 1)
    degree = jnp.sum(both, axis=1, keepdims=True) + LAMBDA_REG
    system = jnp.where(row == column, degree, 0.0) - both
    for k in range(count):
        inverse = 1.0 / system[k : k + 1, k : k + 1]
        pivot_s, pivot_r = system[k : k + 1, :] * inverse, right[k : k + 1, :] * inverse
        lead = system[:, k : k + 1]
        chosen = row[:, :1] == k
        system = jnp.where(chosen, pivot_s, system - lead * pivot_s)
        right = jnp.where(chosen, pivot_r, right - lead * pivot_r)
    out_ref[...] = right[:, :9]
    member = meta_ref[0]
    mate = member + 1 - 2 * (member % 2)
    cols = back_ref.shape[1]
    padded = cols + 2 * SIDE
    col = lax.broadcasted_iota(jnp.int32, (1, padded), 1) - SIDE
    x = centers(col, cols)
    terms = [jnp.ones_like(x), x, 2.0 * x * x - 1.0]
    fields = [jnp.where(inside(col, start_ref[e], width), t, 0.0) for e in (member, mate) for t in terms]
    fields = jnp.concatenate(fields + [jnp.zeros((2, padded), F32)], axis=0)
    taps = tap_values()
    total = float(taps[RADIUS]) * fields
    for shift in range(1, RADIUS + 1):
        both = pltpu.roll(fields, shift, 1) + pltpu.roll(fields, padded - shift, 1)
        total = total + float(taps[RADIUS + shift]) * both
    total = total[:, SIDE : SIDE + cols]
    rows = lax.broadcasted_iota(jnp.int32, (count, 16), 0)
    for k, which in enumerate((member, mate)):
        mine = jnp.sum(jnp.where(rows == which, right, 0.0), axis=0, keepdims=True)
        for u in range(3):
            back_ref[3 * k + u : 3 * k + u + 1, :] = sum(
                mine[:, 3 * u + v : 3 * u + v + 1] * total[3 * k + v : 3 * k + v + 1, :] for v in range(3)
            )
    back_ref[6:8, :] = jnp.zeros((2, cols), F32)


def filtered_rows(total_rows):
    y = (2.0 * np.arange(total_rows) + 1.0) / total_rows - 1.0
    terms = np.stack([np.ones_like(y), y, 2.0 * y * y - 1.0])
    padded = np.pad(terms, ((0, 0), (RADIUS, RADIUS)))
    taps = tap_values()
    return sum(taps[t] * padded[:, t : t + total_rows] for t in range(2 * RADIUS + 1)).T.astype(np.float32)


def per_device(image, variance, mask, foot_start, pair_owner):
    frame, spread, blocks = image[0], variance[0], mask[0]
    rows, cols = frame.shape
    exposures, sky_count = lax.axis_size("exp"), lax.axis_size("sky")
    member = lax.axis_index("exp")
    meta = jnp.stack([member, lax.axis_index("sky")])
    width = 3 * cols // 4
    layout = Places(exposures, cols)
    share, places, quarter = layout.share, layout.places, layout.quarter
    ends, middle_count = layout.ends, layout.middle
    units = quarter + middle_count
    folded = [(i // 2, i % 2 == 0) for i in range(ends)]
    sent = folded + [(quarter + i, True) for i in range(middle_count)]
    rest = [None] * ends + [(i, True) for i in range(middle_count + places)]

    def sent_then_kept(i, meta):
        return jnp.where(i < places, layout.sent_block(i, meta), layout.kept_block(i - places, meta))

    swap = [(i, i ^ 1) for i in range(exposures)]

    def swapped(parts):
        return [lax.ppermute(part, "exp", swap) for part in parts]

    den_ends = pixel_weights(
        layout.sent_block, folded, quarter, meta, foot_start, None, spread, blocks, share, width
    )
    *den_middle, den_kept, gathered = pixel_weights(
        sent_then_kept, rest, middle_count, meta, foot_start, frame, spread, blocks, share, width, after=den_ends
    )
    got_ends = swapped(den_ends)
    got_middle = swapped(den_middle)
    den_got = got_ends + got_middle

    up = [(i, i + 1) for i in range(sky_count - 1)]
    down = [(j, i) for i, j in up]
    above = lax.ppermute(frame[rows - HALO :], "sky", up)
    below = lax.ppermute(frame[:HALO], "sky", down)
    smooth = functools.partial(
        smoothed_terms, meta=meta, starts=foot_start, frame=frame, above=above, below=below, share=share, width=width
    )

    held = [0]
    bits = [1 << k for k in range(exposures.bit_length() - 1)]

    def asked(gathered, bit):
        return lax.ppermute(gathered, "exp", [(i, i ^ bit) for i in range(exposures)])

    def joined(gathered, other, bit):
        low = (member & bit) == 0
        held.extend([e | bit for e in held])
        return jnp.concatenate([jnp.where(low, gathered, other), jnp.where(low, other, gathered)])

    for bit in bits[1:]:
        if bit > 2:
            (gathered,) = held_until([gathered], got_ends)
        gathered = joined(gathered, asked(gathered, bit), bit)

    def to_right(step):
        return lambda z: choose(z < step, z + places - step, places - 1)

    def to_left(step):
        return lambda z: choose(z >= places - step, z - places + step, 0)

    def outward(step):
        return lambda z: choose(z < places // 2, to_right(step)(z), to_left(step)(z))

    def shift(value, rights, lefts):
        pairs = [(2 * z + s, 2 * z + 2 + s) for z in rights for s in range(2)]
        pairs += [(2 * z + s, 2 * z - 2 + s) for z in lefts for s in range(2)]
        return lax.ppermute(value, "exp", pairs)

    def along_places(step, term, sums, after):
        rights, lefts = range(step), range(places - step, places)
        if step <= places // 2:
            value, token = term(outward(step), [*rights, *lefts], sums, after)
            if step < places // 2:
                return (shift(value, rights, lefts),), (token,)
            return (shift(value, rights, []), shift(value, [], lefts)), (token,)
        right, token = term(to_right(step), rights, sums[:1], after)
        left, token_left = term(to_left(step), lefts, sums[1:], after)
        return (shift(right, rights, []), shift(left, [], lefts)), (token, token_left)

    def den_term(wanted, senders, sums, after):
        parts = [(den_kept, den_got)]
        return block_term(layout, width, wanted, senders, meta, foot_start, parts, sums, after=after)

    den_sums, den_values = along_places(1, den_term, (), [gathered])
    *num_sent, token = smooth(layout.sent_block, sent, [*den_ends, *den_middle], after=den_values)
    other = asked(gathered, bits[0])
    num_kept, token = smooth(layout.kept_block, [(i, True) for i in range(places)], [den_kept], after=[token])
    num_sent = held_until(num_sent, [token, other])
    num_got = swapped(num_sent)
    den_sums, den_values = along_places(2, den_term, den_sums, [token])

    (gathered,) = held_until([joined(gathered, other, bits[0])], den_values)
    scalars = pl.BlockSpec(memory_space=pltpu.SMEM)
    vmem = pl.BlockSpec(memory_space=pltpu.VMEM)
    moments = pl.pallas_call(
        functools.partial(moments_kernel, held, sky_count),
        in_specs=[scalars, vmem],
        out_shape=jax.ShapeDtypeStruct((16, 5 * SIDE), F32),
        compiler_params=pltpu.CompilerParams(vmem_limit_bytes=SOME),
        cost_estimate=SMALL,
        name="pair_moments",
    )(meta, gathered)
    bit = 1
    while bit < sky_count:
        moments = moments + lax.ppermute(moments, "sky", [(i, i ^ bit) for i in range(sky_count)])
        bit *= 2
    offsets, back = pl.pallas_call(
        functools.partial(solve_kernel, width),
        in_specs=[scalars, scalars, vmem, vmem],
        out_shape=[jax.ShapeDtypeStruct((exposures, 9), F32), jax.ShapeDtypeStruct((8, cols), F32)],
        compiler_params=pltpu.CompilerParams(vmem_limit_bytes=SOME),
        cost_estimate=SMALL,
        name="offsets",
    )(meta, foot_start, moments, pair_owner)

    tables = (jnp.asarray(filtered_rows(rows * sky_count)), back)
    parts = [(den_kept, den_got), (num_kept, num_got)]

    def num_term(wanted, senders, sums, after):
        return block_term(
            layout, width, wanted, senders, meta, foot_start, parts, sums, tables, after
        )

    num_sums, num_values = along_places(1, num_term, (), den_values)
    for step in range(3, places):
        den_sums, den_values = along_places(step, den_term, den_sums, num_values)
        num_sums, num_values = along_places(step - 1, num_term, num_sums, den_values)

    ahead = [*num_values, arrived(den_sums)]
    terms = []
    for wanted, senders in ((to_right(places - 1), range(places - 1)), (to_left(places - 1), range(1, places))):
        value, token = num_term(wanted, senders, (), ahead)
        terms.append(value)
        ahead = [token]
    rightward = shift(terms[0] + num_sums[0], range(places - 1), [])
    leftward = shift(terms[1] + num_sums[1], [], range(1, places))
    own_den, token = den_term(lambda z: z, range(places), den_sums, ahead)
    own_num, _ = num_term(lambda z: z, range(places), (), [token])
    coadd = (own_num + rightward + leftward) / (PRIOR + own_den)
    return (coadd, offsets)


def solution(mesh):
    placed = (P("exp", "sky", None), P("exp", "sky", None), P("exp", "sky", None), P(), P())
    return jax.shard_map(
        per_device, mesh=mesh, in_specs=placed, out_specs=(P("sky", "exp"), P()), check_vma=False
    )
```

```python
import functools

import jax
import jax.numpy as jnp
import numpy as np
from jax import lax
from jax.experimental import pallas as pl
from jax.experimental.pallas import tpu as pltpu
from jax.sharding import PartitionSpec as P

BIN = 16
RADIUS = 10
HALO = 16
SIDE = 128
TOKEN = (8, 128)
TILE = 256
CHUNK = 64

HIGH = lax.Precision.HIGHEST
LAMBDA_REG = 0.25
PRIOR = 1.0
VMEM = 127 * 512 * 1024
SOME = 24 * 1024 * 1024
BF16 = jnp.bfloat16
F32 = jnp.float32
SMALL = pl.CostEstimate(flops=1000, bytes_accessed=1000, transcendentals=0)


def tap_values():
    offs = np.arange(-RADIUS, RADIUS + 1).astype(np.float64)
    taps = np.exp(-offs * offs / 50.0)
    return taps / taps.sum()


def band(out, width, lead):
    taps = tap_values()
    full = np.zeros((out, width), np.float64)
    for shift in range(-RADIUS, RADIUS + 1):
        rows = np.arange(out)
        full[rows, rows + lead + shift] = taps[shift + RADIUS]
    return full


def centers(index, total):
    return (2.0 * index.astype(F32) + 1.0) / total - 1.0


def split_high_low(value):
    high = value.astype(BF16)
    return high, (value - high.astype(F32)).astype(BF16)


def mm(left, right):
    return jnp.dot(left, right, preferred_element_type=F32)


def choose(condition, left, right):
    if isinstance(condition, (bool, np.bool_)):
        return left if condition else right
    return jnp.where(condition, left, right)


class Places:
    def __init__(self, exposures, cols):
        self.share = cols // exposures
        self.places = exposures // 2
        self.quarter = self.places // 4
        self.ends = 2 * self.quarter
        self.middle = self.places - self.ends

    def place_of(self, at, place):
        down = place < self.places // 2
        pair = at // 2
        end = choose(down, self.quarter - 1 - pair, pair) + (at % 2) * (self.places - self.quarter)
        turn = at - self.ends
        mid = choose(down, self.places - self.quarter - 1 - turn, self.quarter + turn)
        return choose(at < self.ends, end, mid)

    def position_of(self, wanted, place):
        down = place < self.places // 2
        right = wanted >= self.places - self.quarter
        low = choose(right, wanted - (self.places - self.quarter), wanted)
        pair = choose(down, self.quarter - 1 - low, low)
        turn = choose(down, self.places - self.quarter - 1 - wanted, wanted - self.quarter)
        is_end = right | (wanted < self.quarter)
        at = choose(is_end, 2 * pair + choose(right, 1, 0), self.ends + turn)
        return at, choose(is_end, pair, self.quarter + turn)

    def sent_block(self, at, meta):
        return 2 * self.place_of(at, meta[0] // 2) + 1 - meta[0] % 2

    def kept_block(self, at, meta):
        return 2 * self.place_of(at, meta[0] // 2) + meta[0] % 2


def inside(col, start, width):
    return (col >= start * BIN) & (col < start * BIN + width)


def columns(block, share, width=None, lead=0):
    return lax.broadcasted_iota(jnp.int32, (1, width or share), 1) + (block * share - lead)


def reciprocal(value):
    rough = pl.reciprocal(value, approx=True)
    rough = rough * (2.0 - value * rough)
    return rough * (2.0 - value * rough)


def expanded(kept, rows):
    return jnp.broadcast_to(kept[:, None, :], (kept.shape[0], BIN, kept.shape[1])).reshape(rows, kept.shape[1])


def folded_kernel(layout, width, meta_ref, start_ref, spread_ref, mask_ref, out_ref, scatter):
    step = pl.program_id(0)
    block = layout.sent_block(step, meta_ref)
    rows, share = spread_ref.shape
    bins_col = mask_ref.shape[1]
    per = share // BIN

    @pl.when(step == 0)
    def _():
        cell = lax.broadcasted_iota(jnp.int32, (SIDE, share), 1) >> 4
        scatter[...] = (cell == lax.broadcasted_iota(jnp.int32, (SIDE, share), 0)).astype(BF16)

    blocks_here = pltpu.roll(mask_ref[...].astype(F32), lax.rem(bins_col - block * per, bins_col), 1)[:, :SIDE]
    kept = mm(blocks_here.astype(BF16), scatter[...])
    kept = jnp.where(inside(columns(block, share), start_ref[meta_ref[0]], width), kept, 0.0)
    for top in range(0, rows, CHUNK):
        here = slice(top, top + CHUNK)
        weight = reciprocal(spread_ref[here]) * expanded(kept[top // BIN : (top + CHUNK) // BIN], CHUNK)
        out_ref[0, here] = jnp.where(step % 2 == 0, weight, out_ref[0, here] + weight)


def weights_kernel(layout, width, meta_ref, start_ref, frame_ref, spread_ref, mask_ref, *refs):
    *outs, kept_ref, bins_ref, scatter, gather, kept_mask, inverse_ref = refs[:-5]
    splits = refs[-5:]
    share = layout.share
    blocks = 2 * layout.places
    rows, cols = spread_ref.shape
    bins_row, bins_col = mask_ref.shape
    per = share // BIN
    start = start_ref[meta_ref[0]]
    half = SIDE * BIN

    @pl.when(pl.program_id(0) == 0)
    def _():
        cell = lax.broadcasted_iota(jnp.int32, (SIDE, half), 1) >> 4
        scatter[...] = (cell == lax.broadcasted_iota(jnp.int32, (SIDE, half), 0)).astype(BF16)
        cell = lax.broadcasted_iota(jnp.int32, (share, SIDE), 0) >> 4
        gather[...] = (cell == lax.broadcasted_iota(jnp.int32, (share, SIDE), 1)).astype(BF16)

    mask = mask_ref[...].astype(F32)
    for part in range(bins_col // SIDE):
        here = slice(part * half, (part + 1) * half)
        kept = mm(mask[:, part * SIDE : (part + 1) * SIDE].astype(BF16), scatter[...])
        kept_mask[:, here] = jnp.where(inside(columns(part, half), start, width), kept, 0.0)
    tall = rows // 2
    for block in range(blocks):
        here = slice(block * share, (block + 1) * share)
        inverse = reciprocal(spread_ref[:, here])
        inverse_ref[:, here] = inverse
        for value, parts in ((frame_ref[:, here], splits[:3]), (inverse, splits[3:])):
            value = value.reshape(bins_row, 2, 8, share).sum(axis=1).reshape(tall, share)
            for split in parts:
                rounded = value.astype(BF16)
                split[block * tall : (block + 1) * tall] = rounded
                value = value - rounded.astype(F32)

    def block_weights(block):
        here = pl.ds(pl.multiple_of(block * share, share), share)
        return inverse_ref[:, here] * expanded(kept_mask[:, here], rows)

    for at, out in enumerate(outs):
        out[...] = block_weights(layout.sent_block(at + layout.ends, meta_ref))
    for at in range(layout.places):
        kept_ref[at] = block_weights(layout.kept_block(at, meta_ref))

    def binned(parts):
        sums = mm(parts[0][...], gather[...])
        for split in parts[1:]:
            sums = sums + mm(split[...], gather[...])
        sums = sums.reshape(blocks * bins_row, 8, SIDE).sum(axis=1)
        halves = []
        for part in range(bins_col // SIDE):
            group = SIDE // per
            halves.append(
                sum(
                    pltpu.roll(sums[block * bins_row : (block + 1) * bins_row], (block % group) * per, 1)
                    for block in range(part * group, (part + 1) * group)
                )
            )
        return jnp.concatenate(halves, axis=1)

    cell = lax.broadcasted_iota(jnp.int32, (1, bins_col), 1) * BIN
    bins_ref[0, 0] = binned(splits[:3]) / (BIN * BIN)
    bins_ref[0, 1] = binned(splits[3:]) * jnp.where(inside(cell, start, width), mask, 0.0)


ANY = pl.BlockSpec(memory_space=pl.ANY)


def whole(shape):
    return pl.BlockSpec(shape, lambda *_: (0,) * len(shape))


def folded_weights(layout, width, meta, starts, spread, mask):
    rows, share = spread.shape[0], layout.share
    out = pl.pallas_call(
        functools.partial(folded_kernel, layout, width),
        grid_spec=pltpu.PrefetchScalarGridSpec(
            num_scalar_prefetch=2,
            grid=(layout.ends,),
            in_specs=[
                pl.BlockSpec((rows, share), lambda i, meta, starts: (0, layout.sent_block(i, meta))),
                whole(mask.shape),
            ],
            out_specs=pl.BlockSpec((1, rows, share), lambda i, meta, starts: (i // 2, 0, 0)),
            scratch_shapes=[pltpu.VMEM((SIDE, share), BF16)],
        ),
        out_shape=pltpu.HBM((layout.quarter, rows, share), F32),
        compiler_params=pltpu.CompilerParams(vmem_limit_bytes=VMEM),
        cost_estimate=SMALL,
        name="folded_weights",
    )(meta, starts, spread, mask)
    return [out.reshape(rows, share)] if layout.quarter == 1 else [out[k] for k in range(layout.quarter)]


def pixel_weights(layout, width, meta, starts, frame, spread, mask, after):
    rows, cols = spread.shape
    bins_row, bins_col = mask.shape
    share, places = layout.share, layout.places
    tall = min(SIDE, rows)
    tile = pl.BlockSpec((tall, cols), lambda i, meta, starts: (i, 0))
    kernel = functools.partial(weights_kernel, layout, width)
    return pl.pallas_call(
        lambda *refs: kernel(*refs[:5], *refs[5 + len(after) :]),
        grid_spec=pltpu.PrefetchScalarGridSpec(
            num_scalar_prefetch=2,
            grid=(rows // tall,),
            in_specs=[tile, tile, pl.BlockSpec((tall // BIN, bins_col), lambda i, meta, starts: (i, 0))]
            + [ANY] * len(after),
            out_specs=[pl.BlockSpec((tall, share), lambda i, meta, starts: (i, 0))] * layout.middle
            + [
                pl.BlockSpec((places, tall, share), lambda i, meta, starts: (0, i, 0)),
                pl.BlockSpec((1, 2, tall // BIN, bins_col), lambda i, meta, starts: (0, 0, i, 0)),
            ],
            scratch_shapes=[
                pltpu.VMEM((SIDE, SIDE * BIN), BF16),
                pltpu.VMEM((share, SIDE), BF16),
                pltpu.VMEM((tall // BIN, cols), F32),
                pltpu.VMEM((tall, cols), F32),
            ]
            + [pltpu.VMEM((2 * places * tall // 2, share), BF16)] * 5,
        ),
        out_shape=[pltpu.HBM((rows, share), F32)] * layout.middle
        + [pltpu.HBM((places, rows, share), F32), jax.ShapeDtypeStruct((1, 2, bins_row, bins_col), F32)],
        compiler_params=pltpu.CompilerParams(vmem_limit_bytes=VMEM),
        cost_estimate=SMALL,
        name="pixel_weights",
    )(meta, starts, frame, spread, mask, *after)


def smooth_kernel(block_of, plan, width, stacked, meta_ref, start_ref, *refs):
    step = pl.program_id(0)
    images, bands, scratch = refs[:9], refs[9:13], refs[-8:]
    refs = refs[13:-8]
    *refs, token_ref = refs
    token_ref[...] = jnp.zeros_like(token_ref)
    weights, outs = refs[: len(refs) // 2], refs[len(refs) // 2 :]

    @pl.when(step == 0)
    def _():
        for k, matrix in enumerate(bands):
            scratch[2 * k][...], scratch[2 * k + 1][...] = split_high_low(matrix[...])

    col_hi, col_lo, row_hi, row_lo, up_hi, up_lo, down_hi, down_lo = scratch
    block = block_of(step, meta_ref)
    start = start_ref[meta_ref[0]]
    rows, share = images[4].shape
    window = share + 2 * SIDE
    field = jnp.concatenate(
        [jnp.concatenate([images[3 * i + j][...] for j in range(3)], axis=1) for i in range(3)], axis=0
    )
    field = jnp.where(inside(columns(block, share, window, SIDE), start, width), field, 0.0)
    high, low = split_high_low(field)

    def three(a_hi, a_lo, b_hi, b_lo):
        return mm(a_hi, b_hi) + (mm(a_lo, b_hi) + mm(a_hi, b_lo))

    tiles = []
    for tile in range(share // TILE):
        lanes = slice(tile * TILE, (tile + 1) * TILE + 2 * SIDE)
        tiles.append(three(high[:, lanes], low[:, lanes], col_hi[...], col_lo[...]))
    across = tiles[0] if len(tiles) == 1 else jnp.concatenate(tiles, axis=1)
    high, low = split_high_low(across)
    height = row_hi.shape[0]
    tiles = []
    for tile in range(rows // height):
        top = tile * height
        mid = slice(top + HALO, top + HALO + height)
        upper = slice(top, top + HALO)
        lower = slice(top + HALO + height, top + 2 * HALO + height)
        main = three(row_hi[...], row_lo[...], high[mid], low[mid])
        tiles += [
            main[:HALO] + three(up_hi[...], up_lo[...], high[upper], low[upper]),
            main[HALO : height - HALO],
            main[height - HALO :] + three(down_hi[...], down_lo[...], high[lower], low[lower]),
        ]
    smoothed = jnp.concatenate(tiles, axis=0)
    smoothed = jnp.where(inside(columns(block, share), start, width), smoothed, 0.0)
    if stacked:
        outs[0][0] = weights[0][0] * smoothed
        return
    for at, (out, fresh) in enumerate(plan):
        @pl.when(step == at)
        def _(out=out, fresh=fresh):
            term = weights[out][...] * smoothed
            outs[out][...] = term if fresh else outs[out][...] + term


def smoothed_terms(block_of, plan, weights, meta, starts, frame, above, below, share, width, after=()):
    rows, cols = frame.shape
    stacked = weights[0].ndim == 3
    count = len(weights)
    per = share // SIDE
    last = cols // SIDE - 1
    specs = []
    for height in (HALO, rows, HALO):
        specs += [
            pl.BlockSpec((height, SIDE), lambda i, m, s: (0, jnp.maximum(block_of(i, m) * per - 1, 0))),
            pl.BlockSpec((height, share), lambda i, m, s: (0, block_of(i, m))),
            pl.BlockSpec((height, SIDE), lambda i, m, s: (0, jnp.minimum(block_of(i, m) * per + per, last))),
        ]
    if stacked:
        parts_spec = pl.BlockSpec((1, rows, share), lambda i, m, s: (i, 0, 0))
    else:
        parts_spec = whole((rows, share))
    height = min(TILE, rows)
    full = band(height, height + 2 * HALO, HALO)
    bands = [
        band(TILE, TILE + 2 * SIDE, SIDE).T,
        full[:, HALO : HALO + height],
        full[:HALO, :HALO],
        full[height - HALO :, HALO + height :],
    ]
    parts = [jnp.asarray(matrix.astype(np.float32)) for matrix in bands]

    def body(*refs):
        lead = 2 + 9 + len(parts) + count
        smooth_kernel(block_of, plan, width, stacked, *refs[:lead], *refs[lead + len(after) :])

    return pl.pallas_call(
        body,
        grid_spec=pltpu.PrefetchScalarGridSpec(
            num_scalar_prefetch=2,
            grid=(len(plan),),
            in_specs=specs + [whole(p.shape) for p in parts] + [parts_spec] * count + [ANY] * len(after),
            out_specs=[parts_spec] * count + [whole(TOKEN)],
            scratch_shapes=[pltpu.VMEM(p.shape, BF16) for p in parts for _ in range(2)],
        ),
        out_shape=[pltpu.HBM(w.shape, F32) for w in weights] + [jax.ShapeDtypeStruct(TOKEN, F32)],
        compiler_params=pltpu.CompilerParams(vmem_limit_bytes=VMEM),
        cost_estimate=SMALL,
        name="smoothed_terms",
    )(meta, starts, *([above] * 3 + [frame] * 3 + [below] * 3), *parts, *weights, *after)


def term_kernel(layout, width, wanted, units, received, numerator, meta_ref, start_ref, *refs):
    place = meta_ref[0] // 2
    block = 2 * wanted(place) + meta_ref[0] % 2
    _, unit = layout.position_of(wanted(place), place)
    mate_start = start_ref[meta_ref[0] + 1 - 2 * (meta_ref[0] % 2)]
    in_mate = inside(columns(block, layout.share), mate_start, width)
    *refs, out_ref, token_ref = refs
    token_ref[...] = jnp.zeros_like(token_ref)

    def pair():
        own = refs.pop(0)[0]
        got = refs.pop(0)[...]
        for u in units[1:]:
            got = jnp.where(unit == u, refs.pop(0)[...], got)
        return own, got

    def added(own, got, names):
        value = own + jnp.where(in_mate, got, 0.0)
        for _ in range(names):
            value = value + refs.pop(0)[...]
        return value

    if not numerator:
        out_ref[...] = added(*pair(), received)
        return
    own_den, mate_den = pair()
    own, mate = pair()
    rows_part, back = refs.pop(0)[...], refs.pop(0)[...]
    own_back = sum(rows_part[:, u : u + 1] * back[u : u + 1, :] for u in range(3))
    mate_back = sum(rows_part[:, u : u + 1] * back[3 + u : 4 + u, :] for u in range(3))
    top = added(own - own_den * own_back, mate - mate_den * mate_back, received)
    out_ref[...] = top


def block_term(layout, width, wanted, senders, meta, starts, parts, received, tables=(), after=()):
    kept = parts[0][0]
    rows, share = kept.shape[1:]
    chunk = min(TILE, rows)

    def at_unit(place):
        return layout.position_of(wanted(place), place)

    units = sorted({int(at_unit(z)[1]) for z in senders})
    flat = pl.BlockSpec((chunk, share), lambda r, m, s: (r, 0))
    specs, args = [], []
    for own, got in parts:
        specs.append(pl.BlockSpec((1, chunk, share), lambda r, m, s: (at_unit(m[0] // 2)[0], r, 0)))
        args.append(pltpu.with_memory_space_constraint(own, pltpu.HBM))
        for u in units:
            specs.append(
                flat
                if len(units) == 1
                else pl.BlockSpec(
                    (chunk, share), lambda r, m, s, u=u: (jnp.where(at_unit(m[0] // 2)[1] == u, r, 0), 0)
                )
            )
            args.append(got[u])
    if tables:
        rows_part, back = tables
        strips = rows // chunk
        specs.append(pl.BlockSpec((chunk, rows_part.shape[1]), lambda r, m, s: (m[1] * strips + r, 0)))
        specs.append(
            pl.BlockSpec((back.shape[0], share), lambda r, m, s: (0, 2 * wanted(m[0] // 2) + m[0] % 2))
        )
        args += [rows_part, back]
    specs += [flat] * len(received)
    args += list(received)
    lead = 2 + len(args)
    body = functools.partial(term_kernel, layout, width, wanted, units, len(received), bool(tables))
    return pl.pallas_call(
        lambda *refs: body(*refs[:lead], *refs[-2:]),
        grid_spec=pltpu.PrefetchScalarGridSpec(
            num_scalar_prefetch=2, grid=(rows // chunk,), in_specs=specs + [ANY] * len(after), out_specs=[flat, whole(TOKEN)]
        ),
        out_shape=[jax.ShapeDtypeStruct((rows, share), F32), jax.ShapeDtypeStruct(TOKEN, F32)],
        compiler_params=pltpu.CompilerParams(vmem_limit_bytes=SOME),
        cost_estimate=SMALL,
        name="block_term",
    )(meta, starts, *args, *after)


def held_until(values, after):
    def body(*refs):
        del refs

    return pl.pallas_call(
        body,
        in_specs=[ANY] * (len(values) + len(after)),
        out_specs=[ANY] * len(values),
        out_shape=[jax.ShapeDtypeStruct(v.shape, v.dtype) for v in values],
        input_output_aliases={i: i for i in range(len(values))},
        compiler_params=pltpu.CompilerParams(vmem_limit_bytes=VMEM),
        cost_estimate=SMALL,
        name="held",
    )(*values, *after)


def arrived(values):
    def body(*refs):
        refs[-1][...] = jnp.zeros_like(refs[-1])

    return pl.pallas_call(
        body,
        in_specs=[ANY] * len(values),
        out_shape=jax.ShapeDtypeStruct(TOKEN, F32),
        compiler_params=pltpu.CompilerParams(vmem_limit_bytes=SOME),
        cost_estimate=pl.CostEstimate(flops=1000, bytes_accessed=8 * 10**6, transcendentals=0),
        name="arrived",
    )(*values)


def contract_last(left, right):
    return lax.dot_general(left, right, (((1,), (1,)), ((), ())), precision=HIGH, preferred_element_type=F32)


def contract_last_three(left, right):
    def one(a, b):
        return lax.dot_general(a, b, (((1,), (1,)), ((), ())), preferred_element_type=F32)

    (l_hi, l_lo), (r_hi, r_lo) = split_high_low(left), split_high_low(right)
    return one(l_hi, r_hi) + (one(l_lo, r_hi) + one(l_hi, r_lo))


def moments_kernel(places, strips, meta_ref, bins_ref, out_ref):
    count, _, rows, cols = bins_ref.shape
    at = [places.index(e) for e in range(count)]
    image = [bins_ref[at[e], 0] for e in range(count)]
    weight = [bins_ref[at[e], 1] for e in range(count)]
    x = centers(lax.broadcasted_iota(jnp.int32, (1, cols), 1), cols)
    tx = [jnp.ones_like(x), x]
    while len(tx) < 5:
        tx.append(2.0 * x * tx[-1] - tx[-2])
    tx = jnp.concatenate(tx + [jnp.zeros((3, cols), F32)], axis=0)
    joint, diffs = [], []
    for apart in range(1, count // 2 + 1):
        group, group_d = [], []
        for i in range(count):
            j = (i + apart) % count
            w = weight[i] * weight[j] / (weight[i] + weight[j] + 1.0)
            group.append(w)
            group_d.append(w * (image[i] - image[j]))
        joint.append(contract_last_three(tx, jnp.concatenate(group, axis=0)))
        diffs.append(contract_last_three(tx, jnp.concatenate(group_d, axis=0)))
    along = jnp.concatenate([jnp.concatenate(joint, axis=1), jnp.concatenate(diffs, axis=1)], axis=0)
    total = along.shape[1]
    row = lax.broadcasted_iota(jnp.int32, (total, SIDE), 0)
    lane = lax.broadcasted_iota(jnp.int32, (total, SIDE), 1)
    mine = row // rows == lane
    y = centers(row % rows + meta_ref[1] * rows, rows * strips)
    a_hi, a_lo = split_high_low(along)
    ty = [jnp.ones_like(y), y]
    for a in range(5):
        if a > 1:
            ty.append(2.0 * y * ty[-1] - ty[-2])
        b_hi, b_lo = split_high_low(jnp.where(mine, ty[a], 0.0))
        out_ref[:, a * SIDE : (a + 1) * SIDE] = mm(a_hi, b_hi) + (mm(a_lo, b_hi) + mm(a_hi, b_lo))


def solve_kernel(width, meta_ref, start_ref, moments_ref, owner_ref, out_ref, back_ref):
    owner = owner_ref[...].astype(F32)
    count = owner.shape[0]
    lanes = count * count // 2
    exposure = lax.broadcasted_iota(jnp.int32, (count, lanes), 0)
    lane = lax.broadcasted_iota(jnp.int32, (count, lanes), 1)
    mine = lane % count
    apart = lane // count + 1
    is_i = (exposure == mine).astype(F32)
    is_j = (exposure == (mine + apart) % count).astype(F32)
    both = owner + owner.T
    listed = jnp.sum(is_i * jnp.dot(both, is_j, precision=HIGH, preferred_element_type=F32), axis=0, keepdims=True)
    lane_row = lax.broadcasted_iota(jnp.int32, (1, lanes), 1)
    once = (lane_row // count + 1 < count // 2) | (lane_row % count < count // 2)
    listed = jnp.where(once, listed, 0.0)
    held = listed > 0.0
    moment = [[moments_ref[b : b + 1, a * SIDE : a * SIDE + lanes] for b in range(5)] for a in range(5)]

    def entry(k, l):
        (u, v), (s, t) = divmod(k, 3), divmod(l, 3)
        total = 0.0
        for a in (u + s, abs(u - s)):
            for b in (v + t, abs(v - t)):
                total = total + moment[a][b]
        return jnp.where(held, 0.25 * total, 1.0 if k == l else 0.0)

    factor = [[None] * 9 for _ in range(9)]
    scale = [None] * 9
    for k in range(9):
        for l in range(k, 9):
            value = entry(l, k)
            for m in range(k):
                value = value - factor[l][m] * factor[k][m]
            if l == k:
                scale[k] = 1.0 / jnp.sqrt(value)
            else:
                factor[l][k] = value * scale[k]
    half = [None] * 9
    for k in range(9):
        a, b = divmod(k, 3)
        value = moments_ref[8 + b : 9 + b, a * SIDE : a * SIDE + lanes]
        for m in range(k):
            value = value - factor[k][m] * half[m]
        half[k] = value * scale[k]
    fit = [None] * 9
    for k in reversed(range(9)):
        value = half[k]
        for m in range(k + 1, 9):
            value = value - factor[m][k] * fit[m]
        fit[k] = value * scale[k]
    fits = jnp.concatenate([jnp.where(held, f, 0.0) for f in fit] + [jnp.zeros((7, lanes), F32)], axis=0)
    right = contract_last((is_i - is_j) * listed, fits)
    row = lax.broadcasted_iota(jnp.int32, (count, count), 0)
    column = lax.broadcasted_iota(jnp.int32, (count, count), 1)
    degree = jnp.sum(both, axis=1, keepdims=True) + LAMBDA_REG
    system = jnp.where(row == column, degree, 0.0) - both
    for k in range(count):
        inverse = 1.0 / system[k : k + 1, k : k + 1]
        pivot_s, pivot_r = system[k : k + 1, :] * inverse, right[k : k + 1, :] * inverse
        lead = system[:, k : k + 1]
        chosen = row[:, :1] == k
        system = jnp.where(chosen, pivot_s, system - lead * pivot_s)
        right = jnp.where(chosen, pivot_r, right - lead * pivot_r)
    out_ref[...] = right[:, :9]
    member = meta_ref[0]
    mate = member + 1 - 2 * (member % 2)
    cols = back_ref.shape[1]
    padded = cols + 2 * SIDE
    col = lax.broadcasted_iota(jnp.int32, (1, padded), 1) - SIDE
    x = centers(col, cols)
    terms = [jnp.ones_like(x), x, 2.0 * x * x - 1.0]
    fields = [jnp.where(inside(col, start_ref[e], width), t, 0.0) for e in (member, mate) for t in terms]
    fields = jnp.concatenate(fields + [jnp.zeros((2, padded), F32)], axis=0)
    taps = tap_values()
    total = float(taps[RADIUS]) * fields
    for shift in range(1, RADIUS + 1):
        both = pltpu.roll(fields, shift, 1) + pltpu.roll(fields, padded - shift, 1)
        total = total + float(taps[RADIUS + shift]) * both
    total = total[:, SIDE : SIDE + cols]
    rows = lax.broadcasted_iota(jnp.int32, (count, 16), 0)
    for k, which in enumerate((member, mate)):
        mine = jnp.sum(jnp.where(rows == which, right, 0.0), axis=0, keepdims=True)
        for u in range(3):
            back_ref[3 * k + u : 3 * k + u + 1, :] = sum(
                mine[:, 3 * u + v : 3 * u + v + 1] * total[3 * k + v : 3 * k + v + 1, :] for v in range(3)
            )
    back_ref[6:8, :] = jnp.zeros((2, cols), F32)


def filtered_rows(total_rows):
    y = (2.0 * np.arange(total_rows) + 1.0) / total_rows - 1.0
    terms = np.stack([np.ones_like(y), y, 2.0 * y * y - 1.0])
    padded = np.pad(terms, ((0, 0), (RADIUS, RADIUS)))
    taps = tap_values()
    return sum(taps[t] * padded[:, t : t + total_rows] for t in range(2 * RADIUS + 1)).T.astype(np.float32)


def per_device(image, variance, mask, foot_start, pair_owner):
    frame, spread, blocks = image[0], variance[0], mask[0]
    rows, cols = frame.shape
    exposures, sky_count = lax.axis_size("exp"), lax.axis_size("sky")
    member = lax.axis_index("exp")
    meta = jnp.stack([member, lax.axis_index("sky")])
    width = 3 * cols // 4
    layout = Places(exposures, cols)
    share, places, quarter = layout.share, layout.places, layout.quarter
    ends, middle_count = layout.ends, layout.middle
    sent = [(i // 2, i % 2 == 0) for i in range(ends)] + [(quarter + i, True) for i in range(middle_count)]
    swap = [(i, i ^ 1) for i in range(exposures)]

    def swapped(parts):
        return [lax.ppermute(part, "exp", swap) for part in parts]

    den_ends = folded_weights(layout, width, meta, foot_start, spread, blocks)
    *den_middle, den_kept, gathered = pixel_weights(
        layout, width, meta, foot_start, frame, spread, blocks, den_ends
    )
    got_ends = swapped(den_ends)
    got_middle = swapped(den_middle)
    den_got = got_ends + got_middle

    up = [(i, i + 1) for i in range(sky_count - 1)]
    down = [(j, i) for i, j in up]
    above = lax.ppermute(frame[rows - HALO :], "sky", up)
    below = lax.ppermute(frame[:HALO], "sky", down)
    smooth = functools.partial(
        smoothed_terms, meta=meta, starts=foot_start, frame=frame, above=above, below=below, share=share, width=width
    )

    held = [0]
    bits = [1 << k for k in range(exposures.bit_length() - 1)]

    def asked(gathered, bit):
        return lax.ppermute(gathered, "exp", [(i, i ^ bit) for i in range(exposures)])

    def joined(gathered, other, bit):
        low = (member & bit) == 0
        held.extend([e | bit for e in held])
        return jnp.concatenate([jnp.where(low, gathered, other), jnp.where(low, other, gathered)])

    for bit in bits[1:]:
        if bit > 2:
            (gathered,) = held_until([gathered], got_ends)
        gathered = joined(gathered, asked(gathered, bit), bit)

    def to_right(step):
        return lambda z: choose(z < step, z + places - step, places - 1)

    def to_left(step):
        return lambda z: choose(z >= places - step, z - places + step, 0)

    def outward(step):
        return lambda z: choose(z < places // 2, to_right(step)(z), to_left(step)(z))

    def shift(value, rights, lefts):
        pairs = [(2 * z + s, 2 * z + 2 + s) for z in rights for s in range(2)]
        pairs += [(2 * z + s, 2 * z - 2 + s) for z in lefts for s in range(2)]
        return lax.ppermute(value, "exp", pairs)

    def along_places(step, term, sums, after):
        rights, lefts = range(step), range(places - step, places)
        if step <= places // 2:
            value, token = term(outward(step), [*rights, *lefts], sums, after)
            if step < places // 2:
                return (shift(value, rights, lefts),), (token,)
            return (shift(value, rights, []), shift(value, [], lefts)), (token,)
        right, token = term(to_right(step), rights, sums[:1], after)
        left, token_left = term(to_left(step), lefts, sums[1:], after)
        return (shift(right, rights, []), shift(left, [], lefts)), (token, token_left)

    def den_term(wanted, senders, sums, after):
        parts = [(den_kept, den_got)]
        return block_term(layout, width, wanted, senders, meta, foot_start, parts, sums, after=after)

    den_sums, den_values = along_places(1, den_term, (), ())
    *num_sent, token = smooth(layout.sent_block, sent, [*den_ends, *den_middle], after=den_values)
    other = asked(gathered, bits[0])
    num_sent = held_until(num_sent, [other, got_middle[0]])
    num_got = swapped(num_sent[:quarter])
    num_got += swapped(held_until(num_sent[quarter:], num_got))
    gathered = joined(gathered, other, bits[0])
    scalars = pl.BlockSpec(memory_space=pltpu.SMEM)
    vmem = pl.BlockSpec(memory_space=pltpu.VMEM)
    moments = pl.pallas_call(
        functools.partial(moments_kernel, held, sky_count),
        in_specs=[scalars, vmem],
        out_shape=jax.ShapeDtypeStruct((16, 5 * SIDE), F32),
        compiler_params=pltpu.CompilerParams(vmem_limit_bytes=SOME),
        cost_estimate=SMALL,
        name="pair_moments",
    )(meta, gathered)
    den_sums, den_values = along_places(2, den_term, den_sums, [token, moments])
    num_kept, token = smooth(layout.kept_block, [(i, True) for i in range(places)], [den_kept], after=den_values)
    bit = 1
    while bit < sky_count:
        moments = moments + lax.ppermute(moments, "sky", [(i, i ^ bit) for i in range(sky_count)])
        (moments,) = held_until([moments], den_values if bit == 1 else [token])
        bit *= 2
    offsets, back = pl.pallas_call(
        functools.partial(solve_kernel, width),
        in_specs=[scalars, scalars, vmem, vmem],
        out_shape=[jax.ShapeDtypeStruct((exposures, 9), F32), jax.ShapeDtypeStruct((8, cols), F32)],
        compiler_params=pltpu.CompilerParams(vmem_limit_bytes=SOME),
        cost_estimate=SMALL,
        name="offsets",
    )(meta, foot_start, moments, pair_owner)

    tables = (jnp.asarray(filtered_rows(rows * sky_count)), back)
    parts = [(den_kept, den_got), (num_kept, num_got)]

    def num_term(wanted, senders, sums, after):
        return block_term(
            layout, width, wanted, senders, meta, foot_start, parts, sums, tables, after
        )

    num_sums, num_values = along_places(1, num_term, (), den_values)
    for step in range(3, places):
        den_sums, den_values = along_places(step, den_term, den_sums, num_values)
        num_sums, num_values = along_places(step - 1, num_term, num_sums, den_values)

    ahead = [*num_values, arrived(den_sums)]
    terms = []
    for wanted, senders in ((to_right(places - 1), range(places - 1)), (to_left(places - 1), range(1, places))):
        value, token = num_term(wanted, senders, (), ahead)
        terms.append(value)
        ahead = [token]
    rightward = shift(terms[0] + num_sums[0], range(places - 1), [])
    leftward = shift(terms[1] + num_sums[1], [], range(1, places))
    own_den, token = den_term(lambda z: z, range(places), den_sums, ahead)
    own_num, _ = num_term(lambda z: z, range(places), (), [token])
    coadd = (own_num + rightward + leftward) / (PRIOR + own_den)
    return (coadd, offsets)


def solution(mesh):
    placed = (P("exp", "sky", None), P("exp", "sky", None), P("exp", "sky", None), P(), P())
    return jax.shard_map(
        per_device, mesh=mesh, in_specs=placed, out_specs=(P("sky", "exp"), P()), check_vma=False
    )
```

```python
import functools

import jax
import jax.numpy as jnp
import numpy as np
from jax import lax
from jax.experimental import pallas as pl
from jax.experimental.pallas import tpu as pltpu
from jax.sharding import PartitionSpec as P

BIN = 16
RADIUS = 10
HALO = 16
SIDE = 128
TOKEN = (8, 128)
TILE = 256
CHUNK = 64

HIGH = lax.Precision.HIGHEST
LAMBDA_REG = 0.25
PRIOR = 1.0
VMEM = 127 * 512 * 1024
SOME = 24 * 1024 * 1024
BF16 = jnp.bfloat16
F32 = jnp.float32
SMALL = pl.CostEstimate(flops=1000, bytes_accessed=1000, transcendentals=0)


def tap_values():
    offs = np.arange(-RADIUS, RADIUS + 1).astype(np.float64)
    taps = np.exp(-offs * offs / 50.0)
    return taps / taps.sum()


def band(out, width, lead):
    taps = tap_values()
    full = np.zeros((out, width), np.float64)
    for shift in range(-RADIUS, RADIUS + 1):
        rows = np.arange(out)
        full[rows, rows + lead + shift] = taps[shift + RADIUS]
    return full


def centers(index, total):
    return (2.0 * index.astype(F32) + 1.0) / total - 1.0


def split_high_low(value):
    high = value.astype(BF16)
    return high, (value - high.astype(F32)).astype(BF16)


def mm(left, right):
    return jnp.dot(left, right, preferred_element_type=F32)


def choose(condition, left, right):
    if isinstance(condition, (bool, np.bool_)):
        return left if condition else right
    return jnp.where(condition, left, right)


class Places:
    def __init__(self, exposures, cols):
        self.share = cols // exposures
        self.places = exposures // 2
        self.quarter = self.places // 4
        self.ends = 2 * self.quarter
        self.middle = self.places - self.ends

    def place_of(self, at, place):
        down = place < self.places // 2
        pair = at // 2
        end = choose(down, self.quarter - 1 - pair, pair) + (at % 2) * (self.places - self.quarter)
        turn = at - self.ends
        mid = choose(down, self.places - self.quarter - 1 - turn, self.quarter + turn)
        return choose(at < self.ends, end, mid)

    def position_of(self, wanted, place):
        down = place < self.places // 2
        right = wanted >= self.places - self.quarter
        low = choose(right, wanted - (self.places - self.quarter), wanted)
        pair = choose(down, self.quarter - 1 - low, low)
        turn = choose(down, self.places - self.quarter - 1 - wanted, wanted - self.quarter)
        is_end = right | (wanted < self.quarter)
        at = choose(is_end, 2 * pair + choose(right, 1, 0), self.ends + turn)
        return at, choose(is_end, pair, self.quarter + turn)

    def sent_block(self, at, meta):
        return 2 * self.place_of(at, meta[0] // 2) + 1 - meta[0] % 2

    def kept_block(self, at, meta):
        return 2 * self.place_of(at, meta[0] // 2) + meta[0] % 2


def inside(col, start, width):
    return (col >= start * BIN) & (col < start * BIN + width)


def columns(block, share, width=None, lead=0):
    return lax.broadcasted_iota(jnp.int32, (1, width or share), 1) + (block * share - lead)


def reciprocal(value):
    rough = pl.reciprocal(value, approx=True)
    rough = rough * (2.0 - value * rough)
    return rough * (2.0 - value * rough)


def expanded(kept, rows):
    return jnp.broadcast_to(kept[:, None, :], (kept.shape[0], BIN, kept.shape[1])).reshape(rows, kept.shape[1])


def folded_kernel(layout, width, meta_ref, start_ref, spread_ref, mask_ref, out_ref, scatter):
    step = pl.program_id(0)
    block = layout.sent_block(step, meta_ref)
    rows, share = spread_ref.shape
    bins_col = mask_ref.shape[1]
    per = share // BIN

    @pl.when(step == 0)
    def _():
        cell = lax.broadcasted_iota(jnp.int32, (SIDE, share), 1) >> 4
        scatter[...] = (cell == lax.broadcasted_iota(jnp.int32, (SIDE, share), 0)).astype(BF16)

    blocks_here = pltpu.roll(mask_ref[...].astype(F32), lax.rem(bins_col - block * per, bins_col), 1)[:, :SIDE]
    kept = mm(blocks_here.astype(BF16), scatter[...])
    kept = jnp.where(inside(columns(block, share), start_ref[meta_ref[0]], width), kept, 0.0)
    for top in range(0, rows, CHUNK):
        here = slice(top, top + CHUNK)
        weight = reciprocal(spread_ref[here]) * expanded(kept[top // BIN : (top + CHUNK) // BIN], CHUNK)
        out_ref[0, here] = jnp.where(step % 2 == 0, weight, out_ref[0, here] + weight)


def weights_kernel(layout, width, meta_ref, start_ref, frame_ref, spread_ref, mask_ref, *refs):
    *outs, kept_ref, bins_ref, scatter, gather, kept_mask, inverse_ref = refs[:-5]
    splits = refs[-5:]
    share = layout.share
    blocks = 2 * layout.places
    rows, cols = spread_ref.shape
    bins_row, bins_col = mask_ref.shape
    per = share // BIN
    start = start_ref[meta_ref[0]]
    half = SIDE * BIN

    @pl.when(pl.program_id(0) == 0)
    def _():
        cell = lax.broadcasted_iota(jnp.int32, (SIDE, half), 1) >> 4
        scatter[...] = (cell == lax.broadcasted_iota(jnp.int32, (SIDE, half), 0)).astype(BF16)
        cell = lax.broadcasted_iota(jnp.int32, (share, SIDE), 0) >> 4
        gather[...] = (cell == lax.broadcasted_iota(jnp.int32, (share, SIDE), 1)).astype(BF16)

    mask = mask_ref[...].astype(F32)
    for part in range(bins_col // SIDE):
        here = slice(part * half, (part + 1) * half)
        kept = mm(mask[:, part * SIDE : (part + 1) * SIDE].astype(BF16), scatter[...])
        kept_mask[:, here] = jnp.where(inside(columns(part, half), start, width), kept, 0.0)
    tall = rows // 2
    for block in range(blocks):
        here = slice(block * share, (block + 1) * share)
        inverse = reciprocal(spread_ref[:, here])
        inverse_ref[:, here] = inverse
        for value, parts in ((frame_ref[:, here], splits[:3]), (inverse, splits[3:])):
            value = value.reshape(bins_row, 2, 8, share).sum(axis=1).reshape(tall, share)
            for split in parts:
                rounded = value.astype(BF16)
                split[block * tall : (block + 1) * tall] = rounded
                value = value - rounded.astype(F32)

    def block_weights(block):
        here = pl.ds(pl.multiple_of(block * share, share), share)
        return inverse_ref[:, here] * expanded(kept_mask[:, here], rows)

    for at, out in enumerate(outs):
        out[...] = block_weights(layout.sent_block(at + layout.ends, meta_ref))
    for at in range(layout.places):
        kept_ref[at] = block_weights(layout.kept_block(at, meta_ref))

    def binned(parts):
        sums = mm(parts[0][...], gather[...])
        for split in parts[1:]:
            sums = sums + mm(split[...], gather[...])
        sums = sums.reshape(blocks * bins_row, 8, SIDE).sum(axis=1)
        halves = []
        for part in range(bins_col // SIDE):
            group = SIDE // per
            halves.append(
                sum(
                    pltpu.roll(sums[block * bins_row : (block + 1) * bins_row], (block % group) * per, 1)
                    for block in range(part * group, (part + 1) * group)
                )
            )
        return jnp.concatenate(halves, axis=1)

    cell = lax.broadcasted_iota(jnp.int32, (1, bins_col), 1) * BIN
    bins_ref[0, 0] = binned(splits[:3]) / (BIN * BIN)
    bins_ref[0, 1] = binned(splits[3:]) * jnp.where(inside(cell, start, width), mask, 0.0)


ANY = pl.BlockSpec(memory_space=pl.ANY)


def whole(shape):
    return pl.BlockSpec(shape, lambda *_: (0,) * len(shape))


def folded_weights(layout, width, meta, starts, spread, mask):
    rows, share = spread.shape[0], layout.share
    out = pl.pallas_call(
        functools.partial(folded_kernel, layout, width),
        grid_spec=pltpu.PrefetchScalarGridSpec(
            num_scalar_prefetch=2,
            grid=(layout.ends,),
            in_specs=[
                pl.BlockSpec((rows, share), lambda i, meta, starts: (0, layout.sent_block(i, meta))),
                whole(mask.shape),
            ],
            out_specs=pl.BlockSpec((1, rows, share), lambda i, meta, starts: (i // 2, 0, 0)),
            scratch_shapes=[pltpu.VMEM((SIDE, share), BF16)],
        ),
        out_shape=pltpu.HBM((layout.quarter, rows, share), F32),
        compiler_params=pltpu.CompilerParams(vmem_limit_bytes=VMEM),
        cost_estimate=SMALL,
        name="folded_weights",
    )(meta, starts, spread, mask)
    return [out.reshape(rows, share)] if layout.quarter == 1 else [out[k] for k in range(layout.quarter)]


def pixel_weights(layout, width, meta, starts, frame, spread, mask, after):
    rows, cols = spread.shape
    bins_row, bins_col = mask.shape
    share, places = layout.share, layout.places
    tall = min(SIDE, rows)
    tile = pl.BlockSpec((tall, cols), lambda i, meta, starts: (i, 0))
    kernel = functools.partial(weights_kernel, layout, width)
    return pl.pallas_call(
        lambda *refs: kernel(*refs[:5], *refs[5 + len(after) :]),
        grid_spec=pltpu.PrefetchScalarGridSpec(
            num_scalar_prefetch=2,
            grid=(rows // tall,),
            in_specs=[tile, tile, pl.BlockSpec((tall // BIN, bins_col), lambda i, meta, starts: (i, 0))]
            + [ANY] * len(after),
            out_specs=[pl.BlockSpec((tall, share), lambda i, meta, starts: (i, 0))] * layout.middle
            + [
                pl.BlockSpec((places, tall, share), lambda i, meta, starts: (0, i, 0)),
                pl.BlockSpec((1, 2, tall // BIN, bins_col), lambda i, meta, starts: (0, 0, i, 0)),
            ],
            scratch_shapes=[
                pltpu.VMEM((SIDE, SIDE * BIN), BF16),
                pltpu.VMEM((share, SIDE), BF16),
                pltpu.VMEM((tall // BIN, cols), F32),
                pltpu.VMEM((tall, cols), F32),
            ]
            + [pltpu.VMEM((2 * places * tall // 2, share), BF16)] * 5,
        ),
        out_shape=[pltpu.HBM((rows, share), F32)] * layout.middle
        + [pltpu.HBM((places, rows, share), F32), jax.ShapeDtypeStruct((1, 2, bins_row, bins_col), F32)],
        compiler_params=pltpu.CompilerParams(vmem_limit_bytes=VMEM),
        cost_estimate=SMALL,
        name="pixel_weights",
    )(meta, starts, frame, spread, mask, *after)


def smooth_kernel(block_of, plan, width, stacked, meta_ref, start_ref, *refs):
    step = pl.program_id(0)
    images, bands, scratch = refs[:9], refs[9:13], refs[-8:]
    refs = refs[13:-8]
    *refs, token_ref = refs
    token_ref[...] = jnp.zeros_like(token_ref)
    weights, outs = refs[: len(refs) // 2], refs[len(refs) // 2 :]

    @pl.when(step == 0)
    def _():
        for k, matrix in enumerate(bands):
            scratch[2 * k][...], scratch[2 * k + 1][...] = split_high_low(matrix[...])

    col_hi, col_lo, row_hi, row_lo, up_hi, up_lo, down_hi, down_lo = scratch
    block = block_of(step, meta_ref)
    start = start_ref[meta_ref[0]]
    rows, share = images[4].shape
    window = share + 2 * SIDE
    field = jnp.concatenate(
        [jnp.concatenate([images[3 * i + j][...] for j in range(3)], axis=1) for i in range(3)], axis=0
    )
    field = jnp.where(inside(columns(block, share, window, SIDE), start, width), field, 0.0)
    high, low = split_high_low(field)

    def three(a_hi, a_lo, b_hi, b_lo):
        return mm(a_hi, b_hi) + (mm(a_lo, b_hi) + mm(a_hi, b_lo))

    tiles = []
    for tile in range(share // TILE):
        lanes = slice(tile * TILE, (tile + 1) * TILE + 2 * SIDE)
        tiles.append(three(high[:, lanes], low[:, lanes], col_hi[...], col_lo[...]))
    across = tiles[0] if len(tiles) == 1 else jnp.concatenate(tiles, axis=1)
    high, low = split_high_low(across)
    height = row_hi.shape[0]
    tiles = []
    for tile in range(rows // height):
        top = tile * height
        mid = slice(top + HALO, top + HALO + height)
        upper = slice(top, top + HALO)
        lower = slice(top + HALO + height, top + 2 * HALO + height)
        main = three(row_hi[...], row_lo[...], high[mid], low[mid])
        tiles += [
            main[:HALO] + three(up_hi[...], up_lo[...], high[upper], low[upper]),
            main[HALO : height - HALO],
            main[height - HALO :] + three(down_hi[...], down_lo[...], high[lower], low[lower]),
        ]
    smoothed = jnp.concatenate(tiles, axis=0)
    smoothed = jnp.where(inside(columns(block, share), start, width), smoothed, 0.0)
    if stacked:
        outs[0][0] = weights[0][0] * smoothed
        return
    for at, (out, fresh) in enumerate(plan):
        @pl.when(step == at)
        def _(out=out, fresh=fresh):
            term = weights[out][...] * smoothed
            outs[out][...] = term if fresh else outs[out][...] + term


def smoothed_terms(block_of, plan, weights, meta, starts, frame, above, below, share, width, after=()):
    rows, cols = frame.shape
    stacked = weights[0].ndim == 3
    count = len(weights)
    per = share // SIDE
    last = cols // SIDE - 1
    specs = []
    for height in (HALO, rows, HALO):
        specs += [
            pl.BlockSpec((height, SIDE), lambda i, m, s: (0, jnp.maximum(block_of(i, m) * per - 1, 0))),
            pl.BlockSpec((height, share), lambda i, m, s: (0, block_of(i, m))),
            pl.BlockSpec((height, SIDE), lambda i, m, s: (0, jnp.minimum(block_of(i, m) * per + per, last))),
        ]
    if stacked:
        parts_spec = pl.BlockSpec((1, rows, share), lambda i, m, s: (i, 0, 0))
    else:
        parts_spec = whole((rows, share))
    height = min(TILE, rows)
    full = band(height, height + 2 * HALO, HALO)
    bands = [
        band(TILE, TILE + 2 * SIDE, SIDE).T,
        full[:, HALO : HALO + height],
        full[:HALO, :HALO],
        full[height - HALO :, HALO + height :],
    ]
    parts = [jnp.asarray(matrix.astype(np.float32)) for matrix in bands]

    def body(*refs):
        lead = 2 + 9 + len(parts) + count
        smooth_kernel(block_of, plan, width, stacked, *refs[:lead], *refs[lead + len(after) :])

    return pl.pallas_call(
        body,
        grid_spec=pltpu.PrefetchScalarGridSpec(
            num_scalar_prefetch=2,
            grid=(len(plan),),
            in_specs=specs + [whole(p.shape) for p in parts] + [parts_spec] * count + [ANY] * len(after),
            out_specs=[parts_spec] * count + [whole(TOKEN)],
            scratch_shapes=[pltpu.VMEM(p.shape, BF16) for p in parts for _ in range(2)],
        ),
        out_shape=[pltpu.HBM(w.shape, F32) for w in weights] + [jax.ShapeDtypeStruct(TOKEN, F32)],
        compiler_params=pltpu.CompilerParams(vmem_limit_bytes=VMEM),
        cost_estimate=SMALL,
        name="smoothed_terms",
    )(meta, starts, *([above] * 3 + [frame] * 3 + [below] * 3), *parts, *weights, *after)


def term_kernel(layout, width, wanted, units, received, numerator, meta_ref, start_ref, *refs):
    place = meta_ref[0] // 2
    block = 2 * wanted(place) + meta_ref[0] % 2
    _, unit = layout.position_of(wanted(place), place)
    mate_start = start_ref[meta_ref[0] + 1 - 2 * (meta_ref[0] % 2)]
    in_mate = inside(columns(block, layout.share), mate_start, width)
    *refs, out_ref, token_ref = refs
    token_ref[...] = jnp.zeros_like(token_ref)

    def pair():
        own = refs.pop(0)[0]
        got = refs.pop(0)[...]
        for u in units[1:]:
            got = jnp.where(unit == u, refs.pop(0)[...], got)
        return own, got

    def added(own, got, names):
        value = own + jnp.where(in_mate, got, 0.0)
        for _ in range(names):
            value = value + refs.pop(0)[...]
        return value

    if not numerator:
        out_ref[...] = added(*pair(), received)
        return
    own_den, mate_den = pair()
    own, mate = pair()
    rows_part, back = refs.pop(0)[...], refs.pop(0)[...]
    own_back = sum(rows_part[:, u : u + 1] * back[u : u + 1, :] for u in range(3))
    mate_back = sum(rows_part[:, u : u + 1] * back[3 + u : 4 + u, :] for u in range(3))
    top = added(own - own_den * own_back, mate - mate_den * mate_back, received)
    out_ref[...] = top


def block_term(layout, width, wanted, senders, meta, starts, parts, received, tables=(), after=()):
    kept = parts[0][0]
    rows, share = kept.shape[1:]
    chunk = min(TILE, rows)

    def at_unit(place):
        return layout.position_of(wanted(place), place)

    units = sorted({int(at_unit(z)[1]) for z in senders})
    flat = pl.BlockSpec((chunk, share), lambda r, m, s: (r, 0))
    specs, args = [], []
    for own, got in parts:
        specs.append(pl.BlockSpec((1, chunk, share), lambda r, m, s: (at_unit(m[0] // 2)[0], r, 0)))
        args.append(pltpu.with_memory_space_constraint(own, pltpu.HBM))
        for u in units:
            specs.append(
                flat
                if len(units) == 1
                else pl.BlockSpec(
                    (chunk, share), lambda r, m, s, u=u: (jnp.where(at_unit(m[0] // 2)[1] == u, r, 0), 0)
                )
            )
            args.append(got[u])
    if tables:
        rows_part, back = tables
        strips = rows // chunk
        specs.append(pl.BlockSpec((chunk, rows_part.shape[1]), lambda r, m, s: (m[1] * strips + r, 0)))
        specs.append(
            pl.BlockSpec((back.shape[0], share), lambda r, m, s: (0, 2 * wanted(m[0] // 2) + m[0] % 2))
        )
        args += [rows_part, back]
    specs += [flat] * len(received)
    args += list(received)
    lead = 2 + len(args)
    body = functools.partial(term_kernel, layout, width, wanted, units, len(received), bool(tables))
    return pl.pallas_call(
        lambda *refs: body(*refs[:lead], *refs[-2:]),
        grid_spec=pltpu.PrefetchScalarGridSpec(
            num_scalar_prefetch=2, grid=(rows // chunk,), in_specs=specs + [ANY] * len(after), out_specs=[flat, whole(TOKEN)]
        ),
        out_shape=[jax.ShapeDtypeStruct((rows, share), F32), jax.ShapeDtypeStruct(TOKEN, F32)],
        compiler_params=pltpu.CompilerParams(vmem_limit_bytes=SOME),
        cost_estimate=SMALL,
        name="block_term",
    )(meta, starts, *args, *after)


def held_until(values, after):
    def body(*refs):
        del refs

    return pl.pallas_call(
        body,
        in_specs=[ANY] * (len(values) + len(after)),
        out_specs=[ANY] * len(values),
        out_shape=[jax.ShapeDtypeStruct(v.shape, v.dtype) for v in values],
        input_output_aliases={i: i for i in range(len(values))},
        compiler_params=pltpu.CompilerParams(vmem_limit_bytes=VMEM),
        cost_estimate=SMALL,
        name="held",
    )(*values, *after)


def arrived(values):
    def body(*refs):
        refs[-1][...] = jnp.zeros_like(refs[-1])

    return pl.pallas_call(
        body,
        in_specs=[ANY] * len(values),
        out_shape=jax.ShapeDtypeStruct(TOKEN, F32),
        compiler_params=pltpu.CompilerParams(vmem_limit_bytes=SOME),
        cost_estimate=pl.CostEstimate(flops=1000, bytes_accessed=8 * 10**6, transcendentals=0),
        name="arrived",
    )(*values)


def contract_last(left, right):
    return lax.dot_general(left, right, (((1,), (1,)), ((), ())), precision=HIGH, preferred_element_type=F32)


def contract_last_three(left, right):
    def one(a, b):
        return lax.dot_general(a, b, (((1,), (1,)), ((), ())), preferred_element_type=F32)

    (l_hi, l_lo), (r_hi, r_lo) = split_high_low(left), split_high_low(right)
    return one(l_hi, r_hi) + (one(l_lo, r_hi) + one(l_hi, r_lo))


def moments_kernel(places, strips, meta_ref, bins_ref, out_ref):
    count, _, rows, cols = bins_ref.shape
    at = [places.index(e) for e in range(count)]
    image = [bins_ref[at[e], 0] for e in range(count)]
    weight = [bins_ref[at[e], 1] for e in range(count)]
    x = centers(lax.broadcasted_iota(jnp.int32, (1, cols), 1), cols)
    tx = [jnp.ones_like(x), x]
    while len(tx) < 5:
        tx.append(2.0 * x * tx[-1] - tx[-2])
    tx = jnp.concatenate(tx + [jnp.zeros((3, cols), F32)], axis=0)
    joint, diffs = [], []
    for apart in range(1, count // 2 + 1):
        group, group_d = [], []
        for i in range(count):
            j = (i + apart) % count
            w = weight[i] * weight[j] / (weight[i] + weight[j] + 1.0)
            group.append(w)
            group_d.append(w * (image[i] - image[j]))
        joint.append(contract_last_three(tx, jnp.concatenate(group, axis=0)))
        diffs.append(contract_last_three(tx, jnp.concatenate(group_d, axis=0)))
    along = jnp.concatenate([jnp.concatenate(joint, axis=1), jnp.concatenate(diffs, axis=1)], axis=0)
    total = along.shape[1]
    row = lax.broadcasted_iota(jnp.int32, (total, SIDE), 0)
    lane = lax.broadcasted_iota(jnp.int32, (total, SIDE), 1)
    mine = row // rows == lane
    y = centers(row % rows + meta_ref[1] * rows, rows * strips)
    a_hi, a_lo = split_high_low(along)
    ty = [jnp.ones_like(y), y]
    for a in range(5):
        if a > 1:
            ty.append(2.0 * y * ty[-1] - ty[-2])
        b_hi, b_lo = split_high_low(jnp.where(mine, ty[a], 0.0))
        out_ref[:, a * SIDE : (a + 1) * SIDE] = mm(a_hi, b_hi) + (mm(a_lo, b_hi) + mm(a_hi, b_lo))


def solve_kernel(width, meta_ref, start_ref, moments_ref, owner_ref, out_ref, back_ref):
    owner = owner_ref[...].astype(F32)
    count = owner.shape[0]
    lanes = count * count // 2
    exposure = lax.broadcasted_iota(jnp.int32, (count, lanes), 0)
    lane = lax.broadcasted_iota(jnp.int32, (count, lanes), 1)
    mine = lane % count
    apart = lane // count + 1
    is_i = (exposure == mine).astype(F32)
    is_j = (exposure == (mine + apart) % count).astype(F32)
    both = owner + owner.T
    listed = jnp.sum(is_i * jnp.dot(both, is_j, precision=HIGH, preferred_element_type=F32), axis=0, keepdims=True)
    lane_row = lax.broadcasted_iota(jnp.int32, (1, lanes), 1)
    once = (lane_row // count + 1 < count // 2) | (lane_row % count < count // 2)
    listed = jnp.where(once, listed, 0.0)
    held = listed > 0.0
    moment = [[moments_ref[b : b + 1, a * SIDE : a * SIDE + lanes] for b in range(5)] for a in range(5)]

    def entry(k, l):
        (u, v), (s, t) = divmod(k, 3), divmod(l, 3)
        total = 0.0
        for a in (u + s, abs(u - s)):
            for b in (v + t, abs(v - t)):
                total = total + moment[a][b]
        return jnp.where(held, 0.25 * total, 1.0 if k == l else 0.0)

    factor = [[None] * 9 for _ in range(9)]
    scale = [None] * 9
    for k in range(9):
        for l in range(k, 9):
            value = entry(l, k)
            for m in range(k):
                value = value - factor[l][m] * factor[k][m]
            if l == k:
                scale[k] = 1.0 / jnp.sqrt(value)
            else:
                factor[l][k] = value * scale[k]
    half = [None] * 9
    for k in range(9):
        a, b = divmod(k, 3)
        value = moments_ref[8 + b : 9 + b, a * SIDE : a * SIDE + lanes]
        for m in range(k):
            value = value - factor[k][m] * half[m]
        half[k] = value * scale[k]
    fit = [None] * 9
    for k in reversed(range(9)):
        value = half[k]
        for m in range(k + 1, 9):
            value = value - factor[m][k] * fit[m]
        fit[k] = value * scale[k]
    fits = jnp.concatenate([jnp.where(held, f, 0.0) for f in fit] + [jnp.zeros((7, lanes), F32)], axis=0)
    right = contract_last((is_i - is_j) * listed, fits)
    row = lax.broadcasted_iota(jnp.int32, (count, count), 0)
    column = lax.broadcasted_iota(jnp.int32, (count, count), 1)
    degree = jnp.sum(both, axis=1, keepdims=True) + LAMBDA_REG
    system = jnp.where(row == column, degree, 0.0) - both
    for k in range(count):
        inverse = 1.0 / system[k : k + 1, k : k + 1]
        pivot_s, pivot_r = system[k : k + 1, :] * inverse, right[k : k + 1, :] * inverse
        lead = system[:, k : k + 1]
        chosen = row[:, :1] == k
        system = jnp.where(chosen, pivot_s, system - lead * pivot_s)
        right = jnp.where(chosen, pivot_r, right - lead * pivot_r)
    out_ref[...] = right[:, :9]
    member = meta_ref[0]
    mate = member + 1 - 2 * (member % 2)
    cols = back_ref.shape[1]
    padded = cols + 2 * SIDE
    col = lax.broadcasted_iota(jnp.int32, (1, padded), 1) - SIDE
    x = centers(col, cols)
    terms = [jnp.ones_like(x), x, 2.0 * x * x - 1.0]
    fields = [jnp.where(inside(col, start_ref[e], width), t, 0.0) for e in (member, mate) for t in terms]
    fields = jnp.concatenate(fields + [jnp.zeros((2, padded), F32)], axis=0)
    taps = tap_values()
    total = float(taps[RADIUS]) * fields
    for shift in range(1, RADIUS + 1):
        both = pltpu.roll(fields, shift, 1) + pltpu.roll(fields, padded - shift, 1)
        total = total + float(taps[RADIUS + shift]) * both
    total = total[:, SIDE : SIDE + cols]
    rows = lax.broadcasted_iota(jnp.int32, (count, 16), 0)
    for k, which in enumerate((member, mate)):
        mine = jnp.sum(jnp.where(rows == which, right, 0.0), axis=0, keepdims=True)
        for u in range(3):
            back_ref[3 * k + u : 3 * k + u + 1, :] = sum(
                mine[:, 3 * u + v : 3 * u + v + 1] * total[3 * k + v : 3 * k + v + 1, :] for v in range(3)
            )
    back_ref[6:8, :] = jnp.zeros((2, cols), F32)


def filtered_rows(total_rows):
    y = (2.0 * np.arange(total_rows) + 1.0) / total_rows - 1.0
    terms = np.stack([np.ones_like(y), y, 2.0 * y * y - 1.0])
    padded = np.pad(terms, ((0, 0), (RADIUS, RADIUS)))
    taps = tap_values()
    return sum(taps[t] * padded[:, t : t + total_rows] for t in range(2 * RADIUS + 1)).T.astype(np.float32)


def per_device(image, variance, mask, foot_start, pair_owner):
    frame, spread, blocks = image[0], variance[0], mask[0]
    rows, cols = frame.shape
    exposures, sky_count = lax.axis_size("exp"), lax.axis_size("sky")
    member = lax.axis_index("exp")
    meta = jnp.stack([member, lax.axis_index("sky")])
    width = 3 * cols // 4
    layout = Places(exposures, cols)
    share, places, quarter = layout.share, layout.places, layout.quarter
    ends, middle_count = layout.ends, layout.middle
    sent = [(i // 2, i % 2 == 0) for i in range(ends)] + [(quarter + i, True) for i in range(middle_count)]
    swap = [(i, i ^ 1) for i in range(exposures)]

    def swapped(parts):
        return [lax.ppermute(part, "exp", swap) for part in parts]

    den_ends = folded_weights(layout, width, meta, foot_start, spread, blocks)
    *den_middle, den_kept, gathered = pixel_weights(
        layout, width, meta, foot_start, frame, spread, blocks, den_ends
    )
    got_ends = swapped(den_ends)
    got_middle = swapped(den_middle)
    den_got = got_ends + got_middle

    up = [(i, i + 1) for i in range(sky_count - 1)]
    down = [(j, i) for i, j in up]
    above = lax.ppermute(frame[rows - HALO :], "sky", up)
    below = lax.ppermute(frame[:HALO], "sky", down)
    smooth = functools.partial(
        smoothed_terms, meta=meta, starts=foot_start, frame=frame, above=above, below=below, share=share, width=width
    )

    held = [0]
    bits = [1 << k for k in range(exposures.bit_length() - 1)]

    def asked(gathered, bit):
        return lax.ppermute(gathered, "exp", [(i, i ^ bit) for i in range(exposures)])

    def joined(gathered, other, bit):
        low = (member & bit) == 0
        held.extend([e | bit for e in held])
        return jnp.concatenate([jnp.where(low, gathered, other), jnp.where(low, other, gathered)])

    def to_right(step):
        return lambda z: choose(z < step, z + places - step, places - 1)

    def to_left(step):
        return lambda z: choose(z >= places - step, z - places + step, 0)

    def outward(step):
        return lambda z: choose(z < places // 2, to_right(step)(z), to_left(step)(z))

    def shift(value, rights, lefts):
        pairs = [(2 * z + s, 2 * z + 2 + s) for z in rights for s in range(2)]
        pairs += [(2 * z + s, 2 * z - 2 + s) for z in lefts for s in range(2)]
        return lax.ppermute(value, "exp", pairs)

    def along_places(step, term, sums, after):
        rights, lefts = range(step), range(places - step, places)
        if step <= places // 2:
            value, token = term(outward(step), [*rights, *lefts], sums, after)
            if step < places // 2:
                return (shift(value, rights, lefts),), (token,)
            return (shift(value, rights, []), shift(value, [], lefts)), (token,)
        right, token = term(to_right(step), rights, sums[:1], after)
        left, token_left = term(to_left(step), lefts, sums[1:], after)
        return (shift(right, rights, []), shift(left, [], lefts)), (token, token_left)

    def den_term(wanted, senders, sums, after):
        parts = [(den_kept, den_got)]
        return block_term(layout, width, wanted, senders, meta, foot_start, parts, sums, after=after)

    gathered = joined(gathered, asked(gathered, bits[1]), bits[1])
    den_sums, den_values = along_places(1, den_term, (), ())
    (gathered,) = held_until([gathered], [*den_values, above, below])
    for bit in bits[2:-1]:
        gathered = joined(gathered, asked(gathered, bit), bit)
    other = asked(gathered, bits[-1])
    *num_sent, token = smooth(layout.sent_block, sent, [*den_ends, *den_middle], after=den_values)
    (other,) = held_until([other], [token])
    gathered = joined(gathered, other, bits[-1])
    other = asked(gathered, bits[0])
    den_sums, den_values = along_places(2, den_term, den_sums, [token])
    num_sent = held_until(num_sent, [other, *den_values])
    num_got = swapped(num_sent[:quarter])
    num_got += swapped(held_until(num_sent[quarter:], num_got))
    (gathered,) = held_until([joined(gathered, other, bits[0])], den_values)
    scalars = pl.BlockSpec(memory_space=pltpu.SMEM)
    vmem = pl.BlockSpec(memory_space=pltpu.VMEM)
    moments = pl.pallas_call(
        functools.partial(moments_kernel, held, sky_count),
        in_specs=[scalars, vmem],
        out_shape=jax.ShapeDtypeStruct((16, 5 * SIDE), F32),
        compiler_params=pltpu.CompilerParams(vmem_limit_bytes=SOME),
        cost_estimate=SMALL,
        name="pair_moments",
    )(meta, gathered)
    num_kept, token = smooth(layout.kept_block, [(i, True) for i in range(places)], [den_kept], after=den_values)
    bit = 1
    while bit < sky_count:
        moments = moments + lax.ppermute(moments, "sky", [(i, i ^ bit) for i in range(sky_count)])
        (moments,) = held_until([moments], den_values if bit == 1 else [token])
        bit *= 2
    offsets, back = pl.pallas_call(
        functools.partial(solve_kernel, width),
        in_specs=[scalars, scalars, vmem, vmem],
        out_shape=[jax.ShapeDtypeStruct((exposures, 9), F32), jax.ShapeDtypeStruct((8, cols), F32)],
        compiler_params=pltpu.CompilerParams(vmem_limit_bytes=SOME),
        cost_estimate=SMALL,
        name="offsets",
    )(meta, foot_start, moments, pair_owner)

    tables = (jnp.asarray(filtered_rows(rows * sky_count)), back)
    parts = [(den_kept, den_got), (num_kept, num_got)]

    def num_term(wanted, senders, sums, after):
        return block_term(
            layout, width, wanted, senders, meta, foot_start, parts, sums, tables, after
        )

    num_sums, num_values = along_places(1, num_term, (), [arrived(den_sums)])
    for step in range(3, places):
        den_sums, den_values = along_places(step, den_term, den_sums, num_values)
        num_sums, num_values = along_places(step - 1, num_term, num_sums, den_values)

    ahead = [*num_values, arrived(den_sums)]
    terms = []
    for wanted, senders in ((to_right(places - 1), range(places - 1)), (to_left(places - 1), range(1, places))):
        value, token = num_term(wanted, senders, (), ahead)
        terms.append(value)
        ahead = [token]
    rightward = shift(terms[0] + num_sums[0], range(places - 1), [])
    leftward = shift(terms[1] + num_sums[1], [], range(1, places))
    own_den, token = den_term(lambda z: z, range(places), den_sums, ahead)
    own_num, _ = num_term(lambda z: z, range(places), (), [token])
    coadd = (own_num + rightward + leftward) / (PRIOR + own_den)
    return (coadd, offsets)


def solution(mesh):
    placed = (P("exp", "sky", None), P("exp", "sky", None), P("exp", "sky", None), P(), P())
    return jax.shard_map(
        per_device, mesh=mesh, in_specs=placed, out_specs=(P("sky", "exp"), P()), check_vma=False
    )
```

```python
import functools

import jax
import jax.numpy as jnp
import numpy as np
from jax import lax
from jax.experimental import pallas as pl
from jax.experimental.pallas import tpu as pltpu
from jax.sharding import PartitionSpec as P

BIN = 16
RADIUS = 10
HALO = 16
SIDE = 128
TOKEN = (8, 128)
TILE = 256
CHUNK = 64

HIGH = lax.Precision.HIGHEST
LAMBDA_REG = 0.25
PRIOR = 1.0
VMEM = 127 * 512 * 1024
SOME = 24 * 1024 * 1024
BF16 = jnp.bfloat16
F32 = jnp.float32
SMALL = pl.CostEstimate(flops=1000, bytes_accessed=1000, transcendentals=0)


def tap_values():
    offs = np.arange(-RADIUS, RADIUS + 1).astype(np.float64)
    taps = np.exp(-offs * offs / 50.0)
    return taps / taps.sum()


def band(out, width, lead):
    taps = tap_values()
    full = np.zeros((out, width), np.float64)
    for shift in range(-RADIUS, RADIUS + 1):
        rows = np.arange(out)
        full[rows, rows + lead + shift] = taps[shift + RADIUS]
    return full


def centers(index, total):
    return (2.0 * index.astype(F32) + 1.0) / total - 1.0


def split_high_low(value):
    high = value.astype(BF16)
    return high, (value - high.astype(F32)).astype(BF16)


def mm(left, right):
    return jnp.dot(left, right, preferred_element_type=F32)


def choose(condition, left, right):
    if isinstance(condition, (bool, np.bool_)):
        return left if condition else right
    return jnp.where(condition, left, right)


class Places:
    def __init__(self, exposures, cols):
        self.share = cols // exposures
        self.places = exposures // 2
        self.quarter = self.places // 4
        self.ends = 2 * self.quarter
        self.middle = self.places - self.ends

    def place_of(self, at, place):
        down = place < self.places // 2
        pair = at // 2
        end = choose(down, self.quarter - 1 - pair, pair) + (at % 2) * (self.places - self.quarter)
        turn = at - self.ends
        mid = choose(down, self.places - self.quarter - 1 - turn, self.quarter + turn)
        return choose(at < self.ends, end, mid)

    def position_of(self, wanted, place):
        down = place < self.places // 2
        right = wanted >= self.places - self.quarter
        low = choose(right, wanted - (self.places - self.quarter), wanted)
        pair = choose(down, self.quarter - 1 - low, low)
        turn = choose(down, self.places - self.quarter - 1 - wanted, wanted - self.quarter)
        is_end = right | (wanted < self.quarter)
        at = choose(is_end, 2 * pair + choose(right, 1, 0), self.ends + turn)
        return at, choose(is_end, pair, self.quarter + turn)

    def sent_block(self, at, meta):
        return 2 * self.place_of(at, meta[0] // 2) + 1 - meta[0] % 2

    def kept_block(self, at, meta):
        return 2 * self.place_of(at, meta[0] // 2) + meta[0] % 2


def inside(col, start, width):
    return (col >= start * BIN) & (col < start * BIN + width)


def columns(block, share, width=None, lead=0):
    return lax.broadcasted_iota(jnp.int32, (1, width or share), 1) + (block * share - lead)


def reciprocal(value):
    rough = pl.reciprocal(value, approx=True)
    rough = rough * (2.0 - value * rough)
    return rough * (2.0 - value * rough)


def expanded(kept, rows):
    return jnp.broadcast_to(kept[:, None, :], (kept.shape[0], BIN, kept.shape[1])).reshape(rows, kept.shape[1])


def folded_kernel(layout, width, meta_ref, start_ref, spread_ref, mask_ref, out_ref, scatter):
    step = pl.program_id(0)
    block = layout.sent_block(step, meta_ref)
    rows, share = spread_ref.shape
    bins_col = mask_ref.shape[1]
    per = share // BIN

    @pl.when(step == 0)
    def _():
        cell = lax.broadcasted_iota(jnp.int32, (SIDE, share), 1) >> 4
        scatter[...] = (cell == lax.broadcasted_iota(jnp.int32, (SIDE, share), 0)).astype(BF16)

    blocks_here = pltpu.roll(mask_ref[...].astype(F32), lax.rem(bins_col - block * per, bins_col), 1)[:, :SIDE]
    kept = mm(blocks_here.astype(BF16), scatter[...])
    kept = jnp.where(inside(columns(block, share), start_ref[meta_ref[0]], width), kept, 0.0)
    for top in range(0, rows, CHUNK):
        here = slice(top, top + CHUNK)
        weight = reciprocal(spread_ref[here]) * expanded(kept[top // BIN : (top + CHUNK) // BIN], CHUNK)
        out_ref[0, here] = jnp.where(step % 2 == 0, weight, out_ref[0, here] + weight)


def weights_kernel(layout, width, meta_ref, start_ref, frame_ref, spread_ref, mask_ref, *refs):
    *outs, kept_ref, bins_ref, scatter, gather, kept_mask, inverse_ref = refs[:-5]
    splits = refs[-5:]
    share = layout.share
    blocks = 2 * layout.places
    rows, cols = spread_ref.shape
    bins_row, bins_col = mask_ref.shape
    per = share // BIN
    start = start_ref[meta_ref[0]]
    half = SIDE * BIN

    @pl.when(pl.program_id(0) == 0)
    def _():
        cell = lax.broadcasted_iota(jnp.int32, (SIDE, half), 1) >> 4
        scatter[...] = (cell == lax.broadcasted_iota(jnp.int32, (SIDE, half), 0)).astype(BF16)
        cell = lax.broadcasted_iota(jnp.int32, (share, SIDE), 0) >> 4
        gather[...] = (cell == lax.broadcasted_iota(jnp.int32, (share, SIDE), 1)).astype(BF16)

    mask = mask_ref[...].astype(F32)
    for part in range(bins_col // SIDE):
        here = slice(part * half, (part + 1) * half)
        kept = mm(mask[:, part * SIDE : (part + 1) * SIDE].astype(BF16), scatter[...])
        kept_mask[:, here] = jnp.where(inside(columns(part, half), start, width), kept, 0.0)
    tall = rows // 2
    for block in range(blocks):
        here = slice(block * share, (block + 1) * share)
        inverse = reciprocal(spread_ref[:, here])
        inverse_ref[:, here] = inverse
        for value, parts in ((frame_ref[:, here], splits[:3]), (inverse, splits[3:])):
            value = value.reshape(bins_row, 2, 8, share).sum(axis=1).reshape(tall, share)
            for split in parts:
                rounded = value.astype(BF16)
                split[block * tall : (block + 1) * tall] = rounded
                value = value - rounded.astype(F32)

    def block_weights(block):
        here = pl.ds(pl.multiple_of(block * share, share), share)
        return inverse_ref[:, here] * expanded(kept_mask[:, here], rows)

    for at, out in enumerate(outs):
        out[...] = block_weights(layout.sent_block(at + layout.ends, meta_ref))
    for at in range(layout.places):
        kept_ref[at] = block_weights(layout.kept_block(at, meta_ref))

    def binned(parts):
        sums = mm(parts[0][...], gather[...])
        for split in parts[1:]:
            sums = sums + mm(split[...], gather[...])
        sums = sums.reshape(blocks * bins_row, 8, SIDE).sum(axis=1)
        halves = []
        for part in range(bins_col // SIDE):
            group = SIDE // per
            halves.append(
                sum(
                    pltpu.roll(sums[block * bins_row : (block + 1) * bins_row], (block % group) * per, 1)
                    for block in range(part * group, (part + 1) * group)
                )
            )
        return jnp.concatenate(halves, axis=1)

    cell = lax.broadcasted_iota(jnp.int32, (1, bins_col), 1) * BIN
    bins_ref[0, 0] = binned(splits[:3]) / (BIN * BIN)
    bins_ref[0, 1] = binned(splits[3:]) * jnp.where(inside(cell, start, width), mask, 0.0)


ANY = pl.BlockSpec(memory_space=pl.ANY)


def whole(shape):
    return pl.BlockSpec(shape, lambda *_: (0,) * len(shape))


def folded_weights(layout, width, meta, starts, spread, mask):
    rows, share = spread.shape[0], layout.share
    out = pl.pallas_call(
        functools.partial(folded_kernel, layout, width),
        grid_spec=pltpu.PrefetchScalarGridSpec(
            num_scalar_prefetch=2,
            grid=(layout.ends,),
            in_specs=[
                pl.BlockSpec((rows, share), lambda i, meta, starts: (0, layout.sent_block(i, meta))),
                whole(mask.shape),
            ],
            out_specs=pl.BlockSpec((1, rows, share), lambda i, meta, starts: (i // 2, 0, 0)),
            scratch_shapes=[pltpu.VMEM((SIDE, share), BF16)],
        ),
        out_shape=pltpu.HBM((layout.quarter, rows, share), F32),
        compiler_params=pltpu.CompilerParams(vmem_limit_bytes=VMEM),
        cost_estimate=SMALL,
        name="folded_weights",
    )(meta, starts, spread, mask)
    return [out.reshape(rows, share)] if layout.quarter == 1 else [out[k] for k in range(layout.quarter)]


def pixel_weights(layout, width, meta, starts, frame, spread, mask, after):
    rows, cols = spread.shape
    bins_row, bins_col = mask.shape
    share, places = layout.share, layout.places
    tall = min(SIDE, rows)
    tile = pl.BlockSpec((tall, cols), lambda i, meta, starts: (i, 0))
    kernel = functools.partial(weights_kernel, layout, width)
    return pl.pallas_call(
        lambda *refs: kernel(*refs[:5], *refs[5 + len(after) :]),
        grid_spec=pltpu.PrefetchScalarGridSpec(
            num_scalar_prefetch=2,
            grid=(rows // tall,),
            in_specs=[tile, tile, pl.BlockSpec((tall // BIN, bins_col), lambda i, meta, starts: (i, 0))]
            + [ANY] * len(after),
            out_specs=[pl.BlockSpec((tall, share), lambda i, meta, starts: (i, 0))] * layout.middle
            + [
                pl.BlockSpec((places, tall, share), lambda i, meta, starts: (0, i, 0)),
                pl.BlockSpec((1, 2, tall // BIN, bins_col), lambda i, meta, starts: (0, 0, i, 0)),
            ],
            scratch_shapes=[
                pltpu.VMEM((SIDE, SIDE * BIN), BF16),
                pltpu.VMEM((share, SIDE), BF16),
                pltpu.VMEM((tall // BIN, cols), F32),
                pltpu.VMEM((tall, cols), F32),
            ]
            + [pltpu.VMEM((2 * places * tall // 2, share), BF16)] * 5,
        ),
        out_shape=[pltpu.HBM((rows, share), F32)] * layout.middle
        + [pltpu.HBM((places, rows, share), F32), jax.ShapeDtypeStruct((1, 2, bins_row, bins_col), F32)],
        compiler_params=pltpu.CompilerParams(vmem_limit_bytes=VMEM),
        cost_estimate=SMALL,
        name="pixel_weights",
    )(meta, starts, frame, spread, mask, *after)


def smooth_kernel(block_of, plan, width, stacked, meta_ref, start_ref, *refs):
    step = pl.program_id(0)
    images, bands, scratch = refs[:9], refs[9:13], refs[-8:]
    refs = refs[13:-8]
    *refs, token_ref = refs
    token_ref[...] = jnp.zeros_like(token_ref)
    weights, outs = refs[: len(refs) // 2], refs[len(refs) // 2 :]

    @pl.when(step == 0)
    def _():
        for k, matrix in enumerate(bands):
            scratch[2 * k][...], scratch[2 * k + 1][...] = split_high_low(matrix[...])

    col_hi, col_lo, row_hi, row_lo, up_hi, up_lo, down_hi, down_lo = scratch
    block = block_of(step, meta_ref)
    start = start_ref[meta_ref[0]]
    rows, share = images[4].shape
    window = share + 2 * SIDE
    field = jnp.concatenate(
        [jnp.concatenate([images[3 * i + j][...] for j in range(3)], axis=1) for i in range(3)], axis=0
    )
    field = jnp.where(inside(columns(block, share, window, SIDE), start, width), field, 0.0)
    high, low = split_high_low(field)

    def three(a_hi, a_lo, b_hi, b_lo):
        return mm(a_hi, b_hi) + (mm(a_lo, b_hi) + mm(a_hi, b_lo))

    tiles = []
    for tile in range(share // TILE):
        lanes = slice(tile * TILE, (tile + 1) * TILE + 2 * SIDE)
        tiles.append(three(high[:, lanes], low[:, lanes], col_hi[...], col_lo[...]))
    across = tiles[0] if len(tiles) == 1 else jnp.concatenate(tiles, axis=1)
    high, low = split_high_low(across)
    height = row_hi.shape[0]
    tiles = []
    for tile in range(rows // height):
        top = tile * height
        mid = slice(top + HALO, top + HALO + height)
        upper = slice(top, top + HALO)
        lower = slice(top + HALO + height, top + 2 * HALO + height)
        main = three(row_hi[...], row_lo[...], high[mid], low[mid])
        tiles += [
            main[:HALO] + three(up_hi[...], up_lo[...], high[upper], low[upper]),
            main[HALO : height - HALO],
            main[height - HALO :] + three(down_hi[...], down_lo[...], high[lower], low[lower]),
        ]
    smoothed = jnp.concatenate(tiles, axis=0)
    smoothed = jnp.where(inside(columns(block, share), start, width), smoothed, 0.0)
    if stacked:
        outs[0][0] = weights[0][0] * smoothed
        return
    for at, (out, fresh) in enumerate(plan):
        @pl.when(step == at)
        def _(out=out, fresh=fresh):
            term = weights[out][...] * smoothed
            outs[out][...] = term if fresh else outs[out][...] + term


def smoothed_terms(block_of, plan, weights, meta, starts, frame, above, below, share, width, after=()):
    rows, cols = frame.shape
    stacked = weights[0].ndim == 3
    count = len(weights)
    per = share // SIDE
    last = cols // SIDE - 1
    specs = []
    for height in (HALO, rows, HALO):
        specs += [
            pl.BlockSpec((height, SIDE), lambda i, m, s: (0, jnp.maximum(block_of(i, m) * per - 1, 0))),
            pl.BlockSpec((height, share), lambda i, m, s: (0, block_of(i, m))),
            pl.BlockSpec((height, SIDE), lambda i, m, s: (0, jnp.minimum(block_of(i, m) * per + per, last))),
        ]
    if stacked:
        parts_spec = pl.BlockSpec((1, rows, share), lambda i, m, s: (i, 0, 0))
    else:
        parts_spec = whole((rows, share))
    height = min(TILE, rows)
    full = band(height, height + 2 * HALO, HALO)
    bands = [
        band(TILE, TILE + 2 * SIDE, SIDE).T,
        full[:, HALO : HALO + height],
        full[:HALO, :HALO],
        full[height - HALO :, HALO + height :],
    ]
    parts = [jnp.asarray(matrix.astype(np.float32)) for matrix in bands]

    def body(*refs):
        lead = 2 + 9 + len(parts) + count
        smooth_kernel(block_of, plan, width, stacked, *refs[:lead], *refs[lead + len(after) :])

    return pl.pallas_call(
        body,
        grid_spec=pltpu.PrefetchScalarGridSpec(
            num_scalar_prefetch=2,
            grid=(len(plan),),
            in_specs=specs + [whole(p.shape) for p in parts] + [parts_spec] * count + [ANY] * len(after),
            out_specs=[parts_spec] * count + [whole(TOKEN)],
            scratch_shapes=[pltpu.VMEM(p.shape, BF16) for p in parts for _ in range(2)],
        ),
        out_shape=[pltpu.HBM(w.shape, F32) for w in weights] + [jax.ShapeDtypeStruct(TOKEN, F32)],
        compiler_params=pltpu.CompilerParams(vmem_limit_bytes=VMEM),
        cost_estimate=SMALL,
        name="smoothed_terms",
    )(meta, starts, *([above] * 3 + [frame] * 3 + [below] * 3), *parts, *weights, *after)


def term_kernel(layout, width, wanted, units, received, numerator, meta_ref, start_ref, *refs):
    place = meta_ref[0] // 2
    block = 2 * wanted(place) + meta_ref[0] % 2
    _, unit = layout.position_of(wanted(place), place)
    mate_start = start_ref[meta_ref[0] + 1 - 2 * (meta_ref[0] % 2)]
    in_mate = inside(columns(block, layout.share), mate_start, width)
    *refs, out_ref, token_ref = refs
    token_ref[...] = jnp.zeros_like(token_ref)

    def pair():
        own = refs.pop(0)[0]
        got = refs.pop(0)[...]
        for u in units[1:]:
            got = jnp.where(unit == u, refs.pop(0)[...], got)
        return own, got

    def added(own, got, names):
        value = own + jnp.where(in_mate, got, 0.0)
        for _ in range(names):
            value = value + refs.pop(0)[...]
        return value

    if not numerator:
        out_ref[...] = added(*pair(), received)
        return
    own_den, mate_den = pair()
    own, mate = pair()
    rows_part, back = refs.pop(0)[...], refs.pop(0)[...]
    own_back = sum(rows_part[:, u : u + 1] * back[u : u + 1, :] for u in range(3))
    mate_back = sum(rows_part[:, u : u + 1] * back[3 + u : 4 + u, :] for u in range(3))
    top = added(own - own_den * own_back, mate - mate_den * mate_back, received)
    out_ref[...] = top


def block_term(layout, width, wanted, senders, meta, starts, parts, received, tables=(), after=()):
    kept = parts[0][0]
    rows, share = kept.shape[1:]
    chunk = min(TILE, rows)

    def at_unit(place):
        return layout.position_of(wanted(place), place)

    units = sorted({int(at_unit(z)[1]) for z in senders})
    flat = pl.BlockSpec((chunk, share), lambda r, m, s: (r, 0))
    specs, args = [], []
    for own, got in parts:
        specs.append(pl.BlockSpec((1, chunk, share), lambda r, m, s: (at_unit(m[0] // 2)[0], r, 0)))
        args.append(pltpu.with_memory_space_constraint(own, pltpu.HBM))
        for u in units:
            specs.append(
                flat
                if len(units) == 1
                else pl.BlockSpec(
                    (chunk, share), lambda r, m, s, u=u: (jnp.where(at_unit(m[0] // 2)[1] == u, r, 0), 0)
                )
            )
            args.append(got[u])
    if tables:
        rows_part, back = tables
        strips = rows // chunk
        specs.append(pl.BlockSpec((chunk, rows_part.shape[1]), lambda r, m, s: (m[1] * strips + r, 0)))
        specs.append(
            pl.BlockSpec((back.shape[0], share), lambda r, m, s: (0, 2 * wanted(m[0] // 2) + m[0] % 2))
        )
        args += [rows_part, back]
    specs += [flat] * len(received)
    args += list(received)
    lead = 2 + len(args)
    body = functools.partial(term_kernel, layout, width, wanted, units, len(received), bool(tables))
    return pl.pallas_call(
        lambda *refs: body(*refs[:lead], *refs[-2:]),
        grid_spec=pltpu.PrefetchScalarGridSpec(
            num_scalar_prefetch=2, grid=(rows // chunk,), in_specs=specs + [ANY] * len(after), out_specs=[flat, whole(TOKEN)]
        ),
        out_shape=[jax.ShapeDtypeStruct((rows, share), F32), jax.ShapeDtypeStruct(TOKEN, F32)],
        compiler_params=pltpu.CompilerParams(vmem_limit_bytes=SOME),
        cost_estimate=SMALL,
        name="block_term",
    )(meta, starts, *args, *after)


def held_until(values, after):
    def body(*refs):
        del refs

    return pl.pallas_call(
        body,
        in_specs=[ANY] * (len(values) + len(after)),
        out_specs=[ANY] * len(values),
        out_shape=[jax.ShapeDtypeStruct(v.shape, v.dtype) for v in values],
        input_output_aliases={i: i for i in range(len(values))},
        compiler_params=pltpu.CompilerParams(vmem_limit_bytes=VMEM),
        cost_estimate=SMALL,
        name="held",
    )(*values, *after)


def arrived(values):
    def body(*refs):
        refs[-1][...] = jnp.zeros_like(refs[-1])

    return pl.pallas_call(
        body,
        in_specs=[ANY] * len(values),
        out_shape=jax.ShapeDtypeStruct(TOKEN, F32),
        compiler_params=pltpu.CompilerParams(vmem_limit_bytes=SOME),
        cost_estimate=pl.CostEstimate(flops=1000, bytes_accessed=8 * 10**6, transcendentals=0),
        name="arrived",
    )(*values)


def contract_last(left, right):
    return lax.dot_general(left, right, (((1,), (1,)), ((), ())), precision=HIGH, preferred_element_type=F32)


def contract_last_three(left, right):
    def one(a, b):
        return lax.dot_general(a, b, (((1,), (1,)), ((), ())), preferred_element_type=F32)

    (l_hi, l_lo), (r_hi, r_lo) = split_high_low(left), split_high_low(right)
    return one(l_hi, r_hi) + (one(l_lo, r_hi) + one(l_hi, r_lo))


def moments_kernel(places, strips, meta_ref, bins_ref, out_ref):
    count, _, rows, cols = bins_ref.shape
    at = [places.index(e) for e in range(count)]
    image = [bins_ref[at[e], 0] for e in range(count)]
    weight = [bins_ref[at[e], 1] for e in range(count)]
    x = centers(lax.broadcasted_iota(jnp.int32, (1, cols), 1), cols)
    tx = [jnp.ones_like(x), x]
    while len(tx) < 5:
        tx.append(2.0 * x * tx[-1] - tx[-2])
    tx = jnp.concatenate(tx + [jnp.zeros((3, cols), F32)], axis=0)
    joint, diffs = [], []
    for apart in range(1, count // 2 + 1):
        group, group_d = [], []
        for i in range(count):
            j = (i + apart) % count
            w = weight[i] * weight[j] / (weight[i] + weight[j] + 1.0)
            group.append(w)
            group_d.append(w * (image[i] - image[j]))
        joint.append(contract_last_three(tx, jnp.concatenate(group, axis=0)))
        diffs.append(contract_last_three(tx, jnp.concatenate(group_d, axis=0)))
    along = jnp.concatenate([jnp.concatenate(joint, axis=1), jnp.concatenate(diffs, axis=1)], axis=0)
    total = along.shape[1]
    row = lax.broadcasted_iota(jnp.int32, (total, SIDE), 0)
    lane = lax.broadcasted_iota(jnp.int32, (total, SIDE), 1)
    mine = row // rows == lane
    y = centers(row % rows + meta_ref[1] * rows, rows * strips)
    a_hi, a_lo = split_high_low(along)
    ty = [jnp.ones_like(y), y]
    for a in range(5):
        if a > 1:
            ty.append(2.0 * y * ty[-1] - ty[-2])
        b_hi, b_lo = split_high_low(jnp.where(mine, ty[a], 0.0))
        out_ref[:, a * SIDE : (a + 1) * SIDE] = mm(a_hi, b_hi) + (mm(a_lo, b_hi) + mm(a_hi, b_lo))


def solve_kernel(width, meta_ref, start_ref, moments_ref, owner_ref, out_ref, back_ref):
    owner = owner_ref[...].astype(F32)
    count = owner.shape[0]
    lanes = count * count // 2
    exposure = lax.broadcasted_iota(jnp.int32, (count, lanes), 0)
    lane = lax.broadcasted_iota(jnp.int32, (count, lanes), 1)
    mine = lane % count
    apart = lane // count + 1
    is_i = (exposure == mine).astype(F32)
    is_j = (exposure == (mine + apart) % count).astype(F32)
    both = owner + owner.T
    listed = jnp.sum(is_i * jnp.dot(both, is_j, precision=HIGH, preferred_element_type=F32), axis=0, keepdims=True)
    lane_row = lax.broadcasted_iota(jnp.int32, (1, lanes), 1)
    once = (lane_row // count + 1 < count // 2) | (lane_row % count < count // 2)
    listed = jnp.where(once, listed, 0.0)
    held = listed > 0.0
    moment = [[moments_ref[b : b + 1, a * SIDE : a * SIDE + lanes] for b in range(5)] for a in range(5)]

    def entry(k, l):
        (u, v), (s, t) = divmod(k, 3), divmod(l, 3)
        total = 0.0
        for a in (u + s, abs(u - s)):
            for b in (v + t, abs(v - t)):
                total = total + moment[a][b]
        return jnp.where(held, 0.25 * total, 1.0 if k == l else 0.0)

    factor = [[None] * 9 for _ in range(9)]
    scale = [None] * 9
    for k in range(9):
        for l in range(k, 9):
            value = entry(l, k)
            for m in range(k):
                value = value - factor[l][m] * factor[k][m]
            if l == k:
                scale[k] = 1.0 / jnp.sqrt(value)
            else:
                factor[l][k] = value * scale[k]
    half = [None] * 9
    for k in range(9):
        a, b = divmod(k, 3)
        value = moments_ref[8 + b : 9 + b, a * SIDE : a * SIDE + lanes]
        for m in range(k):
            value = value - factor[k][m] * half[m]
        half[k] = value * scale[k]
    fit = [None] * 9
    for k in reversed(range(9)):
        value = half[k]
        for m in range(k + 1, 9):
            value = value - factor[m][k] * fit[m]
        fit[k] = value * scale[k]
    fits = jnp.concatenate([jnp.where(held, f, 0.0) for f in fit] + [jnp.zeros((7, lanes), F32)], axis=0)
    right = contract_last((is_i - is_j) * listed, fits)
    row = lax.broadcasted_iota(jnp.int32, (count, count), 0)
    column = lax.broadcasted_iota(jnp.int32, (count, count), 1)
    degree = jnp.sum(both, axis=1, keepdims=True) + LAMBDA_REG
    system = jnp.where(row == column, degree, 0.0) - both
    for k in range(count):
        inverse = 1.0 / system[k : k + 1, k : k + 1]
        pivot_s, pivot_r = system[k : k + 1, :] * inverse, right[k : k + 1, :] * inverse
        lead = system[:, k : k + 1]
        chosen = row[:, :1] == k
        system = jnp.where(chosen, pivot_s, system - lead * pivot_s)
        right = jnp.where(chosen, pivot_r, right - lead * pivot_r)
    out_ref[...] = right[:, :9]
    member = meta_ref[0]
    mate = member + 1 - 2 * (member % 2)
    cols = back_ref.shape[1]
    padded = cols + 2 * SIDE
    col = lax.broadcasted_iota(jnp.int32, (1, padded), 1) - SIDE
    x = centers(col, cols)
    terms = [jnp.ones_like(x), x, 2.0 * x * x - 1.0]
    fields = [jnp.where(inside(col, start_ref[e], width), t, 0.0) for e in (member, mate) for t in terms]
    fields = jnp.concatenate(fields + [jnp.zeros((2, padded), F32)], axis=0)
    taps = tap_values()
    total = float(taps[RADIUS]) * fields
    for shift in range(1, RADIUS + 1):
        both = pltpu.roll(fields, shift, 1) + pltpu.roll(fields, padded - shift, 1)
        total = total + float(taps[RADIUS + shift]) * both
    total = total[:, SIDE : SIDE + cols]
    rows = lax.broadcasted_iota(jnp.int32, (count, 16), 0)
    for k, which in enumerate((member, mate)):
        mine = jnp.sum(jnp.where(rows == which, right, 0.0), axis=0, keepdims=True)
        for u in range(3):
            back_ref[3 * k + u : 3 * k + u + 1, :] = sum(
                mine[:, 3 * u + v : 3 * u + v + 1] * total[3 * k + v : 3 * k + v + 1, :] for v in range(3)
            )
    back_ref[6:8, :] = jnp.zeros((2, cols), F32)


def filtered_rows(total_rows):
    y = (2.0 * np.arange(total_rows) + 1.0) / total_rows - 1.0
    terms = np.stack([np.ones_like(y), y, 2.0 * y * y - 1.0])
    padded = np.pad(terms, ((0, 0), (RADIUS, RADIUS)))
    taps = tap_values()
    return sum(taps[t] * padded[:, t : t + total_rows] for t in range(2 * RADIUS + 1)).T.astype(np.float32)


def per_device(image, variance, mask, foot_start, pair_owner):
    frame, spread, blocks = image[0], variance[0], mask[0]
    rows, cols = frame.shape
    exposures, sky_count = lax.axis_size("exp"), lax.axis_size("sky")
    member = lax.axis_index("exp")
    meta = jnp.stack([member, lax.axis_index("sky")])
    width = 3 * cols // 4
    layout = Places(exposures, cols)
    share, places, quarter = layout.share, layout.places, layout.quarter
    ends, middle_count = layout.ends, layout.middle
    sent = [(i // 2, i % 2 == 0) for i in range(ends)] + [(quarter + i, True) for i in range(middle_count)]
    swap = [(i, i ^ 1) for i in range(exposures)]

    def swapped(parts):
        return [lax.ppermute(part, "exp", swap) for part in parts]

    den_ends = folded_weights(layout, width, meta, foot_start, spread, blocks)
    *den_middle, den_kept, gathered = pixel_weights(
        layout, width, meta, foot_start, frame, spread, blocks, den_ends
    )
    got_ends = swapped(den_ends)
    got_middle = swapped(den_middle)
    den_got = got_ends + got_middle

    up = [(i, i + 1) for i in range(sky_count - 1)]
    down = [(j, i) for i, j in up]
    above = lax.ppermute(frame[rows - HALO :], "sky", up)
    below = lax.ppermute(frame[:HALO], "sky", down)
    smooth = functools.partial(
        smoothed_terms, meta=meta, starts=foot_start, frame=frame, above=above, below=below, share=share, width=width
    )

    held = [0]
    bits = [1 << k for k in range(exposures.bit_length() - 1)]

    def asked(gathered, bit):
        return lax.ppermute(gathered, "exp", [(i, i ^ bit) for i in range(exposures)])

    def joined(gathered, other, bit):
        low = (member & bit) == 0
        held.extend([e | bit for e in held])
        return jnp.concatenate([jnp.where(low, gathered, other), jnp.where(low, other, gathered)])

    def to_right(step):
        return lambda z: choose(z < step, z + places - step, places - 1)

    def to_left(step):
        return lambda z: choose(z >= places - step, z - places + step, 0)

    def outward(step):
        return lambda z: choose(z < places // 2, to_right(step)(z), to_left(step)(z))

    def shift(value, rights, lefts):
        pairs = [(2 * z + s, 2 * z + 2 + s) for z in rights for s in range(2)]
        pairs += [(2 * z + s, 2 * z - 2 + s) for z in lefts for s in range(2)]
        return lax.ppermute(value, "exp", pairs)

    def along_places(step, term, sums, after):
        rights, lefts = range(step), range(places - step, places)
        if step <= places // 2:
            value, token = term(outward(step), [*rights, *lefts], sums, after)
            if step < places // 2:
                return (shift(value, rights, lefts),), (token,)
            return (shift(value, rights, []), shift(value, [], lefts)), (token,)
        right, token = term(to_right(step), rights, sums[:1], after)
        left, token_left = term(to_left(step), lefts, sums[1:], after)
        return (shift(right, rights, []), shift(left, [], lefts)), (token, token_left)

    def den_term(wanted, senders, sums, after):
        parts = [(den_kept, den_got)]
        return block_term(layout, width, wanted, senders, meta, foot_start, parts, sums, after=after)

    gathered = joined(gathered, asked(gathered, bits[1]), bits[1])
    den_sums, den_values = along_places(1, den_term, (), ())
    (gathered,) = held_until([gathered], [*den_values, above, below])
    for bit in bits[2:-1]:
        gathered = joined(gathered, asked(gathered, bit), bit)
    other = asked(gathered, bits[-1])
    *num_sent, token = smooth(layout.sent_block, sent, [*den_ends, *den_middle], after=den_values)
    num_kept, token = smooth(layout.kept_block, [(i, True) for i in range(places)], [den_kept], after=[token])
    (other,) = held_until([other], [token])
    gathered = joined(gathered, other, bits[-1])
    other = asked(gathered, bits[0])
    den_sums, den_values = along_places(2, den_term, den_sums, [token])
    num_sent = held_until(num_sent, [other, *den_values])
    num_got = swapped(num_sent[:quarter])
    num_got += swapped(held_until(num_sent[quarter:], num_got))
    (gathered,) = held_until([joined(gathered, other, bits[0])], den_values)
    scalars = pl.BlockSpec(memory_space=pltpu.SMEM)
    vmem = pl.BlockSpec(memory_space=pltpu.VMEM)
    moments = pl.pallas_call(
        functools.partial(moments_kernel, held, sky_count),
        in_specs=[scalars, vmem],
        out_shape=jax.ShapeDtypeStruct((16, 5 * SIDE), F32),
        compiler_params=pltpu.CompilerParams(vmem_limit_bytes=SOME),
        cost_estimate=SMALL,
        name="pair_moments",
    )(meta, gathered)
    bit = 1
    while bit < sky_count:
        moments = moments + lax.ppermute(moments, "sky", [(i, i ^ bit) for i in range(sky_count)])
        bit *= 2
    offsets, back = pl.pallas_call(
        functools.partial(solve_kernel, width),
        in_specs=[scalars, scalars, vmem, vmem],
        out_shape=[jax.ShapeDtypeStruct((exposures, 9), F32), jax.ShapeDtypeStruct((8, cols), F32)],
        compiler_params=pltpu.CompilerParams(vmem_limit_bytes=SOME),
        cost_estimate=SMALL,
        name="offsets",
    )(meta, foot_start, moments, pair_owner)

    tables = (jnp.asarray(filtered_rows(rows * sky_count)), back)
    parts = [(den_kept, den_got), (num_kept, num_got)]

    def num_term(wanted, senders, sums, after):
        return block_term(
            layout, width, wanted, senders, meta, foot_start, parts, sums, tables, after
        )

    num_sums, num_values = along_places(1, num_term, (), [arrived(den_sums)])
    for step in range(3, places):
        den_sums, den_values = along_places(step, den_term, den_sums, num_values)
        num_sums, num_values = along_places(step - 1, num_term, num_sums, den_values)

    ahead = [*num_values, arrived(den_sums)]
    terms = []
    for wanted, senders in ((to_right(places - 1), range(places - 1)), (to_left(places - 1), range(1, places))):
        value, token = num_term(wanted, senders, (), ahead)
        terms.append(value)
        ahead = [token]
    rightward = shift(terms[0] + num_sums[0], range(places - 1), [])
    leftward = shift(terms[1] + num_sums[1], [], range(1, places))
    own_den, token = den_term(lambda z: z, range(places), den_sums, ahead)
    own_num, _ = num_term(lambda z: z, range(places), (), [token])
    coadd = (own_num + rightward + leftward) / (PRIOR + own_den)
    return (coadd, offsets)


def solution(mesh):
    placed = (P("exp", "sky", None), P("exp", "sky", None), P("exp", "sky", None), P(), P())
    return jax.shard_map(
        per_device, mesh=mesh, in_specs=placed, out_specs=(P("sky", "exp"), P()), check_vma=False
    )
```
